512 devices in a mesh: section: 8 (over z_hi, x), dp: 64 (over z_lo, y, core).
Axes of the slice: x: 4, y: 4, z: 16 (z_hi: 2, z_lo: 8; z = z_hi * 8 + z_lo), core: 2. Of those that a mesh axis runs over, the one named last changes fastest.
Arguments:
- inputs: bfloat16 [8192, 512], P('dp'), may hold values from -16 to 16
- targets: bfloat16 [8192, 512], P('dp'), may hold values from -6 to 6
- w_in: bfloat16 [8, 512, 2048], P('section', 'dp'), may hold values from -0.25 to 0.25
- w_out: bfloat16 [8, 2048, 512], P('section', 'dp'), may hold values from -0.125 to 0.125
- probes: bfloat16 [8, 512, 2048], P('section'), may hold values from -1 to 1, as said below
Outputs:
- diagonal: float32 [8, 512, 2048], P('section', 'dp')
The draws below stay inside these ranges and needn't reach their ends.
Inputs may be any that keep to these rules, and one draw needn't show every extreme that they name: `probes`: every entry is -1 or +1.
All inputs are finite; a program needn't handle non-finite values.
Results may differ from the reference program's by a relative error of at most 0.01.
Values may be sent and summed in bfloat16 or wider, within the bound.
No kernel may reach another device: no remote copies, remote signals or barrier semaphores. Data moves between devices by JAX's collectives and lax.ppermute only.
A program may use at most 64 MiB of HBM per device.

```python
import jax
import jax.numpy as jnp
from jax import lax

D = 512
FF = 2048
MICRO = 2
MB_ROWS = 64
LAYERS = 8
TOKENS = 8192
N_DP = 64


def draw_probes(key, part):
    key = jax.random.fold_in(key, 11)
    return jax.random.rademacher(key, (LAYERS, D, FF), jnp.float32).astype(jnp.bfloat16)


def with_spikes(array, stream_key, source, target, shards_of, factor):
    owner, partner = [(jnp.arange(array.shape[position]) // (array.shape[position] // shards_of)).reshape([-1 if axis == position else 1 for axis in range(array.ndim)]) for position in (source, target)]
    chosen = jax.random.permutation(stream_key, shards_of)[partner]
    strong = (owner == chosen) | (owner == (partner + shards_of // 2) % shards_of)
    return jnp.where(strong, factor * array, array)


def steps_of(own_key, extent, split, low, top_value):
    loudness = 1.0
    for position, parts in split:
        draws = jax.random.uniform(jax.random.fold_in(jax.random.fold_in(own_key, 6), position), (parts,), jnp.float32, low / len(split), top_value / len(split))
        loudness = loudness * jnp.repeat(jnp.exp(draws), extent[position] // parts).reshape((-1,) + (1,) * (len(extent) - 1 - position))
    return loudness


def normal_values(own_key, dims, width, reach, shards=(), dtype=jnp.bfloat16):
    entries = width * jax.random.normal(own_key, dims, jnp.float32)
    if shards:
        entries = entries * steps_of(own_key, dims, shards, -0.22, 0.18)
    return jnp.clip(entries, -reach, reach).astype(dtype)


def bell_draw_with(stream_key, shape, deviation, reach, shards, heavy, kind=jnp.bfloat16):
    values = deviation * jax.random.normal(stream_key, shape, jnp.float32)
    if shards:
        values = values * steps_of(stream_key, shape, shards, -0.22, 0.18)
    return jnp.clip(with_spikes(values, jax.random.fold_in(stream_key, 3), *heavy), -reach, reach).astype(kind)


def setup_inputs(seed: int = 0) -> dict:
    arg_keys = jax.random.split(jax.random.key(seed), 6)
    inputs = bell_draw_with(arg_keys[0], (TOKENS, D), 1.0, 16.0, ((0, 64),), (0, 1, 64, 4.0))
    targets = normal_values(arg_keys[1], (TOKENS, D), 1.0, 6.0, ((0, 64),))
    w_in = normal_values(arg_keys[2], (LAYERS, D, FF), D ** -0.5, 0.25, ((0, 8), (1, 64)))
    w_out = normal_values(arg_keys[3], (LAYERS, FF, D), FF ** -0.5, 0.125, ((0, 8), (1, 64)))
    probes = draw_probes(jax.random.fold_in(arg_keys[5], 71), 0)
    return dict(inputs=inputs, targets=targets, w_in=w_in, w_out=w_out, probes=probes)


EPSILON = 1e-05
SQRT_HALF = 0.7071067811865476
INV_ROOT_TWO_PI = 0.3989422804014327
CONTRACT_LAST = (((1,), (1,)), ((), ()))
CONTRACT_FIRST = (((0,), (0,)), ((), ()))

def row_mean(values):
    return lax.optimization_barrier(jnp.mean(values, axis=-1, keepdims=True))

def rounded(values):
    return lax.optimization_barrier(values.astype(jnp.bfloat16)).astype(jnp.float32)

def gelu_terms(preact):
    normal_cdf = 0.5 * (1.0 + lax.erf(preact * SQRT_HALF))
    density = INV_ROOT_TWO_PI * jnp.exp(-0.5 * preact * preact)
    return (preact * normal_cdf, normal_cdf + preact * density, density * (2.0 - preact * preact))

def forward_layer(inflow, inflow_t, weight_in, weight_out, probe_mat):
    centred = inflow - row_mean(inflow)
    rscale = lax.rsqrt(row_mean(centred * centred) + EPSILON)
    normed = centred * rscale
    tangent_dot = row_mean(normed * inflow_t)
    normed_t = rscale * (inflow_t - row_mean(inflow_t) - normed * tangent_dot)
    low_normed = normed.astype(jnp.bfloat16)
    preact = jnp.dot(low_normed, weight_in, preferred_element_type=jnp.float32)
    preact_t = jnp.dot(normed_t.astype(jnp.bfloat16), weight_in, preferred_element_type=jnp.float32) + jnp.dot(low_normed, probe_mat, preferred_element_type=jnp.float32)
    activation, slope_one, slope_two = gelu_terms(preact)
    hidden = activation.astype(jnp.bfloat16)
    hidden_t = (slope_one * preact_t).astype(jnp.bfloat16)
    outflow = inflow + jnp.dot(hidden, weight_out, preferred_element_type=jnp.float32)
    outflow_t = inflow_t + jnp.dot(hidden_t, weight_out, preferred_element_type=jnp.float32)
    return (outflow, outflow_t, (normed, normed_t, rscale, tangent_dot, preact, preact_t))

def norm_apply(values, normed, rscale):
    return rscale * (values - row_mean(values) - normed * row_mean(normed * values))

def backward_layer(adjoint, adjoint_t, stored, weight_in, weight_out, probe_mat):
    normed, normed_t, rscale, tangent_dot, preact, preact_t = stored
    activation, slope_one, slope_two = gelu_terms(preact)
    grad_hidden = lax.dot_general(adjoint.astype(jnp.bfloat16), weight_out, CONTRACT_LAST, preferred_element_type=jnp.float32)
    grad_hidden_t = lax.dot_general(adjoint_t.astype(jnp.bfloat16), weight_out, CONTRACT_LAST, preferred_element_type=jnp.float32)
    grad_pre = grad_hidden * slope_one
    grad_pre_t = grad_hidden_t * slope_one + grad_hidden * slope_two * preact_t
    low_grad = grad_pre.astype(jnp.bfloat16)
    low_grad_t = grad_pre_t.astype(jnp.bfloat16)
    grad_norm = lax.dot_general(low_grad, weight_in, CONTRACT_LAST, preferred_element_type=jnp.float32)
    grad_norm_t = lax.dot_general(low_grad_t, weight_in, CONTRACT_LAST, preferred_element_type=jnp.float32) + lax.dot_general(low_grad, probe_mat, CONTRACT_LAST, preferred_element_type=jnp.float32)
    through = norm_apply(grad_norm, normed, rscale)
    through_t = norm_apply(grad_norm_t, normed, rscale) - rscale * tangent_dot * through - rscale * (normed_t * row_mean(normed * grad_norm) + normed * row_mean(normed_t * grad_norm))
    return (adjoint + through, adjoint_t + through_t, low_grad, low_grad_t)

def curvature(normed, normed_t, low_grad, low_grad_t):
    first_term = lax.dot_general(normed.astype(jnp.bfloat16), low_grad_t, CONTRACT_FIRST, preferred_element_type=jnp.float32)
    second_term = lax.dot_general(normed_t.astype(jnp.bfloat16), low_grad, CONTRACT_FIRST, preferred_element_type=jnp.float32)
    return first_term + second_term

def replica_sum(normed, normed_t, low_grad, low_grad_t):
    group_rows = MICRO * MB_ROWS

    def add_group(total, pieces):
        return (total + curvature(pieces[0], pieces[1], pieces[2], pieces[3]), None)
    grouped = tuple((values.reshape(N_DP, group_rows, values.shape[-1]) for values in (normed, normed_t, low_grad, low_grad_t)))
    total, unused = lax.scan(add_group, jnp.zeros((D, FF), jnp.float32), grouped)
    return total

def reference(inputs, targets, w_in, w_out, probes):
    inflow = inputs.astype(jnp.float32)
    inflow_t = jnp.zeros_like(inflow)
    stored_all = []
    for layer_index in range(LAYERS):
        outflow, outflow_t, stored = forward_layer(inflow, inflow_t, w_in[layer_index], w_out[layer_index], probes[layer_index])
        stored_all.append(stored)
        inflow = rounded(outflow)
        inflow_t = rounded(outflow_t)
    adjoint = rounded((outflow - targets.astype(jnp.float32)) / TOKENS)
    adjoint_t = rounded(outflow_t / TOKENS)
    diagonals = []
    for layer_index in range(LAYERS - 1, -1, -1):
        stored = stored_all[layer_index]
        upstream, upstream_t, low_grad, low_grad_t = backward_layer(adjoint, adjoint_t, stored, w_in[layer_index], w_out[layer_index], probes[layer_index])
        hessian_term = replica_sum(stored[0], stored[1], low_grad, low_grad_t)
        diagonals.append(probes[layer_index].astype(jnp.float32) * hessian_term)
        adjoint = rounded(upstream)
        adjoint_t = rounded(upstream_t)
    return jnp.stack(diagonals[::-1])
```

```python
import functools
import itertools

import jax
import jax.numpy as jnp
from jax import lax
from jax.experimental import pallas as pl
from jax.experimental.pallas import tpu as pltpu
from jax.sharding import Mesh, PartitionSpec as P

EPSILON = 1e-05
SQRT_HALF = 0.7071067811865476
INV_ROOT_TWO_PI = 0.3989422804014327
CONTRACT_LAST = (((1,), (1,)), ((), ()))
CONTRACT_FIRST = (((0,), (0,)), ((), ()))

NAMES = ("zh", "x", "b4", "b2", "b1", "y", "c")
SIZES = (2, 4, 2, 2, 2, 4, 2)
SECTION = ("zh", "x")
DP = ("b4", "b2", "b1", "y", "c")
LAYERS = 8
FEATURES = 512
HIDDEN = 2048
ROWS = 128
TOKENS = 8192
CHUNK = 512
CHUNKS = HIDDEN // CHUNK
VMEM_BYTES = 40 * 1024 * 1024
ANY = pl.BlockSpec(memory_space=pl.ANY)
SMEM = pl.BlockSpec(memory_space=pltpu.SMEM)


def flat(place):
    index = 0
    for size, at in zip(SIZES, place):
        index = index * size + at
    return index


def routed(value, route):
    pairs = []
    for place in itertools.product(*(range(size) for size in SIZES)):
        there = route(*place)
        if there is not None:
            pairs.append((flat(place), flat(there)))
    return lax.ppermute(value, NAMES, pairs)


def swap_b4(zh, x, b4, b2, b1, y, c):
    return (zh, x, 1 - b4, b2, b1, y, c)


def swap_b2(zh, x, b4, b2, b1, y, c):
    return (zh, x, b4, 1 - b2, b1, y, c)


def swap_b1(zh, x, b4, b2, b1, y, c):
    return (zh, x, b4, b2, 1 - b1, y, c)


def swap_even(zh, x, b4, b2, b1, y, c):
    return (zh, x, b4, b2, b1, y ^ 1, c)


def swap_odd(zh, x, b4, b2, b1, y, c):
    return (zh, x, b4, b2, b1, y ^ 3, c)


def swap_core(zh, x, b4, b2, b1, y, c):
    return (zh, x, b4, b2, b1, y, 1 - c)


def up_from(section):
    def route(zh, x, b4, b2, b1, y, c):
        if zh * 4 + x != section:
            return None
        if x == 3:
            return (zh + 1, 0, 1 - b4, b2, b1, y, c)
        return (zh, x + 1, b4, b2, b1, y, c)

    return route


def down_from(section):
    def route(zh, x, b4, b2, b1, y, c):
        if zh * 4 + x != section:
            return None
        if x == 0:
            return (zh - 1, 3, 1 - b4, b2, b1, y, c)
        return (zh, x - 1, b4, b2, b1, y, c)

    return route


def merged(own, other, bit):
    first = bit == 0
    return jnp.concatenate([jnp.where(first, own, other), jnp.where(first, other, own)], axis=0)


def gathered(block):
    block = merged(block, routed(block, swap_b4), lax.axis_index("b4"))
    block = merged(block, routed(block, swap_b2), lax.axis_index("b2"))
    block = merged(block, routed(block, swap_b1), lax.axis_index("b1"))
    rows, half = block.shape[0], block.shape[1] // 2
    y = lax.axis_index("y")
    left, right = block[:, :half], block[:, half:]
    left_two = merged(left, routed(left, swap_even), y % 2)
    right_two = merged(right, routed(right, swap_odd), y // 2)
    left_four = merged(left_two, routed(left_two, swap_odd), y // 2)
    other = routed(right_two, swap_even)
    outer = (y == 0) | (y == 3)
    own_a, own_b, oth_a, oth_b = right_two[:rows], right_two[rows:], other[:rows], other[rows:]
    right_four = jnp.concatenate(
        [
            jnp.where(outer, own_a, oth_a),
            jnp.where(outer, oth_a, own_a),
            jnp.where(outer, oth_b, own_b),
            jnp.where(outer, own_b, oth_b),
        ],
        axis=0,
    )
    core = lax.axis_index("c")
    return jnp.concatenate(
        [
            merged(left_four, routed(left_four, swap_core), core),
            merged(right_four, routed(right_four, swap_core), core),
        ],
        axis=1,
    )


def feature_order():
    position = lax.broadcasted_iota(jnp.int32, (FEATURES, FEATURES), 1)
    natural = lax.broadcasted_iota(jnp.int32, (FEATURES, FEATURES), 0)
    core, y = position // 256, (position // 64) % 4
    b1, b2, b4, row = (position // 32) % 2, (position // 16) % 2, (position // 8) % 2, position % 8
    return (natural == (b4 * 4 + b2 * 2 + b1) * 64 + y * 16 + core * 8 + row).astype(jnp.bfloat16)


def row_mean(values):
    return jnp.mean(values, axis=-1, keepdims=True)


def copies(pairs, sem):
    return [pltpu.make_async_copy(src, dst, sem.at[i]) for i, (src, dst) in enumerate(pairs)]


def columns(ref, chunk):
    return ref.at[:, pl.ds(pl.multiple_of(chunk * CHUNK, CHUNK), CHUNK)]


def lines(ref, chunk):
    return ref.at[pl.ds(pl.multiple_of(chunk * CHUNK, CHUNK), CHUNK), :]


def forward_kernel(tick, *refs):
    last, first = tick == LAYERS - 1, tick == 0
    section, pair_in, w_in, probe, w_out = refs[:5]
    refs = refs[5:]
    if last:
        goal, refs = refs[0], refs[1:]
    if not first:
        refs = refs[3:]
    pair_out, norm_out, stat_out, slope_out = refs[:4]
    refs = refs[4:]
    pair_v, in_v, probe_v, out_v, norm_v, stat_v, slope_v, lhs_v, acc_v, send_v, goal_v = refs[:11]
    head_sem, weight_sem, store_sem = refs[11:]

    @pl.when(section[0] == tick)
    def _():
        def weights(chunk):
            return [
                pltpu.make_async_copy(columns(w_in, chunk), in_v.at[chunk], weight_sem.at[0, chunk]),
                pltpu.make_async_copy(columns(probe, chunk), probe_v.at[chunk], weight_sem.at[1, chunk]),
                pltpu.make_async_copy(lines(w_out, chunk), out_v.at[chunk], weight_sem.at[2, chunk]),
            ]

        head = [pltpu.make_async_copy(pair_in, pair_v, head_sem.at[0])]
        if last:
            head.append(pltpu.make_async_copy(goal, goal_v, head_sem.at[1]))
        for copy in head:
            copy.start()
        for chunk in range(CHUNKS):
            for copy in weights(chunk):
                copy.start()
        for copy in head:
            copy.wait()
        inflow = pair_v[0].astype(jnp.float32)
        inflow_t = pair_v[1].astype(jnp.float32)
        centred = inflow - row_mean(inflow)
        rscale = lax.rsqrt(row_mean(centred * centred) + EPSILON)
        normed = centred * rscale
        tangent_dot = row_mean(normed * inflow_t)
        normed_t = rscale * (inflow_t - row_mean(inflow_t) - normed * tangent_dot)
        norm_v[0] = normed
        norm_v[1] = normed_t
        stat_v[0] = jnp.broadcast_to(rscale, (ROWS, 128))
        stat_v[1] = jnp.broadcast_to(tangent_dot, (ROWS, 128))
        lhs_v[:ROWS] = normed.astype(jnp.bfloat16)
        lhs_v[ROWS:] = normed_t.astype(jnp.bfloat16)
        acc_v[:ROWS] = inflow
        acc_v[ROWS:] = inflow_t
        stores = [
            pltpu.make_async_copy(norm_v, norm_out, head_sem.at[2]),
            pltpu.make_async_copy(stat_v, stat_out, head_sem.at[3]),
        ]
        for copy in stores:
            copy.start()

        def slopes(chunk):
            return pltpu.make_async_copy(slope_v.at[chunk], slope_out.at[chunk], store_sem.at[chunk])

        def step(chunk, carry):
            for copy in weights(chunk):
                copy.wait()
            both = jnp.dot(lhs_v[...], in_v[chunk], preferred_element_type=jnp.float32)
            preact = both[:ROWS]
            preact_t = both[ROWS:] + jnp.dot(lhs_v[:ROWS], probe_v[chunk], preferred_element_type=jnp.float32)
            normal_cdf = 0.5 * (1.0 + lax.erf(preact * SQRT_HALF))
            density = INV_ROOT_TWO_PI * jnp.exp(-0.5 * preact * preact)
            slope = normal_cdf + preact * density
            slope_v[chunk, 0] = slope
            slope_v[chunk, 1] = density * (2.0 - preact * preact) * preact_t
            slopes(chunk).start()
            hidden = jnp.concatenate([preact * normal_cdf, slope * preact_t], axis=0).astype(jnp.bfloat16)
            acc_v[...] += jnp.dot(hidden, out_v[chunk], preferred_element_type=jnp.float32)
            return carry

        lax.fori_loop(0, CHUNKS, step, 0)
        if last:
            send_v[0] = ((acc_v[:ROWS] - goal_v[...].astype(jnp.float32)) / TOKENS).astype(jnp.bfloat16)
            send_v[1] = (acc_v[ROWS:] / TOKENS).astype(jnp.bfloat16)
        else:
            send_v[0] = acc_v[:ROWS].astype(jnp.bfloat16)
            send_v[1] = acc_v[ROWS:].astype(jnp.bfloat16)
        send = pltpu.make_async_copy(send_v, pair_out, head_sem.at[4])
        send.start()
        for copy in stores:
            copy.wait()
        for chunk in range(CHUNKS):
            slopes(chunk).wait()
        send.wait()


NORM = jax.ShapeDtypeStruct((2, ROWS, FEATURES), jnp.float32)
STAT = jax.ShapeDtypeStruct((2, ROWS, 128), jnp.float32)
SLOPE = jax.ShapeDtypeStruct((CHUNKS, 2, ROWS, CHUNK), jnp.float32)
PAIR = jax.ShapeDtypeStruct((2, ROWS, FEATURES), jnp.bfloat16)
GRADS = jax.ShapeDtypeStruct((CHUNKS, 2 * ROWS, CHUNK), jnp.bfloat16)


def vmem(struct):
    return pltpu.VMEM(struct.shape, struct.dtype)


WEIGHT = pltpu.VMEM((CHUNKS, FEATURES, CHUNK), jnp.bfloat16)


def forward_call(tick, section, pair, w_in, probe, w_out, goal, kept):
    last = tick == LAYERS - 1
    operands = [section, pair, w_in, probe, w_out] + ([goal] if last else []) + list(kept)
    start = len(operands) - len(kept)
    aliases = {start + i: 1 + i for i in range(len(kept))}
    return pl.pallas_call(
        functools.partial(forward_kernel, tick),
        out_shape=[PAIR, NORM, STAT, SLOPE],
        in_specs=[SMEM] + [ANY] * (len(operands) - 1),
        out_specs=[ANY] * 4,
        scratch_shapes=[
            vmem(PAIR),
            WEIGHT,
            WEIGHT,
            WEIGHT,
            vmem(NORM),
            vmem(STAT),
            vmem(SLOPE),
            pltpu.VMEM((2 * ROWS, FEATURES), jnp.bfloat16),
            pltpu.VMEM((2 * ROWS, FEATURES), jnp.float32),
            vmem(PAIR),
            pltpu.VMEM((ROWS, FEATURES), jnp.bfloat16),
            pltpu.SemaphoreType.DMA((5,)),
            pltpu.SemaphoreType.DMA((3, CHUNKS)),
            pltpu.SemaphoreType.DMA((CHUNKS,)),
        ],
        input_output_aliases=aliases,
        compiler_params=pltpu.CompilerParams(vmem_limit_bytes=VMEM_BYTES),
        name=f"layer_up_{tick}",
    )(*operands)


def hidden_grads(pair_v, out_chunk, slope_chunk, curve_chunk):
    both = lax.dot_general(pair_v, out_chunk, CONTRACT_LAST, preferred_element_type=jnp.float32)
    grad_hidden, grad_hidden_t = both[:ROWS], both[ROWS:]
    grad_pre = grad_hidden * slope_chunk
    grad_pre_t = grad_hidden_t * slope_chunk + grad_hidden * curve_chunk
    return grad_pre.astype(jnp.bfloat16), grad_pre_t.astype(jnp.bfloat16)


def norm_apply(values, normed, rscale):
    return rscale * (values - row_mean(values) - normed * row_mean(normed * values))


def backward_kernel(tick, *refs):
    section, pair_in, w_in, probe, w_out, norm, stat, slope = refs[:8]
    refs = refs[8:] if tick == 0 else refs[9:]
    pair_out, grads_out = refs[:2]
    pair_v, in_v, probe_v, out_v, norm_v, stat_v, slope_v, grads_v, acc_v, acc_t_v, send_v = refs[2:13]
    head_sem, weight_sem, store_sem = refs[13:]

    @pl.when(section[0] == LAYERS - 1 - tick)
    def _():
        def weights(chunk):
            return [
                pltpu.make_async_copy(lines(w_out, chunk), out_v.at[chunk], weight_sem.at[0, chunk]),
                pltpu.make_async_copy(slope.at[chunk], slope_v.at[chunk], weight_sem.at[1, chunk]),
                pltpu.make_async_copy(columns(w_in, chunk), in_v.at[chunk], weight_sem.at[2, chunk]),
                pltpu.make_async_copy(columns(probe, chunk), probe_v.at[chunk], weight_sem.at[3, chunk]),
            ]

        head = pltpu.make_async_copy(pair_in, pair_v, head_sem.at[0])
        head.start()
        for chunk in range(CHUNKS):
            for copy in weights(chunk):
                copy.start()
        tail = [
            pltpu.make_async_copy(norm, norm_v, head_sem.at[1]),
            pltpu.make_async_copy(stat, stat_v, head_sem.at[2]),
        ]
        for copy in tail:
            copy.start()
        acc_v[...] = jnp.zeros_like(acc_v)
        acc_t_v[...] = jnp.zeros_like(acc_t_v)
        head.wait()

        def grads(chunk):
            return pltpu.make_async_copy(grads_v.at[chunk], grads_out.at[chunk], store_sem.at[chunk])

        def step(chunk, carry):
            for copy in weights(chunk):
                copy.wait()
            low_grad, low_grad_t = hidden_grads(
                pair_v[...].reshape(2 * ROWS, FEATURES), out_v[chunk], slope_v[chunk, 0], slope_v[chunk, 1]
            )
            grads_v[chunk, :ROWS] = low_grad_t
            grads_v[chunk, ROWS:] = low_grad
            grads(chunk).start()
            both = jnp.concatenate([low_grad_t, low_grad], axis=0)
            acc_v[...] += lax.dot_general(both, in_v[chunk], CONTRACT_LAST, preferred_element_type=jnp.float32)
            acc_t_v[...] += lax.dot_general(
                low_grad, probe_v[chunk], CONTRACT_LAST, preferred_element_type=jnp.float32
            )
            return carry

        lax.fori_loop(0, CHUNKS, step, 0)
        for copy in tail:
            copy.wait()
        normed, normed_t = norm_v[0], norm_v[1]
        rscale, tangent_dot = stat_v[0][:, :1], stat_v[1][:, :1]
        grad_norm = acc_v[ROWS:]
        grad_norm_t = acc_v[:ROWS] + acc_t_v[...]
        through = norm_apply(grad_norm, normed, rscale)
        through_t = (
            norm_apply(grad_norm_t, normed, rscale)
            - rscale * tangent_dot * through
            - rscale * (normed_t * row_mean(normed * grad_norm) + normed * row_mean(normed_t * grad_norm))
        )
        send_v[0] = (pair_v[0].astype(jnp.float32) + through).astype(jnp.bfloat16)
        send_v[1] = (pair_v[1].astype(jnp.float32) + through_t).astype(jnp.bfloat16)
        send = pltpu.make_async_copy(send_v, pair_out, head_sem.at[3])
        send.start()
        for chunk in range(CHUNKS):
            grads(chunk).wait()
        send.wait()


def backward_call(tick, section, pair, w_in, probe, w_out, kept, grads):
    operands = [section, pair, w_in, probe, w_out, *kept, *grads]
    return pl.pallas_call(
        functools.partial(backward_kernel, tick),
        out_shape=[PAIR, GRADS],
        in_specs=[SMEM] + [ANY] * (len(operands) - 1),
        out_specs=[ANY] * 2,
        scratch_shapes=[
            vmem(PAIR),
            WEIGHT,
            WEIGHT,
            WEIGHT,
            vmem(NORM),
            vmem(STAT),
            vmem(SLOPE),
            vmem(GRADS),
            pltpu.VMEM((2 * ROWS, FEATURES), jnp.float32),
            pltpu.VMEM((ROWS, FEATURES), jnp.float32),
            vmem(PAIR),
            pltpu.SemaphoreType.DMA((4,)),
            pltpu.SemaphoreType.DMA((4, CHUNKS)),
            pltpu.SemaphoreType.DMA((CHUNKS,)),
        ],
        input_output_aliases={8: 1} if grads else {},
        compiler_params=pltpu.CompilerParams(vmem_limit_bytes=VMEM_BYTES),
        name=f"layer_down_{tick}",
    )(*operands)


def curvature_kernel(*refs):
    section, core, pair_in, w_out, norm, slope, grads, away_out, stay_out = refs[:9]
    pair_v, out_v, norm_v, slope_v, grads_v, half_v, away_v, stay_v = refs[9:17]
    head_sem, weight_sem, store_sem = refs[17:]
    bottom = section[0] == 0
    load_norm = pltpu.make_async_copy(norm, norm_v, head_sem.at[0])
    load_norm.start()

    @pl.when(bottom)
    def _():
        load_pair = pltpu.make_async_copy(pair_in, pair_v, head_sem.at[1])
        load_pair.start()

        def weights(chunk):
            return [
                pltpu.make_async_copy(lines(w_out, chunk), out_v.at[chunk], weight_sem.at[0, chunk]),
                pltpu.make_async_copy(slope.at[chunk], slope_v.at[chunk], weight_sem.at[1, chunk]),
            ]

        for chunk in range(CHUNKS):
            for copy in weights(chunk):
                copy.start()
        load_pair.wait()

        def step(chunk, carry):
            for copy in weights(chunk):
                copy.wait()
            low_grad, low_grad_t = hidden_grads(
                pair_v[...].reshape(2 * ROWS, FEATURES), out_v[chunk], slope_v[chunk, 0], slope_v[chunk, 1]
            )
            grads_v[chunk, :ROWS] = low_grad_t
            grads_v[chunk, ROWS:] = low_grad
            return carry

        lax.fori_loop(0, CHUNKS, step, 0)

    @pl.when(jnp.logical_not(bottom))
    def _():
        load_grads = pltpu.make_async_copy(grads, grads_v, head_sem.at[2])
        load_grads.start()
        load_grads.wait()

    load_norm.wait()
    for half in range(2):
        for which in range(2):
            half_v[half, which * ROWS : (which + 1) * ROWS] = norm_v[which, :, half * 256 : (half + 1) * 256].astype(
                jnp.bfloat16
            )
    own = core[0]

    def away(chunk):
        return pltpu.make_async_copy(away_v.at[chunk], columns(away_out, chunk), store_sem.at[0, chunk])

    def stay(chunk):
        return pltpu.make_async_copy(stay_v.at[chunk], columns(stay_out, chunk), store_sem.at[1, chunk])

    def step(chunk, carry):
        away_v[chunk] = lax.dot_general(
            half_v[1 - own], grads_v[chunk], CONTRACT_FIRST, preferred_element_type=jnp.float32
        ).astype(jnp.bfloat16)
        away(chunk).start()
        stay_v[chunk] = lax.dot_general(half_v[own], grads_v[chunk], CONTRACT_FIRST, preferred_element_type=jnp.float32)
        stay(chunk).start()
        return carry

    lax.fori_loop(0, CHUNKS, step, 0)
    for chunk in range(CHUNKS):
        away(chunk).wait()
        stay(chunk).wait()


def curvature_call(section, core, pair, w_out, norm, slope, grads):
    half = FEATURES // 2
    return pl.pallas_call(
        curvature_kernel,
        out_shape=[
            jax.ShapeDtypeStruct((half, HIDDEN), jnp.bfloat16),
            jax.ShapeDtypeStruct((half, HIDDEN), jnp.float32),
        ],
        in_specs=[SMEM, SMEM] + [ANY] * 5,
        out_specs=[ANY] * 2,
        scratch_shapes=[
            vmem(PAIR),
            WEIGHT,
            vmem(NORM),
            vmem(SLOPE),
            vmem(GRADS),
            pltpu.VMEM((2, 2 * ROWS, half), jnp.bfloat16),
            pltpu.VMEM((CHUNKS, half, CHUNK), jnp.bfloat16),
            pltpu.VMEM((CHUNKS, half, CHUNK), jnp.float32),
            pltpu.SemaphoreType.DMA((3,)),
            pltpu.SemaphoreType.DMA((2, CHUNKS)),
            pltpu.SemaphoreType.DMA((2, CHUNKS)),
        ],
        compiler_params=pltpu.CompilerParams(vmem_limit_bytes=VMEM_BYTES),
        name="layer_curvature",
    )(section, core, pair, w_out, norm, slope, grads)


def shards(inputs, targets, w_in, w_out, probes):
    section = jnp.reshape(lax.axis_index(SECTION), (1,)).astype(jnp.int32)
    core = jnp.reshape(lax.axis_index("c"), (1,)).astype(jnp.int32)
    order = feature_order()
    full_in = gathered(w_in[0])
    full_out = gathered(jnp.dot(w_out[0], order))
    full_out = (
        full_out.reshape(2, 4, 2, 2, 2, 32, FEATURES).transpose(4, 3, 2, 1, 0, 5, 6).reshape(HIDDEN, FEATURES)
    )
    probe = lax.dot_general(order, probes[0], CONTRACT_FIRST, preferred_element_type=jnp.bfloat16)
    fresh = jnp.dot(inputs, order)
    goal = jnp.dot(routed(targets, swap_b4), order)
    pair = jnp.stack([fresh, jnp.zeros_like(fresh)])
    kept = ()
    for tick in range(LAYERS):
        pair, *kept = forward_call(tick, section, pair, full_in, probe, full_out, goal, kept)
        if tick < LAYERS - 1:
            pair = routed(pair, up_from(tick))
    grads = ()
    for tick in range(LAYERS - 1):
        pair, *grads = backward_call(tick, section, pair, full_in, probe, full_out, kept, grads)
        pair = routed(pair, down_from(LAYERS - 1 - tick))
    away, stay = curvature_call(section, core, pair, full_out, kept[0], kept[2], grads[0])
    summed = (stay + routed(away, swap_core).astype(jnp.float32)).astype(jnp.bfloat16)
    summed = lax.all_to_all(summed.reshape(4, 64, HIDDEN), "y", 0, 0, tiled=True)
    summed = jnp.sum(summed.astype(jnp.float32), axis=0).astype(jnp.bfloat16)
    summed = lax.all_to_all(summed.reshape(8, 8, HIDDEN), ("b1", "b2", "b4"), 0, 0, tiled=True)
    summed = jnp.sum(summed.astype(jnp.float32), axis=0)
    probe_own = lax.dynamic_slice_in_dim(probes[0], lax.axis_index(DP) * 8, 8, 0)
    return (probe_own.astype(jnp.float32) * summed)[None]


def solution(mesh):
    fine = Mesh(mesh.devices.reshape(SIZES), NAMES)
    return jax.shard_map(
        shards,
        mesh=fine,
        in_specs=(
            P(DP, None),
            P(DP, None),
            P(SECTION, DP, None),
            P(SECTION, DP, None),
            P(SECTION, None, None),
        ),
        out_specs=P(SECTION, DP, None),
        check_vma=False,
    )
```

```python
import functools
import itertools

import jax
import jax.numpy as jnp
from jax import lax
from jax.experimental import pallas as pl
from jax.experimental.pallas import tpu as pltpu
from jax.sharding import Mesh, PartitionSpec as P

EPSILON = 1e-05
SQRT_HALF = 0.7071067811865476
INV_ROOT_TWO_PI = 0.3989422804014327
CONTRACT_LAST = (((1,), (1,)), ((), ()))
CONTRACT_FIRST = (((0,), (0,)), ((), ()))

NAMES = ("zh", "x", "b4", "b2", "b1", "y", "c")
SIZES = (2, 4, 2, 2, 2, 4, 2)
SECTION = ("zh", "x")
DP = ("b4", "b2", "b1", "y", "c")
LAYERS = 8
FEATURES = 512
HIDDEN = 2048
MICRO = 2
ROWS = 64
UNROLL = 2
TOKENS = 8192
CHUNK = 512
CHUNKS = HIDDEN // CHUNK
VMEM_BYTES = 8 * 1024 * 1024
WHOLE = pl.BlockSpec(memory_space=pltpu.VMEM)
SMEM = pl.BlockSpec(memory_space=pltpu.SMEM)


def flat(place):
    index = 0
    for size, at in zip(SIZES, place):
        index = index * size + at
    return index


def routed(value, route):
    pairs = []
    for place in itertools.product(*(range(size) for size in SIZES)):
        there = route(*place)
        if there is not None:
            pairs.append((flat(place), flat(there)))
    return lax.ppermute(value, NAMES, pairs)


def swap_b4(zh, x, b4, b2, b1, y, c):
    return (zh, x, 1 - b4, b2, b1, y, c)


def swap_b2(zh, x, b4, b2, b1, y, c):
    return (zh, x, b4, 1 - b2, b1, y, c)


def swap_b1(zh, x, b4, b2, b1, y, c):
    return (zh, x, b4, b2, 1 - b1, y, c)


def swap_even(zh, x, b4, b2, b1, y, c):
    return (zh, x, b4, b2, b1, y ^ 1, c)


def swap_odd(zh, x, b4, b2, b1, y, c):
    return (zh, x, b4, b2, b1, y ^ 3, c)


def swap_core(zh, x, b4, b2, b1, y, c):
    return (zh, x, b4, b2, b1, y, 1 - c)


def up_from(section):
    def route(zh, x, b4, b2, b1, y, c):
        if zh * 4 + x != section:
            return None
        if x == 3:
            return (zh + 1, 0, 1 - b4, b2, b1, y, c)
        return (zh, x + 1, b4, b2, b1, y, c)

    return route


def down_from(section):
    def route(zh, x, b4, b2, b1, y, c):
        if zh * 4 + x != section:
            return None
        if x == 0:
            return (zh - 1, 3, 1 - b4, b2, b1, y, c)
        return (zh, x - 1, b4, b2, b1, y, c)

    return route


def merged(own, other, bit):
    first = bit == 0
    return jnp.concatenate([jnp.where(first, own, other), jnp.where(first, other, own)], axis=0)


def gathered(block):
    block = merged(block, routed(block, swap_b4), lax.axis_index("b4"))
    block = merged(block, routed(block, swap_b2), lax.axis_index("b2"))
    block = merged(block, routed(block, swap_b1), lax.axis_index("b1"))
    rows, half = block.shape[0], block.shape[1] // 2
    y = lax.axis_index("y")
    left, right = block[:, :half], block[:, half:]
    left_two = merged(left, routed(left, swap_even), y % 2)
    right_two = merged(right, routed(right, swap_odd), y // 2)
    left_four = merged(left_two, routed(left_two, swap_odd), y // 2)
    other = routed(right_two, swap_even)
    outer = (y == 0) | (y == 3)
    own_a, own_b, oth_a, oth_b = right_two[:rows], right_two[rows:], other[:rows], other[rows:]
    right_four = jnp.concatenate(
        [
            jnp.where(outer, own_a, oth_a),
            jnp.where(outer, oth_a, own_a),
            jnp.where(outer, oth_b, own_b),
            jnp.where(outer, own_b, oth_b),
        ],
        axis=0,
    )
    core = lax.axis_index("c")
    return jnp.concatenate(
        [
            merged(left_four, routed(left_four, swap_core), core),
            merged(right_four, routed(right_four, swap_core), core),
        ],
        axis=1,
    )


def feature_order():
    position = lax.broadcasted_iota(jnp.int32, (FEATURES, FEATURES), 1)
    natural = lax.broadcasted_iota(jnp.int32, (FEATURES, FEATURES), 0)
    core, y = position // 256, (position // 64) % 4
    b1, b2, b4, row = (position // 32) % 2, (position // 16) % 2, (position // 8) % 2, position % 8
    return (natural == (b4 * 4 + b2 * 2 + b1) * 64 + y * 16 + core * 8 + row).astype(jnp.bfloat16)


def row_mean(values):
    return jnp.mean(values, axis=-1, keepdims=True)


def columns(chunk):
    return pl.ds(pl.multiple_of(chunk * CHUNK, CHUNK), CHUNK)


def forward_kernel(tick, *refs):
    last = tick == LAYERS - 1
    section, pair, w_in, probe, w_out = refs[:5]
    refs = refs[5:]
    if last:
        goal, refs = refs[0], refs[1:]
    pair_out, norm, stat, slope_out, lhs, acc = refs

    @pl.when(section[0] == tick)
    def _():
        inflow = pair[0].astype(jnp.float32)
        inflow_t = pair[1].astype(jnp.float32)
        centred = inflow - row_mean(inflow)
        rscale = lax.rsqrt(row_mean(centred * centred) + EPSILON)
        normed = centred * rscale
        tangent_dot = row_mean(normed * inflow_t)
        normed_t = rscale * (inflow_t - row_mean(inflow_t) - normed * tangent_dot)
        norm[0] = normed
        norm[1] = normed_t
        stat[0] = jnp.broadcast_to(rscale, (ROWS, 128))
        stat[1] = jnp.broadcast_to(tangent_dot, (ROWS, 128))
        lhs[:ROWS] = normed.astype(jnp.bfloat16)
        lhs[ROWS:] = normed_t.astype(jnp.bfloat16)
        acc[:ROWS] = inflow
        acc[ROWS:] = inflow_t

        def step(chunk, carry):
            both = jnp.dot(lhs[...], w_in[:, columns(chunk)], preferred_element_type=jnp.float32)
            preact = both[:ROWS]
            preact_t = both[ROWS:] + jnp.dot(lhs[:ROWS], probe[:, columns(chunk)], preferred_element_type=jnp.float32)
            normal_cdf = 0.5 * (1.0 + lax.erf(preact * SQRT_HALF))
            density = INV_ROOT_TWO_PI * jnp.exp(-0.5 * preact * preact)
            slope = normal_cdf + preact * density
            slope_out[0, :, columns(chunk)] = slope
            slope_out[1, :, columns(chunk)] = density * (2.0 - preact * preact) * preact_t
            hidden = jnp.concatenate([preact * normal_cdf, slope * preact_t], axis=0).astype(jnp.bfloat16)
            acc[...] += jnp.dot(hidden, w_out[columns(chunk), :], preferred_element_type=jnp.float32)
            return carry

        lax.fori_loop(0, CHUNKS, step, 0, unroll=UNROLL)
        if last:
            pair_out[0] = ((acc[:ROWS] - goal[...].astype(jnp.float32)) / TOKENS).astype(jnp.bfloat16)
            pair_out[1] = (acc[ROWS:] / TOKENS).astype(jnp.bfloat16)
        else:
            pair_out[0] = acc[:ROWS].astype(jnp.bfloat16)
            pair_out[1] = acc[ROWS:].astype(jnp.bfloat16)


NORM = jax.ShapeDtypeStruct((2, ROWS, FEATURES), jnp.float32)
STAT = jax.ShapeDtypeStruct((2, ROWS, 128), jnp.float32)
SLOPE = jax.ShapeDtypeStruct((2, ROWS, HIDDEN), jnp.float32)
PAIR = jax.ShapeDtypeStruct((2, ROWS, FEATURES), jnp.bfloat16)
GRADS = jax.ShapeDtypeStruct((2 * ROWS, HIDDEN), jnp.bfloat16)
PARAMS = pltpu.CompilerParams(vmem_limit_bytes=VMEM_BYTES)


def forward_call(tick, section, pair, w_in, probe, w_out, goal):
    last = tick == LAYERS - 1
    operands = [section, pair, w_in, probe, w_out] + ([goal] if last else [])
    return pl.pallas_call(
        functools.partial(forward_kernel, tick),
        out_shape=[PAIR, NORM, STAT, SLOPE],
        in_specs=[SMEM] + [WHOLE] * (len(operands) - 1),
        out_specs=[WHOLE] * 4,
        scratch_shapes=[
            pltpu.VMEM((2 * ROWS, FEATURES), jnp.bfloat16),
            pltpu.VMEM((2 * ROWS, FEATURES), jnp.float32),
        ],
        compiler_params=PARAMS,
        name=f"layer_up_{tick}",
    )(*operands)


def hidden_grads(pair, w_out, slope, chunk):
    both = lax.dot_general(
        pair[...].reshape(2 * ROWS, FEATURES),
        w_out[columns(chunk), :],
        CONTRACT_LAST,
        preferred_element_type=jnp.float32,
    )
    grad_hidden, grad_hidden_t = both[:ROWS], both[ROWS:]
    slope_chunk = slope[0, :, columns(chunk)]
    grad_pre = grad_hidden * slope_chunk
    grad_pre_t = grad_hidden_t * slope_chunk + grad_hidden * slope[1, :, columns(chunk)]
    return grad_pre.astype(jnp.bfloat16), grad_pre_t.astype(jnp.bfloat16)


def norm_apply(values, normed, rscale):
    return rscale * (values - row_mean(values) - normed * row_mean(normed * values))


def backward_kernel(tick, *refs):
    section, pair, w_in, probe, w_out, norm, stat, slope = refs[:8]
    pair_out, grads, acc, acc_t = refs[8:]

    @pl.when(section[0] == LAYERS - 1 - tick)
    def _():
        acc[...] = jnp.zeros_like(acc)
        acc_t[...] = jnp.zeros_like(acc_t)

        def step(chunk, carry):
            low_grad, low_grad_t = hidden_grads(pair, w_out, slope, chunk)
            both = jnp.concatenate([low_grad_t, low_grad], axis=0)
            grads[:, columns(chunk)] = both
            acc[...] += lax.dot_general(
                both, w_in[:, columns(chunk)], CONTRACT_LAST, preferred_element_type=jnp.float32
            )
            acc_t[...] += lax.dot_general(
                low_grad, probe[:, columns(chunk)], CONTRACT_LAST, preferred_element_type=jnp.float32
            )
            return carry

        lax.fori_loop(0, CHUNKS, step, 0, unroll=UNROLL)
        normed, normed_t = norm[0], norm[1]
        rscale, tangent_dot = stat[0][:, :1], stat[1][:, :1]
        grad_norm = acc[ROWS:]
        grad_norm_t = acc[:ROWS] + acc_t[...]
        through = norm_apply(grad_norm, normed, rscale)
        through_t = (
            norm_apply(grad_norm_t, normed, rscale)
            - rscale * tangent_dot * through
            - rscale * (normed_t * row_mean(normed * grad_norm) + normed * row_mean(normed_t * grad_norm))
        )
        pair_out[0] = (pair[0].astype(jnp.float32) + through).astype(jnp.bfloat16)
        pair_out[1] = (pair[1].astype(jnp.float32) + through_t).astype(jnp.bfloat16)


def backward_call(tick, section, pair, w_in, probe, w_out, kept):
    operands = [section, pair, w_in, probe, w_out, *kept]
    return pl.pallas_call(
        functools.partial(backward_kernel, tick),
        out_shape=[PAIR, GRADS],
        in_specs=[SMEM] + [WHOLE] * (len(operands) - 1),
        out_specs=[WHOLE] * 2,
        scratch_shapes=[
            pltpu.VMEM((2 * ROWS, FEATURES), jnp.float32),
            pltpu.VMEM((ROWS, FEATURES), jnp.float32),
        ],
        compiler_params=PARAMS,
        name=f"layer_down_{tick}",
    )(*operands)


def core_half(index):
    return pl.ds(pl.multiple_of(index * (FEATURES // 2), FEATURES // 2), FEATURES // 2)


def curvature_kernel(final, *refs):
    section, core, pair, w_out, slope = refs[:5]
    norms, refs = refs[5 : 5 + LAYERS], refs[5 + LAYERS :]
    grads, refs = refs[: LAYERS - 1], refs[LAYERS - 1 :]
    if final:
        away_in, stay_in, refs = refs[0], refs[1], refs[2:]
    away, stay, lhs, rhs = refs
    for layer in range(LAYERS):

        @pl.when(section[0] == layer)
        def _():
            lhs[...] = norms[layer][...].reshape(2 * ROWS, FEATURES).astype(jnp.bfloat16)
            if layer:
                rhs[...] = grads[LAYERS - 1 - layer][...]
            else:

                def bottom(chunk, carry):
                    low_grad, low_grad_t = hidden_grads(pair, w_out, slope, chunk)
                    rhs[:, columns(chunk)] = jnp.concatenate([low_grad_t, low_grad], axis=0)
                    return carry

                lax.fori_loop(0, CHUNKS, bottom, 0, unroll=UNROLL)

    def step(chunk, carry):
        now = columns(chunk)

        def product(half):
            return lax.dot_general(lhs[:, core_half(half)], rhs[:, now], CONTRACT_FIRST, preferred_element_type=jnp.float32)

        if final:
            away[:, now] = (away_in[:, now] + product(1 - core[0])).astype(jnp.bfloat16)
            stay[:, now] = stay_in[:, now] + product(core[0])
        else:
            away[:, now] = product(1 - core[0])
            stay[:, now] = product(core[0])
        return carry

    lax.fori_loop(0, CHUNKS, step, 0)


def curvature_call(section, core, pair, w_out, slope, norms, grads, sums):
    half = (FEATURES // 2, HIDDEN)
    final = bool(sums)
    operands = [section, core, pair, w_out, slope, *norms, *grads, *sums]
    return pl.pallas_call(
        functools.partial(curvature_kernel, final),
        out_shape=[
            jax.ShapeDtypeStruct(half, jnp.bfloat16 if final else jnp.float32),
            jax.ShapeDtypeStruct(half, jnp.float32),
        ],
        in_specs=[SMEM, SMEM] + [WHOLE] * (len(operands) - 2),
        out_specs=[WHOLE] * 2,
        scratch_shapes=[
            pltpu.VMEM((2 * ROWS, FEATURES), jnp.bfloat16),
            pltpu.VMEM((2 * ROWS, HIDDEN), jnp.bfloat16),
        ],
        compiler_params=PARAMS,
        name="curvature_last" if final else "curvature_first",
    )(*operands)


def shards(inputs, targets, w_in, w_out, probes):
    section = jnp.reshape(lax.axis_index(SECTION), (1,)).astype(jnp.int32)
    core = jnp.reshape(lax.axis_index("c"), (1,)).astype(jnp.int32)
    order = feature_order()
    full_in = gathered(w_in[0])
    full_out = gathered(jnp.dot(w_out[0], order))
    full_out = (
        full_out.reshape(2, 4, 2, 2, 2, 32, FEATURES).transpose(4, 3, 2, 1, 0, 5, 6).reshape(HIDDEN, FEATURES)
    )
    probe = lax.dot_general(order, probes[0], CONTRACT_FIRST, preferred_element_type=jnp.bfloat16)
    fresh = jnp.dot(inputs, order)
    goal = jnp.dot(routed(targets, swap_b4), order)
    pairs, goals, kept, grads = [], [], [], []
    for micro in range(MICRO):
        rows = slice(micro * ROWS, (micro + 1) * ROWS)
        pairs.append(jnp.stack([fresh[rows], jnp.zeros_like(fresh[rows])]))
        goals.append(goal[rows])
        kept.append([])
        grads.append([])
    for tick in range(LAYERS):
        for micro in range(MICRO):
            pairs[micro], *stores = forward_call(
                tick, section, pairs[micro], full_in, probe, full_out, goals[micro]
            )
            kept[micro].append(stores)
            if tick < LAYERS - 1:
                pairs[micro] = routed(pairs[micro], up_from(tick))
    for tick in range(LAYERS - 1):
        for micro in range(MICRO):
            pairs[micro], low_grads = backward_call(
                tick, section, pairs[micro], full_in, probe, full_out, kept[micro][LAYERS - 1 - tick]
            )
            grads[micro].append(low_grads)
            pairs[micro] = routed(pairs[micro], down_from(LAYERS - 1 - tick))
    sums = ()
    for micro in range(MICRO):
        norms = [stores[0] for stores in kept[micro]]
        sums = curvature_call(
            section, core, pairs[micro], full_out, kept[micro][0][2], norms, grads[micro], sums
        )
    away, stay = sums
    summed = (stay + routed(away, swap_core).astype(jnp.float32)).astype(jnp.bfloat16)
    summed = lax.all_to_all(summed.reshape(4, 64, HIDDEN), "y", 0, 0, tiled=True)
    summed = jnp.sum(summed.astype(jnp.float32), axis=0).astype(jnp.bfloat16)
    summed = lax.all_to_all(summed.reshape(8, 8, HIDDEN), ("b1", "b2", "b4"), 0, 0, tiled=True)
    summed = jnp.sum(summed.astype(jnp.float32), axis=0)
    probe_own = lax.dynamic_slice_in_dim(probes[0], lax.axis_index(DP) * 8, 8, 0)
    return (probe_own.astype(jnp.float32) * summed)[None]


def solution(mesh):
    fine = Mesh(mesh.devices.reshape(SIZES), NAMES)
    return jax.shard_map(
        shards,
        mesh=fine,
        in_specs=(
            P(DP, None),
            P(DP, None),
            P(SECTION, DP, None),
            P(SECTION, DP, None),
            P(SECTION, None, None),
        ),
        out_specs=P(SECTION, DP, None),
        check_vma=False,
    )
```

```python
import functools
import itertools

import jax
import jax.numpy as jnp
from jax import lax
from jax.experimental import pallas as pl
from jax.experimental.pallas import tpu as pltpu
from jax.sharding import Mesh, PartitionSpec as P

EPSILON = 1e-05
SQRT_HALF = 0.7071067811865476
INV_ROOT_TWO_PI = 0.3989422804014327
CONTRACT_LAST = (((1,), (1,)), ((), ()))
CONTRACT_FIRST = (((0,), (0,)), ((), ()))

NAMES = ("zh", "x", "b4", "b2", "b1", "y", "c")
SIZES = (2, 4, 2, 2, 2, 4, 2)
SECTION = ("zh", "x")
DP = ("b4", "b2", "b1", "y", "c")
LAYERS = 8
FEATURES = 512
HIDDEN = 2048
MICRO = 2
ROWS = 64
UNROLL = 2
TOKENS = 8192
CHUNK = 512
CHUNKS = HIDDEN // CHUNK
VMEM_BYTES = 8 * 1024 * 1024
WHOLE = pl.BlockSpec(memory_space=pltpu.VMEM)
SMEM = pl.BlockSpec(memory_space=pltpu.SMEM)


def flat(place):
    index = 0
    for size, at in zip(SIZES, place):
        index = index * size + at
    return index


def routed(value, route):
    pairs = []
    for place in itertools.product(*(range(size) for size in SIZES)):
        there = route(*place)
        if there is not None:
            pairs.append((flat(place), flat(there)))
    return lax.ppermute(value, NAMES, pairs)


def swap_b4(zh, x, b4, b2, b1, y, c):
    return (zh, x, 1 - b4, b2, b1, y, c)


def goal_route(zh, x, b4, b2, b1, y, c):
    return (zh, x, 1 - b4, b2, b1, y, c) if (zh, x) == (1, 3) else None


def swap_b2(zh, x, b4, b2, b1, y, c):
    return (zh, x, b4, 1 - b2, b1, y, c)


def swap_b1(zh, x, b4, b2, b1, y, c):
    return (zh, x, b4, b2, 1 - b1, y, c)


def swap_even(zh, x, b4, b2, b1, y, c):
    return (zh, x, b4, b2, b1, y ^ 1, c)


def swap_odd(zh, x, b4, b2, b1, y, c):
    return (zh, x, b4, b2, b1, y ^ 3, c)


def swap_core(zh, x, b4, b2, b1, y, c):
    return (zh, x, b4, b2, b1, y, 1 - c)


def up_from(section):
    def route(zh, x, b4, b2, b1, y, c):
        if x != section % 4 or (x == 3 and zh == 1):
            return None
        if x == 3:
            return (1, 0, 1 - b4, b2, b1, y, c)
        return (zh, x + 1, b4, b2, b1, y, c)

    return route


def down_from(section):
    def route(zh, x, b4, b2, b1, y, c):
        if x != section % 4 or (x == 0 and zh == 0):
            return None
        if x == 0:
            return (0, 3, 1 - b4, b2, b1, y, c)
        return (zh, x - 1, b4, b2, b1, y, c)

    return route


def merged(own, other, bit):
    first = bit == 0
    return jnp.concatenate([jnp.where(first, own, other), jnp.where(first, other, own)], axis=0)


def gathered(block):
    block = merged(block, routed(block, swap_b4), lax.axis_index("b4"))
    block = merged(block, routed(block, swap_b2), lax.axis_index("b2"))
    block = merged(block, routed(block, swap_b1), lax.axis_index("b1"))
    rows, half = block.shape[0], block.shape[1] // 2
    y = lax.axis_index("y")
    left, right = block[:, :half], block[:, half:]
    left_two = merged(left, routed(left, swap_even), y % 2)
    right_two = merged(right, routed(right, swap_odd), y // 2)
    left_four = merged(left_two, routed(left_two, swap_odd), y // 2)
    other = routed(right_two, swap_even)
    outer = (y == 0) | (y == 3)
    own_a, own_b, oth_a, oth_b = right_two[:rows], right_two[rows:], other[:rows], other[rows:]
    right_four = jnp.concatenate(
        [
            jnp.where(outer, own_a, oth_a),
            jnp.where(outer, oth_a, own_a),
            jnp.where(outer, oth_b, own_b),
            jnp.where(outer, own_b, oth_b),
        ],
        axis=0,
    )
    half = jnp.concatenate([left_four, right_four], axis=1)
    return merged(half, routed(half, swap_core), lax.axis_index("c"))


def feature_order():
    position = lax.broadcasted_iota(jnp.int32, (FEATURES, FEATURES), 1)
    natural = lax.broadcasted_iota(jnp.int32, (FEATURES, FEATURES), 0)
    core, y = position // 256, (position // 64) % 4
    b1, b2, b4, row = (position // 32) % 2, (position // 16) % 2, (position // 8) % 2, position % 8
    return (natural == (b4 * 4 + b2 * 2 + b1) * 64 + y * 16 + core * 8 + row).astype(jnp.bfloat16)


def row_mean(values):
    return jnp.mean(values, axis=-1, keepdims=True)


def columns(chunk):
    return pl.ds(pl.multiple_of(chunk * CHUNK, CHUNK), CHUNK)


def forward_kernel(tick, *refs):
    last = tick == LAYERS - 1
    section, pair, w_in, probe, w_out = refs[:5]
    refs = refs[5:]
    if last:
        goal, refs = refs[0], refs[1:]
    pair_out, norm, stat, slope_out, lhs, acc = refs

    @pl.when(section[0] == tick)
    def _():
        inflow = pair[0].astype(jnp.float32)
        inflow_t = pair[1].astype(jnp.float32)
        centred = inflow - row_mean(inflow)
        rscale = lax.rsqrt(row_mean(centred * centred) + EPSILON)
        normed = centred * rscale
        tangent_dot = row_mean(normed * inflow_t)
        normed_t = rscale * (inflow_t - row_mean(inflow_t) - normed * tangent_dot)
        norm[0] = normed
        norm[1] = normed_t
        stat[0] = jnp.broadcast_to(rscale, (ROWS, 128))
        stat[1] = jnp.broadcast_to(tangent_dot, (ROWS, 128))
        lhs[:ROWS] = normed.astype(jnp.bfloat16)
        lhs[ROWS:] = normed_t.astype(jnp.bfloat16)
        acc[:ROWS] = inflow
        acc[ROWS:] = inflow_t

        def step(chunk, carry):
            both = jnp.dot(lhs[...], w_in[:, columns(chunk)], preferred_element_type=jnp.float32)
            preact = both[:ROWS]
            preact_t = both[ROWS:] + jnp.dot(lhs[:ROWS], probe[:, columns(chunk)], preferred_element_type=jnp.float32)
            normal_cdf = 0.5 * (1.0 + lax.erf(preact * SQRT_HALF))
            density = INV_ROOT_TWO_PI * jnp.exp(-0.5 * preact * preact)
            slope = normal_cdf + preact * density
            slope_out[0, :, columns(chunk)] = slope
            slope_out[1, :, columns(chunk)] = density * (2.0 - preact * preact) * preact_t
            hidden = jnp.concatenate([preact * normal_cdf, slope * preact_t], axis=0).astype(jnp.bfloat16)
            acc[...] += jnp.dot(hidden, w_out[columns(chunk), :], preferred_element_type=jnp.float32)
            return carry

        lax.fori_loop(0, CHUNKS, step, 0, unroll=UNROLL)
        if last:
            pair_out[0] = ((acc[:ROWS] - goal[...].astype(jnp.float32)) / TOKENS).astype(jnp.bfloat16)
            pair_out[1] = (acc[ROWS:] / TOKENS).astype(jnp.bfloat16)
        else:
            pair_out[0] = acc[:ROWS].astype(jnp.bfloat16)
            pair_out[1] = acc[ROWS:].astype(jnp.bfloat16)


NORM = jax.ShapeDtypeStruct((2, ROWS, FEATURES), jnp.float32)
STAT = jax.ShapeDtypeStruct((2, ROWS, 128), jnp.float32)
SLOPE = jax.ShapeDtypeStruct((2, ROWS, HIDDEN), jnp.float32)
PAIR = jax.ShapeDtypeStruct((2, ROWS, FEATURES), jnp.bfloat16)
GRADS = jax.ShapeDtypeStruct((2 * ROWS, HIDDEN), jnp.bfloat16)
PARAMS = pltpu.CompilerParams(vmem_limit_bytes=VMEM_BYTES)


def forward_call(tick, section, pair, w_in, probe, w_out, goal):
    last = tick == LAYERS - 1
    operands = [section, pair, w_in, probe, w_out] + ([goal] if last else [])
    return pl.pallas_call(
        functools.partial(forward_kernel, tick),
        out_shape=[PAIR, NORM, STAT, SLOPE],
        in_specs=[SMEM] + [WHOLE] * (len(operands) - 1),
        out_specs=[WHOLE] * 4,
        scratch_shapes=[
            pltpu.VMEM((2 * ROWS, FEATURES), jnp.bfloat16),
            pltpu.VMEM((2 * ROWS, FEATURES), jnp.float32),
        ],
        compiler_params=PARAMS,
        name=f"layer_up_{tick}",
    )(*operands)


def hidden_grads(pair, w_out, slope, chunk):
    both = lax.dot_general(
        pair[...].reshape(2 * ROWS, FEATURES),
        w_out[columns(chunk), :],
        CONTRACT_LAST,
        preferred_element_type=jnp.float32,
    )
    grad_hidden, grad_hidden_t = both[:ROWS], both[ROWS:]
    slope_chunk = slope[0, :, columns(chunk)]
    grad_pre = grad_hidden * slope_chunk
    grad_pre_t = grad_hidden_t * slope_chunk + grad_hidden * slope[1, :, columns(chunk)]
    return grad_pre.astype(jnp.bfloat16), grad_pre_t.astype(jnp.bfloat16)


def norm_apply(values, normed, rscale):
    return rscale * (values - row_mean(values) - normed * row_mean(normed * values))


def backward_kernel(tick, *refs):
    section, pair, w_in, probe, w_out, norm, stat, slope = refs[:8]
    pair_out, grads, acc, acc_t = refs[8:]

    @pl.when(section[0] == LAYERS - 1 - tick)
    def _():
        acc[...] = jnp.zeros_like(acc)
        acc_t[...] = jnp.zeros_like(acc_t)

        def step(chunk, carry):
            low_grad, low_grad_t = hidden_grads(pair, w_out, slope, chunk)
            both = jnp.concatenate([low_grad_t, low_grad], axis=0)
            grads[:, columns(chunk)] = both
            acc[...] += lax.dot_general(
                both, w_in[:, columns(chunk)], CONTRACT_LAST, preferred_element_type=jnp.float32
            )
            acc_t[...] += lax.dot_general(
                low_grad, probe[:, columns(chunk)], CONTRACT_LAST, preferred_element_type=jnp.float32
            )
            return carry

        lax.fori_loop(0, CHUNKS, step, 0, unroll=UNROLL)
        normed, normed_t = norm[0], norm[1]
        rscale, tangent_dot = stat[0][:, :1], stat[1][:, :1]
        grad_norm = acc[ROWS:]
        grad_norm_t = acc[:ROWS] + acc_t[...]
        through = norm_apply(grad_norm, normed, rscale)
        through_t = (
            norm_apply(grad_norm_t, normed, rscale)
            - rscale * tangent_dot * through
            - rscale * (normed_t * row_mean(normed * grad_norm) + normed * row_mean(normed_t * grad_norm))
        )
        pair_out[0] = (pair[0].astype(jnp.float32) + through).astype(jnp.bfloat16)
        pair_out[1] = (pair[1].astype(jnp.float32) + through_t).astype(jnp.bfloat16)


def backward_call(tick, section, pair, w_in, probe, w_out, kept):
    operands = [section, pair, w_in, probe, w_out, *kept]
    return pl.pallas_call(
        functools.partial(backward_kernel, tick),
        out_shape=[PAIR, GRADS],
        in_specs=[SMEM] + [WHOLE] * (len(operands) - 1),
        out_specs=[WHOLE] * 2,
        scratch_shapes=[
            pltpu.VMEM((2 * ROWS, FEATURES), jnp.float32),
            pltpu.VMEM((ROWS, FEATURES), jnp.float32),
        ],
        compiler_params=PARAMS,
        name=f"layer_down_{tick}",
    )(*operands)


def core_half(index):
    return pl.ds(pl.multiple_of(index * (FEATURES // 2), FEATURES // 2), FEATURES // 2)


def curvature_kernel(final, *refs):
    section, core, pair, w_out, slope = refs[:5]
    norms, refs = refs[5 : 5 + LAYERS], refs[5 + LAYERS :]
    grads, refs = refs[: LAYERS - 1], refs[LAYERS - 1 :]
    if final:
        away_in, stay_in, refs = refs[0], refs[1], refs[2:]
    away, stay, lhs, rhs = refs
    for layer in range(LAYERS):

        @pl.when(section[0] == layer)
        def _():
            lhs[...] = norms[layer][...].reshape(2 * ROWS, FEATURES).astype(jnp.bfloat16)
            if layer:
                rhs[...] = grads[LAYERS - 1 - layer][...]
            else:

                def bottom(chunk, carry):
                    low_grad, low_grad_t = hidden_grads(pair, w_out, slope, chunk)
                    rhs[:, columns(chunk)] = jnp.concatenate([low_grad_t, low_grad], axis=0)
                    return carry

                lax.fori_loop(0, CHUNKS, bottom, 0, unroll=UNROLL)

    def step(chunk, carry):
        now = columns(chunk)

        def product(half):
            return lax.dot_general(lhs[:, core_half(half)], rhs[:, now], CONTRACT_FIRST, preferred_element_type=jnp.float32)

        if final:
            away[:, now] = (away_in[:, now] + product(1 - core[0])).astype(jnp.bfloat16)
            stay[:, now] = stay_in[:, now] + product(core[0])
        else:
            away[:, now] = product(1 - core[0])
            stay[:, now] = product(core[0])
        return carry

    lax.fori_loop(0, CHUNKS, step, 0)


def curvature_call(section, core, pair, w_out, slope, norms, grads, sums):
    half = (FEATURES // 2, HIDDEN)
    final = bool(sums)
    operands = [section, core, pair, w_out, slope, *norms, *grads, *sums]
    return pl.pallas_call(
        functools.partial(curvature_kernel, final),
        out_shape=[
            jax.ShapeDtypeStruct(half, jnp.bfloat16 if final else jnp.float32),
            jax.ShapeDtypeStruct(half, jnp.float32),
        ],
        in_specs=[SMEM, SMEM] + [WHOLE] * (len(operands) - 2),
        out_specs=[WHOLE] * 2,
        scratch_shapes=[
            pltpu.VMEM((2 * ROWS, FEATURES), jnp.bfloat16),
            pltpu.VMEM((2 * ROWS, HIDDEN), jnp.bfloat16),
        ],
        compiler_params=PARAMS,
        name="curvature_last" if final else "curvature_first",
    )(*operands)


def shards(inputs, targets, w_in, w_out, probes):
    section = jnp.reshape(lax.axis_index(SECTION), (1,)).astype(jnp.int32)
    core = jnp.reshape(lax.axis_index("c"), (1,)).astype(jnp.int32)
    order = feature_order()
    full_in = gathered(w_in[0])
    full_out = gathered(jnp.dot(w_out[0], order))
    full_out = (
        full_out.reshape(2, 4, 2, 2, 2, 32, FEATURES).transpose(4, 3, 2, 1, 0, 5, 6).reshape(HIDDEN, FEATURES)
    )
    probe = lax.dot_general(order, probes[0], CONTRACT_FIRST, preferred_element_type=jnp.bfloat16)
    fresh = jnp.dot(inputs, order)
    goal = jnp.dot(routed(targets, goal_route), order)
    pairs, goals, kept, grads = [], [], [], []
    for micro in range(MICRO):
        rows = slice(micro * ROWS, (micro + 1) * ROWS)
        pairs.append(jnp.stack([fresh[rows], jnp.zeros_like(fresh[rows])]))
        goals.append(goal[rows])
        kept.append([])
        grads.append([])
    for tick in range(LAYERS):
        for micro in range(MICRO):
            pairs[micro], *stores = forward_call(
                tick, section, pairs[micro], full_in, probe, full_out, goals[micro]
            )
            kept[micro].append(stores)
            if tick < LAYERS - 1:
                pairs[micro] = routed(pairs[micro], up_from(tick))
    for tick in range(LAYERS - 1):
        for micro in range(MICRO):
            pairs[micro], low_grads = backward_call(
                tick, section, pairs[micro], full_in, probe, full_out, kept[micro][LAYERS - 1 - tick]
            )
            grads[micro].append(low_grads)
            pairs[micro] = routed(pairs[micro], down_from(LAYERS - 1 - tick))
    sums = ()
    for micro in range(MICRO):
        norms = [stores[0] for stores in kept[micro]]
        sums = curvature_call(
            section, core, pairs[micro], full_out, kept[micro][0][2], norms, grads[micro], sums
        )
    away, stay = sums
    summed = (stay + routed(away, swap_core).astype(jnp.float32)).astype(jnp.bfloat16)
    summed = lax.all_to_all(summed.reshape(4, 64, HIDDEN), "y", 0, 0, tiled=True)
    summed = jnp.sum(summed.astype(jnp.float32), axis=0).astype(jnp.bfloat16)
    summed = lax.all_to_all(summed.reshape(8, 8, HIDDEN), ("b1", "b2", "b4"), 0, 0, tiled=True)
    summed = jnp.sum(summed.astype(jnp.float32), axis=0)
    probe_own = lax.dynamic_slice_in_dim(probes[0], lax.axis_index(DP) * 8, 8, 0)
    return (probe_own.astype(jnp.float32) * summed)[None]


def solution(mesh):
    fine = Mesh(mesh.devices.reshape(SIZES), NAMES)
    return jax.shard_map(
        shards,
        mesh=fine,
        in_specs=(
            P(DP, None),
            P(DP, None),
            P(SECTION, DP, None),
            P(SECTION, DP, None),
            P(SECTION, None, None),
        ),
        out_specs=P(SECTION, DP, None),
        check_vma=False,
    )
```

```python
import functools
import itertools

import jax
import jax.numpy as jnp
import numpy as np
from jax import lax
from jax.experimental import pallas as pl
from jax.experimental.pallas import tpu as pltpu
from jax.sharding import Mesh, PartitionSpec as P

EPSILON = 1e-05
SQRT_HALF = 0.7071067811865476
INV_ROOT_TWO_PI = 0.3989422804014327
CONTRACT_FIRST = (((0,), (0,)), ((), ()))

NAMES = ("zh", "x", "b4", "b2", "b1", "y", "c")
SIZES = (2, 4, 2, 2, 2, 4, 2)
SECTION = ("zh", "x")
DP = ("b4", "b2", "b1", "y", "c")
LAYERS = 8
FEATURES = 512
HIDDEN = 2048
MICRO = 2
ROWS = 64
UNROLL = 2
TURN_TICK = 3
TOKENS = 8192
CHUNK = 1024
CHUNKS = HIDDEN // CHUNK
VMEM_BYTES = 8 * 1024 * 1024
WHOLE = pl.BlockSpec(memory_space=pltpu.VMEM)
SMEM = pl.BlockSpec(memory_space=pltpu.SMEM)


def flat(place):
    index = 0
    for size, at in zip(SIZES, place):
        index = index * size + at
    return index


def routed(value, route):
    pairs = []
    for place in itertools.product(*(range(size) for size in SIZES)):
        there = route(*place)
        if there is not None:
            pairs.append((flat(place), flat(there)))
    return lax.ppermute(value, NAMES, pairs)


def swap_b4(zh, x, b4, b2, b1, y, c):
    return (zh, x, 1 - b4, b2, b1, y, c)


def goal_route(zh, x, b4, b2, b1, y, c):
    return (zh, x, 1 - b4, b2, b1, y, c) if (zh, x) == (1, 3) else None


def swap_b2(zh, x, b4, b2, b1, y, c):
    return (zh, x, b4, 1 - b2, b1, y, c)


def swap_b1(zh, x, b4, b2, b1, y, c):
    return (zh, x, b4, b2, 1 - b1, y, c)


def swap_even(zh, x, b4, b2, b1, y, c):
    return (zh, x, b4, b2, b1, y ^ 1, c)


def swap_odd(zh, x, b4, b2, b1, y, c):
    return (zh, x, b4, b2, b1, y ^ 3, c)


def swap_core(zh, x, b4, b2, b1, y, c):
    return (zh, x, b4, b2, b1, y, 1 - c)


def up_from(section):
    def route(zh, x, b4, b2, b1, y, c):
        if x != section % 4 or (x == 3 and zh == 1):
            return None
        if x == 3:
            return (1, 0, 1 - b4, b2, b1, y, c)
        return (zh, x + 1, b4, b2, b1, y, c)

    return route


def down_from(section):
    def route(zh, x, b4, b2, b1, y, c):
        if x != section % 4 or (x == 0 and zh == 0):
            return None
        if x == 0:
            return (0, 3, 1 - b4, b2, b1, y, c)
        return (zh, x - 1, b4, b2, b1, y, c)

    return route


def merged(own, other, bit):
    first = bit == 0
    return jnp.concatenate([jnp.where(first, own, other), jnp.where(first, other, own)], axis=0)


def merged_outer(own, other):
    y = lax.axis_index("y")
    outer = (y == 0) | (y == 3)
    rows = own.shape[0] // 2
    own_a, own_b, oth_a, oth_b = own[:rows], own[rows:], other[:rows], other[rows:]
    return jnp.concatenate(
        [
            jnp.where(outer, own_a, oth_a),
            jnp.where(outer, oth_a, own_a),
            jnp.where(outer, oth_b, own_b),
            jnp.where(outer, own_b, oth_b),
        ],
        axis=0,
    )


def gathered(block, even_first):
    block = merged(block, routed(block, swap_b4), lax.axis_index("b4"))
    block = merged(block, routed(block, swap_b2), lax.axis_index("b2"))
    block = merged(block, routed(block, swap_b1), lax.axis_index("b1"))
    y = lax.axis_index("y")
    if even_first:
        block = merged(block, routed(block, swap_even), y % 2)
        block = merged(block, routed(block, swap_odd), y // 2)
    else:
        block = merged(block, routed(block, swap_odd), y // 2)
        block = merged_outer(block, routed(block, swap_even))
    return merged(block, routed(block, swap_core), lax.axis_index("c"))


def feature_order():
    position = np.arange(FEATURES)
    core, y = position // 256, (position // 64) % 4
    b1, b2, b4, row = (position // 32) % 2, (position // 16) % 2, (position // 8) % 2, position % 8
    natural = (b4 * 4 + b2 * 2 + b1) * 64 + y * 16 + core * 8 + row
    one_hot = np.zeros((FEATURES, FEATURES), np.float32)
    one_hot[natural, position] = 1.0
    return jnp.asarray(one_hot.astype(jnp.bfloat16))


def row_mean(values):
    return jnp.mean(values, axis=-1, keepdims=True)


def columns(chunk):
    return pl.ds(pl.multiple_of(chunk * CHUNK, CHUNK), CHUNK)


def forward_kernel(tick, *refs):
    first, last = tick == 0, tick == LAYERS - 1
    section, pair, w_in, probe, w_out, order = refs[:6]
    refs = refs[6:]
    if last:
        goal, refs = refs[0], refs[1:]
    pair_out, norm, stat, slope_out, lhs, natural, acc = refs

    @pl.when(section[0] == tick)
    def _():
        if first:
            inflow = pair[...].astype(jnp.float32)
        else:
            inflow = pair[0].astype(jnp.float32)
        centred = inflow - row_mean(inflow)
        rscale = lax.rsqrt(row_mean(centred * centred) + EPSILON)
        normed = centred * rscale
        if first:
            natural[...] = normed.astype(jnp.bfloat16)
            placed = jnp.dot(natural[...], order[...], preferred_element_type=jnp.float32)
            norm[0] = placed
            norm[1] = jnp.zeros_like(placed)
            lhs[:ROWS] = placed.astype(jnp.bfloat16)
            acc[:ROWS] = jnp.dot(pair[...], order[...], preferred_element_type=jnp.float32)
            acc[ROWS:] = jnp.zeros_like(placed)
        else:
            inflow_t = pair[1].astype(jnp.float32)
            tangent_dot = row_mean(normed * inflow_t)
            normed_t = rscale * (inflow_t - row_mean(inflow_t) - normed * tangent_dot)
            norm[0] = normed
            norm[1] = normed_t
            stat[0] = jnp.broadcast_to(rscale, (ROWS, 128))
            stat[1] = jnp.broadcast_to(tangent_dot, (ROWS, 128))
            lhs[:ROWS] = normed.astype(jnp.bfloat16)
            lhs[ROWS:] = normed_t.astype(jnp.bfloat16)
            acc[:ROWS] = inflow
            acc[ROWS:] = inflow_t
            natural[...] = lax.dot_general(
                lhs[:ROWS], order[...], (((1,), (1,)), ((), ())), preferred_element_type=jnp.float32
            ).astype(jnp.bfloat16)

        def step(chunk, carry):
            preact_t = jnp.dot(natural[...], probe[:, columns(chunk)], preferred_element_type=jnp.float32)
            if first:
                preact = jnp.dot(lhs[:ROWS], w_in[:, columns(chunk)], preferred_element_type=jnp.float32)
            else:
                both = jnp.dot(lhs[...], w_in[:, columns(chunk)], preferred_element_type=jnp.float32)
                preact = both[:ROWS]
                preact_t = both[ROWS:] + preact_t
            normal_cdf = 0.5 * (1.0 + lax.erf(preact * SQRT_HALF))
            density = INV_ROOT_TWO_PI * jnp.exp(-0.5 * preact * preact)
            slope = normal_cdf + preact * density
            slope_out[0, :, columns(chunk)] = slope
            slope_out[1, :, columns(chunk)] = density * (2.0 - preact * preact) * preact_t
            hidden = jnp.concatenate([preact * normal_cdf, slope * preact_t], axis=0).astype(jnp.bfloat16)
            acc[...] += jnp.dot(hidden, w_out[columns(chunk), :], preferred_element_type=jnp.float32)
            return carry

        lax.fori_loop(0, CHUNKS, step, 0, unroll=UNROLL)
        if last:
            pair_out[0] = ((acc[:ROWS] - goal[...].astype(jnp.float32)) / TOKENS).astype(jnp.bfloat16)
            pair_out[1] = (acc[ROWS:] / TOKENS).astype(jnp.bfloat16)
        else:
            pair_out[0] = acc[:ROWS].astype(jnp.bfloat16)
            pair_out[1] = acc[ROWS:].astype(jnp.bfloat16)


NORM = jax.ShapeDtypeStruct((2, ROWS, FEATURES), jnp.float32)
STAT = jax.ShapeDtypeStruct((2, ROWS, 128), jnp.float32)
SLOPE = jax.ShapeDtypeStruct((2, ROWS, HIDDEN), jnp.float32)
PAIR = jax.ShapeDtypeStruct((2, ROWS, FEATURES), jnp.bfloat16)
GRADS = jax.ShapeDtypeStruct((2 * ROWS, HIDDEN), jnp.bfloat16)
PARAMS = pltpu.CompilerParams(vmem_limit_bytes=VMEM_BYTES)


def forward_call(tick, section, pair, w_in, probe, w_out, order, goal):
    last = tick == LAYERS - 1
    operands = [section, pair, w_in, probe, w_out, order] + ([goal] if last else [])
    return pl.pallas_call(
        functools.partial(forward_kernel, tick),
        out_shape=[PAIR, NORM, STAT, SLOPE],
        in_specs=[SMEM] + [WHOLE] * (len(operands) - 1),
        out_specs=[WHOLE] * 4,
        scratch_shapes=[
            pltpu.VMEM((2 * ROWS, FEATURES), jnp.bfloat16),
            pltpu.VMEM((ROWS, FEATURES), jnp.bfloat16),
            pltpu.VMEM((2 * ROWS, FEATURES), jnp.float32),
        ],
        compiler_params=PARAMS,
        name=f"layer_up_{tick}",
    )(*operands)


def turned_kernel(w_in, probe, w_out, order, token, w_in_t, probe_t, w_out_t):
    probe_t[...] = lax.dot_general(
        probe[...], order[...], CONTRACT_FIRST, preferred_element_type=jnp.float32
    ).astype(jnp.bfloat16)
    w_in_t[...] = w_in[...].T
    w_out_t[...] = w_out[...].T


def turned_call(w_in, probe, w_out, order, token):
    tall = jax.ShapeDtypeStruct((HIDDEN, FEATURES), jnp.bfloat16)
    wide = jax.ShapeDtypeStruct((FEATURES, HIDDEN), jnp.bfloat16)
    return pl.pallas_call(
        turned_kernel,
        out_shape=[tall, tall, wide],
        in_specs=[WHOLE] * 4 + [pl.BlockSpec(memory_space=pl.ANY)],
        out_specs=[WHOLE] * 3,
        compiler_params=PARAMS,
        name="turned_weights",
    )(w_in, probe, w_out, order, token)


def hidden_grads(pair, w_out_t, slope, chunk):
    both = jnp.dot(
        pair[...].reshape(2 * ROWS, FEATURES), w_out_t[:, columns(chunk)], preferred_element_type=jnp.float32
    )
    grad_hidden, grad_hidden_t = both[:ROWS], both[ROWS:]
    slope_chunk = slope[0, :, columns(chunk)]
    grad_pre = grad_hidden * slope_chunk
    grad_pre_t = grad_hidden_t * slope_chunk + grad_hidden * slope[1, :, columns(chunk)]
    return grad_pre.astype(jnp.bfloat16), grad_pre_t.astype(jnp.bfloat16)


def norm_apply(values, normed, rscale):
    return rscale * (values - row_mean(values) - normed * row_mean(normed * values))


def backward_kernel(tick, *refs):
    section, pair, w_in_t, probe_t, w_out_t, norm, stat, slope = refs[:8]
    pair_out, grads, acc, acc_t = refs[8:]

    @pl.when(section[0] == LAYERS - 1 - tick)
    def _():
        acc[...] = jnp.zeros_like(acc)
        acc_t[...] = jnp.zeros_like(acc_t)

        def step(chunk, carry):
            low_grad, low_grad_t = hidden_grads(pair, w_out_t, slope, chunk)
            both = jnp.concatenate([low_grad_t, low_grad], axis=0)
            grads[:, columns(chunk)] = both
            acc[...] += jnp.dot(both, w_in_t[columns(chunk), :], preferred_element_type=jnp.float32)
            acc_t[...] += jnp.dot(low_grad, probe_t[columns(chunk), :], preferred_element_type=jnp.float32)
            return carry

        lax.fori_loop(0, CHUNKS, step, 0, unroll=UNROLL)
        normed, normed_t = norm[0], norm[1]
        rscale, tangent_dot = stat[0][:, :1], stat[1][:, :1]
        grad_norm = acc[ROWS:]
        grad_norm_t = acc[:ROWS] + acc_t[...]
        through = norm_apply(grad_norm, normed, rscale)
        through_t = (
            norm_apply(grad_norm_t, normed, rscale)
            - rscale * tangent_dot * through
            - rscale * (normed_t * row_mean(normed * grad_norm) + normed * row_mean(normed_t * grad_norm))
        )
        pair_out[0] = (pair[0].astype(jnp.float32) + through).astype(jnp.bfloat16)
        pair_out[1] = (pair[1].astype(jnp.float32) + through_t).astype(jnp.bfloat16)


def backward_call(tick, section, pair, w_in_t, probe_t, w_out_t, kept):
    operands = [section, pair, w_in_t, probe_t, w_out_t, *kept]
    return pl.pallas_call(
        functools.partial(backward_kernel, tick),
        out_shape=[PAIR, GRADS],
        in_specs=[SMEM] + [WHOLE] * (len(operands) - 1),
        out_specs=[WHOLE] * 2,
        scratch_shapes=[
            pltpu.VMEM((2 * ROWS, FEATURES), jnp.float32),
            pltpu.VMEM((ROWS, FEATURES), jnp.float32),
        ],
        compiler_params=PARAMS,
        name=f"layer_down_{tick}",
    )(*operands)


def core_half(index):
    return pl.ds(pl.multiple_of(index * (FEATURES // 2), FEATURES // 2), FEATURES // 2)


def curvature_kernel(final, *refs):
    section, core, pair, w_out_t, slope = refs[:5]
    norms, refs = refs[5 : 5 + LAYERS], refs[5 + LAYERS :]
    grads, refs = refs[: LAYERS - 1], refs[LAYERS - 1 :]
    if final:
        away_in, stay_in, refs = refs[0], refs[1], refs[2:]
    away, stay, lhs, rhs = refs
    for layer in range(LAYERS):

        @pl.when(section[0] == layer)
        def _():
            lhs[...] = norms[layer][...].reshape(2 * ROWS, FEATURES).astype(jnp.bfloat16)
            if layer:
                rhs[...] = grads[LAYERS - 1 - layer][...]
            else:

                def bottom(chunk, carry):
                    low_grad, low_grad_t = hidden_grads(pair, w_out_t, slope, chunk)
                    rhs[:, columns(chunk)] = jnp.concatenate([low_grad_t, low_grad], axis=0)
                    return carry

                lax.fori_loop(0, CHUNKS, bottom, 0, unroll=UNROLL)

    def step(chunk, carry):
        now = columns(chunk)

        def product(half):
            return lax.dot_general(lhs[:, core_half(half)], rhs[:, now], CONTRACT_FIRST, preferred_element_type=jnp.float32)

        if final:
            away[:, now] = (away_in[:, now] + product(1 - core[0])).astype(jnp.bfloat16)
            stay[:, now] = stay_in[:, now] + product(core[0])
        else:
            away[:, now] = product(1 - core[0])
            stay[:, now] = product(core[0])
        return carry

    lax.fori_loop(0, CHUNKS, step, 0)


def curvature_call(section, core, pair, w_out_t, slope, norms, grads, sums):
    half = (FEATURES // 2, HIDDEN)
    final = bool(sums)
    operands = [section, core, pair, w_out_t, slope, *norms, *grads, *sums]
    return pl.pallas_call(
        functools.partial(curvature_kernel, final),
        out_shape=[
            jax.ShapeDtypeStruct(half, jnp.bfloat16 if final else jnp.float32),
            jax.ShapeDtypeStruct(half, jnp.float32),
        ],
        in_specs=[SMEM, SMEM] + [WHOLE] * (len(operands) - 2),
        out_specs=[WHOLE] * 2,
        scratch_shapes=[
            pltpu.VMEM((2 * ROWS, FEATURES), jnp.bfloat16),
            pltpu.VMEM((2 * ROWS, HIDDEN), jnp.bfloat16),
        ],
        compiler_params=PARAMS,
        name="curvature_last" if final else "curvature_first",
    )(*operands)


def shards(inputs, targets, w_in, w_out, probes):
    section = jnp.reshape(lax.axis_index(SECTION), (1,)).astype(jnp.int32)
    core = jnp.reshape(lax.axis_index("c"), (1,)).astype(jnp.int32)
    order = feature_order()
    full_in = gathered(w_in[0], True)
    full_out = gathered(jnp.dot(w_out[0], order), False)
    full_out = (
        full_out.reshape(2, 4, 2, 2, 2, 32, FEATURES).transpose(4, 3, 2, 1, 0, 5, 6).reshape(HIDDEN, FEATURES)
    )
    probe = probes[0]
    goal = jnp.dot(routed(targets, goal_route), order)
    pairs, goals, kept, grads = [], [], [], []
    for micro in range(MICRO):
        rows = slice(micro * ROWS, (micro + 1) * ROWS)
        pairs.append(inputs[rows])
        goals.append(goal[rows])
        kept.append([])
        grads.append([])
    for tick in range(LAYERS):
        for micro in range(MICRO):
            pairs[micro], *stores = forward_call(
                tick, section, pairs[micro], full_in, probe, full_out, order, goals[micro]
            )
            kept[micro].append(stores)
            if tick < LAYERS - 1:
                pairs[micro] = routed(pairs[micro], up_from(tick))
        if tick == TURN_TICK:
            turned = turned_call(full_in, probe, full_out, order, kept[-1][tick][0])
    for tick in range(LAYERS - 1):
        for micro in range(MICRO):
            pairs[micro], low_grads = backward_call(
                tick, section, pairs[micro], *turned, kept[micro][LAYERS - 1 - tick]
            )
            grads[micro].append(low_grads)
            pairs[micro] = routed(pairs[micro], down_from(LAYERS - 1 - tick))
    sums = ()
    for micro in range(MICRO):
        norms = [stores[0] for stores in kept[micro]]
        sums = curvature_call(
            section, core, pairs[micro], turned[2], kept[micro][0][2], norms, grads[micro], sums
        )
    away, stay = sums
    summed = (stay + routed(away, swap_core).astype(jnp.float32)).astype(jnp.bfloat16)
    summed = lax.all_to_all(summed.reshape(4, 64, HIDDEN), "y", 0, 0, tiled=True)
    summed = jnp.sum(summed.astype(jnp.float32), axis=0).astype(jnp.bfloat16)
    summed = lax.all_to_all(summed.reshape(8, 8, HIDDEN), ("b1", "b2", "b4"), 0, 0, tiled=True)
    summed = jnp.sum(summed.astype(jnp.float32), axis=0)
    probe_own = lax.dynamic_slice_in_dim(probe, lax.axis_index(DP) * 8, 8, 0)
    return (probe_own.astype(jnp.float32) * summed)[None]


def solution(mesh):
    fine = Mesh(mesh.devices.reshape(SIZES), NAMES)
    return jax.shard_map(
        shards,
        mesh=fine,
        in_specs=(
            P(DP, None),
            P(DP, None),
            P(SECTION, DP, None),
            P(SECTION, DP, None),
            P(SECTION, None, None),
        ),
        out_specs=P(SECTION, DP, None),
        check_vma=False,
    )
```

```python
import functools
import itertools

import jax
import jax.numpy as jnp
from jax import lax
from jax.experimental import pallas as pl
from jax.experimental.pallas import tpu as pltpu
from jax.sharding import Mesh, PartitionSpec as P

EPSILON = 1e-05
SQRT_HALF = 0.7071067811865476
INV_ROOT_TWO_PI = 0.3989422804014327
CONTRACT_FIRST = (((0,), (0,)), ((), ()))

NAMES = ("zh", "x", "b4", "b2", "b1", "y", "c")
SIZES = (2, 4, 2, 2, 2, 4, 2)
SECTION = ("zh", "x")
DP = ("b4", "b2", "b1", "y", "c")
LAYERS = 8
FEATURES = 512
HIDDEN = 2048
MICRO = 2
ROWS = 128 // MICRO
UNROLL = 2
TURN_TICK = 3
TOKENS = 8192
CHUNK = 1024
CHUNKS = HIDDEN // CHUNK
VMEM_BYTES = 8 * 1024 * 1024
WHOLE = pl.BlockSpec(memory_space=pltpu.VMEM)
SMEM = pl.BlockSpec(memory_space=pltpu.SMEM)


def flat(place):
    index = 0
    for size, at in zip(SIZES, place):
        index = index * size + at
    return index


def routed(value, route):
    pairs = []
    for place in itertools.product(*(range(size) for size in SIZES)):
        there = route(*place)
        if there is not None:
            pairs.append((flat(place), flat(there)))
    return lax.ppermute(value, NAMES, pairs)


def swap_b4(zh, x, b4, b2, b1, y, c):
    return (zh, x, 1 - b4, b2, b1, y, c)


def goal_route(zh, x, b4, b2, b1, y, c):
    return (zh, x, 1 - b4, 1 - b2, 1 - b1, y, c) if (zh, x) == (1, 3) else None


def swap_b2(zh, x, b4, b2, b1, y, c):
    return (zh, x, b4, 1 - b2, b1, y, c)


def swap_b1(zh, x, b4, b2, b1, y, c):
    return (zh, x, b4, b2, 1 - b1, y, c)


def swap_even(zh, x, b4, b2, b1, y, c):
    return (zh, x, b4, b2, b1, y ^ 1, c)


def swap_odd(zh, x, b4, b2, b1, y, c):
    return (zh, x, b4, b2, b1, y ^ 3, c)


def swap_far(zh, x, b4, b2, b1, y, c):
    return (zh, x, b4, b2, b1, y ^ 2, c)


def swap_core(zh, x, b4, b2, b1, y, c):
    return (zh, x, b4, b2, b1, y, 1 - c)


def up_from(section):
    def route(zh, x, b4, b2, b1, y, c):
        if x != section % 4 or (x == 3 and zh == 1):
            return None
        if x == 3:
            return (1, 0, 1 - b4, 1 - b2, 1 - b1, y, c)
        return (zh, x + 1, b4, b2, b1, y, c)

    return route


def down_from(section):
    def route(zh, x, b4, b2, b1, y, c):
        if x != section % 4 or (x == 0 and zh == 0):
            return None
        if x == 0:
            return (0, 3, 1 - b4, 1 - b2, 1 - b1, y, c)
        return (zh, x - 1, b4, b2, b1, y, c)

    return route


def merged(own, other, bit):
    first = bit == 0
    return jnp.concatenate([jnp.where(first, own, other), jnp.where(first, other, own)], axis=0)


def merged_outer(own, other):
    y = lax.axis_index("y")
    outer = (y == 0) | (y == 3)
    rows = own.shape[0] // 2
    own_a, own_b, oth_a, oth_b = own[:rows], own[rows:], other[:rows], other[rows:]
    return jnp.concatenate(
        [
            jnp.where(outer, own_a, oth_a),
            jnp.where(outer, oth_a, own_a),
            jnp.where(outer, oth_b, own_b),
            jnp.where(outer, own_b, oth_b),
        ],
        axis=0,
    )


def gathered(block, even_first, beside=None):
    results = ()
    block = merged(block, routed(block, swap_b4), lax.axis_index("b4"))
    block = merged(block, routed(block, swap_b2), lax.axis_index("b2"))
    block = merged(block, routed(block, swap_b1), lax.axis_index("b1"))
    y = lax.axis_index("y")
    if even_first:
        if beside is not None:
            block, results = beside(block)
        block = merged(block, routed(block, swap_even), y % 2)
        block, *results = lax.optimization_barrier((block, *results))
        block = merged(block, routed(block, swap_odd), y // 2)
    else:
        block = merged(block, routed(block, swap_odd), y // 2)
        block = merged_outer(block, routed(block, swap_even))
    return merged(block, routed(block, swap_core), lax.axis_index("c")), *results


def row_mean(values):
    return jnp.mean(values, axis=-1, keepdims=True)


def columns(chunk):
    return pl.ds(pl.multiple_of(chunk * CHUNK, CHUNK), CHUNK)


def opening_kernel(inputs, probe, order, lhs, preact_t):
    position = lax.broadcasted_iota(jnp.int32, (FEATURES, FEATURES), 1)
    natural = lax.broadcasted_iota(jnp.int32, (FEATURES, FEATURES), 0)
    core, y = position // 256, (position // 64) % 4
    b1, b2, b4, row = (position // 32) % 2, (position // 16) % 2, (position // 8) % 2, position % 8
    at = (b4 * 4 + b2 * 2 + b1) * 64 + y * 16 + core * 8 + row
    order[...] = jnp.where(natural == at, 1.0, 0.0).astype(jnp.bfloat16)
    inflow = inputs[...].astype(jnp.float32)
    centred = inflow - row_mean(inflow)
    normed = (centred * lax.rsqrt(row_mean(centred * centred) + EPSILON)).astype(jnp.bfloat16)
    lhs[...] = jnp.dot(normed, order[...], preferred_element_type=jnp.float32).astype(jnp.bfloat16)

    def step(chunk, carry):
        preact_t[:, columns(chunk)] = jnp.dot(normed, probe[:, columns(chunk)], preferred_element_type=jnp.float32)
        return carry

    lax.fori_loop(0, CHUNKS, step, 0)


def opening_call(inputs, probe):
    rows = inputs.shape[0]
    return pl.pallas_call(
        opening_kernel,
        out_shape=[
            jax.ShapeDtypeStruct((FEATURES, FEATURES), jnp.bfloat16),
            jax.ShapeDtypeStruct((rows, FEATURES), jnp.bfloat16),
            jax.ShapeDtypeStruct((rows, HIDDEN), jnp.float32),
        ],
        in_specs=[WHOLE] * 2,
        out_specs=[WHOLE] * 3,
        compiler_params=PARAMS,
        name="opening",
    )(inputs, probe)


def gelu_slopes(preact, preact_t, slope_out, chunk):
    normal_cdf = 0.5 * (1.0 + lax.erf(preact * SQRT_HALF))
    density = INV_ROOT_TWO_PI * jnp.exp(-0.5 * preact * preact)
    slope = normal_cdf + preact * density
    slope_out[0, :, columns(chunk)] = slope
    slope_out[1, :, columns(chunk)] = density * (2.0 - preact * preact) * preact_t
    return jnp.concatenate([preact * normal_cdf, slope * preact_t], axis=0).astype(jnp.bfloat16)


def first_kernel(micro, section, inputs, opening_lhs, opening_t, w_in, w_out, pair_out, slope_out, acc):
    rows = slice(micro * ROWS, (micro + 1) * ROWS)

    @pl.when(section[0] == 0)
    def _():
        acc[:ROWS] = inputs[rows].astype(jnp.float32)
        acc[ROWS:] = jnp.zeros((ROWS, FEATURES), jnp.float32)

        def step(chunk, carry):
            preact = jnp.dot(opening_lhs[rows], w_in[:, columns(chunk)], preferred_element_type=jnp.float32)
            hidden = gelu_slopes(preact, opening_t[rows, columns(chunk)], slope_out, chunk)
            acc[...] += jnp.dot(hidden, w_out[columns(chunk), :], preferred_element_type=jnp.float32)
            return carry

        lax.fori_loop(0, CHUNKS, step, 0, unroll=UNROLL)
        pair_out[0] = acc[:ROWS].astype(jnp.bfloat16)
        pair_out[1] = acc[ROWS:].astype(jnp.bfloat16)


def forward_kernel(tick, *refs):
    last = tick == LAYERS - 1
    section, pair, w_in, probe, w_out, order = refs[:6]
    refs = refs[6:]
    if last:
        goal, refs = refs[0], refs[1:]
    pair_out, norm, stat, slope_out, natural, lhs, acc = refs

    @pl.when(section[0] == tick)
    def _():
        inflow = pair[0].astype(jnp.float32)
        inflow_t = pair[1].astype(jnp.float32)
        centred = inflow - row_mean(inflow)
        rscale = lax.rsqrt(row_mean(centred * centred) + EPSILON)
        normed = centred * rscale
        tangent_dot = row_mean(normed * inflow_t)
        normed_t = rscale * (inflow_t - row_mean(inflow_t) - normed * tangent_dot)
        norm[0] = normed
        norm[1] = normed_t
        stat[0] = jnp.broadcast_to(rscale, (ROWS, 128))
        stat[1] = jnp.broadcast_to(tangent_dot, (ROWS, 128))
        acc[:ROWS] = inflow
        acc[ROWS:] = inflow_t
        natural[:ROWS] = normed.astype(jnp.bfloat16)
        natural[ROWS:] = normed_t.astype(jnp.bfloat16)
        lhs[...] = jnp.dot(natural[...], order[...], preferred_element_type=jnp.float32).astype(jnp.bfloat16)

        def step(chunk, carry):
            both = jnp.dot(lhs[...], w_in[:, columns(chunk)], preferred_element_type=jnp.float32)
            preact_t = both[ROWS:] + jnp.dot(
                natural[:ROWS], probe[:, columns(chunk)], preferred_element_type=jnp.float32
            )
            hidden = gelu_slopes(both[:ROWS], preact_t, slope_out, chunk)
            acc[...] += jnp.dot(hidden, w_out[columns(chunk), :], preferred_element_type=jnp.float32)
            return carry

        lax.fori_loop(0, CHUNKS, step, 0, unroll=UNROLL)
        if last:
            pair_out[0] = ((acc[:ROWS] - goal[...].astype(jnp.float32)) / TOKENS).astype(jnp.bfloat16)
            pair_out[1] = (acc[ROWS:] / TOKENS).astype(jnp.bfloat16)
        else:
            pair_out[0] = acc[:ROWS].astype(jnp.bfloat16)
            pair_out[1] = acc[ROWS:].astype(jnp.bfloat16)


NORM = jax.ShapeDtypeStruct((2, ROWS, FEATURES), jnp.float32)
STAT = jax.ShapeDtypeStruct((2, ROWS, 128), jnp.float32)
SLOPE = jax.ShapeDtypeStruct((2, ROWS, HIDDEN), jnp.float32)
PAIR = jax.ShapeDtypeStruct((2, ROWS, FEATURES), jnp.bfloat16)
GRADS = jax.ShapeDtypeStruct((2 * ROWS, HIDDEN), jnp.bfloat16)
PARAMS = pltpu.CompilerParams(vmem_limit_bytes=VMEM_BYTES)


def first_call(micro, section, inputs, opening_lhs, opening_t, w_in, w_out):
    return pl.pallas_call(
        functools.partial(first_kernel, micro),
        out_shape=[PAIR, SLOPE],
        in_specs=[SMEM] + [WHOLE] * 5,
        out_specs=[WHOLE] * 2,
        scratch_shapes=[pltpu.VMEM((2 * ROWS, FEATURES), jnp.float32)],
        compiler_params=PARAMS,
        name="layer_up_0",
    )(section, inputs, opening_lhs, opening_t, w_in, w_out)


def forward_call(tick, section, pair, w_in, probe, w_out, order, goal):
    operands = [section, pair, w_in, probe, w_out, order] + ([goal] if tick == LAYERS - 1 else [])
    return pl.pallas_call(
        functools.partial(forward_kernel, tick),
        out_shape=[PAIR, NORM, STAT, SLOPE],
        in_specs=[SMEM] + [WHOLE] * (len(operands) - 1),
        out_specs=[WHOLE] * 4,
        scratch_shapes=[
            pltpu.VMEM((2 * ROWS, FEATURES), jnp.bfloat16),
            pltpu.VMEM((2 * ROWS, FEATURES), jnp.bfloat16),
            pltpu.VMEM((2 * ROWS, FEATURES), jnp.float32),
        ],
        compiler_params=PARAMS,
        name=f"layer_up_{tick}",
    )(*operands)


def turned_kernel(w_in, probe, w_out, order, token, w_in_t, probe_t, w_out_t):
    w_in_t[...] = lax.dot_general(
        w_in[...], order[...], (((0,), (1,)), ((), ())), preferred_element_type=jnp.float32
    ).astype(jnp.bfloat16)
    probe_t[...] = probe[...].T
    w_out_t[...] = w_out[...].T


def turned_call(w_in, probe, w_out, order, token):
    tall = jax.ShapeDtypeStruct((HIDDEN, FEATURES), jnp.bfloat16)
    wide = jax.ShapeDtypeStruct((FEATURES, HIDDEN), jnp.bfloat16)
    return pl.pallas_call(
        turned_kernel,
        out_shape=[tall, tall, wide],
        in_specs=[WHOLE] * 4 + [pl.BlockSpec(memory_space=pl.ANY)],
        out_specs=[WHOLE] * 3,
        compiler_params=PARAMS,
        name="turned_weights",
    )(w_in, probe, w_out, order, token)


def hidden_grads(pair, w_out_t, slope, chunk):
    both = jnp.dot(
        pair[...].reshape(2 * ROWS, FEATURES), w_out_t[:, columns(chunk)], preferred_element_type=jnp.float32
    )
    grad_hidden, grad_hidden_t = both[:ROWS], both[ROWS:]
    slope_chunk = slope[0, :, columns(chunk)]
    grad_pre = grad_hidden * slope_chunk
    grad_pre_t = grad_hidden_t * slope_chunk + grad_hidden * slope[1, :, columns(chunk)]
    return grad_pre.astype(jnp.bfloat16), grad_pre_t.astype(jnp.bfloat16)


def norm_apply(values, normed, rscale):
    return rscale * (values - row_mean(values) - normed * row_mean(normed * values))


def backward_kernel(tick, *refs):
    section, pair, w_in_t, probe_t, w_out_t, norm, stat, slope = refs[:8]
    pair_out, grads, acc, acc_t = refs[8:]

    @pl.when(section[0] == LAYERS - 1 - tick)
    def _():
        acc[...] = jnp.zeros_like(acc)
        acc_t[...] = jnp.zeros_like(acc_t)

        def step(chunk, carry):
            low_grad, low_grad_t = hidden_grads(pair, w_out_t, slope, chunk)
            both = jnp.concatenate([low_grad_t, low_grad], axis=0)
            grads[:, columns(chunk)] = both
            acc[...] += jnp.dot(both, w_in_t[columns(chunk), :], preferred_element_type=jnp.float32)
            acc_t[...] += jnp.dot(low_grad, probe_t[columns(chunk), :], preferred_element_type=jnp.float32)
            return carry

        lax.fori_loop(0, CHUNKS, step, 0, unroll=UNROLL)
        normed, normed_t = norm[0], norm[1]
        rscale, tangent_dot = stat[0][:, :1], stat[1][:, :1]
        grad_norm = acc[ROWS:]
        grad_norm_t = acc[:ROWS] + acc_t[...]
        through = norm_apply(grad_norm, normed, rscale)
        through_t = (
            norm_apply(grad_norm_t, normed, rscale)
            - rscale * tangent_dot * through
            - rscale * (normed_t * row_mean(normed * grad_norm) + normed * row_mean(normed_t * grad_norm))
        )
        pair_out[0] = (pair[0].astype(jnp.float32) + through).astype(jnp.bfloat16)
        pair_out[1] = (pair[1].astype(jnp.float32) + through_t).astype(jnp.bfloat16)


def backward_call(tick, section, pair, w_in_t, probe_t, w_out_t, kept):
    operands = [section, pair, w_in_t, probe_t, w_out_t, *kept]
    return pl.pallas_call(
        functools.partial(backward_kernel, tick),
        out_shape=[PAIR, GRADS],
        in_specs=[SMEM] + [WHOLE] * (len(operands) - 1),
        out_specs=[WHOLE] * 2,
        scratch_shapes=[
            pltpu.VMEM((2 * ROWS, FEATURES), jnp.float32),
            pltpu.VMEM((ROWS, FEATURES), jnp.float32),
        ],
        compiler_params=PARAMS,
        name=f"layer_down_{tick}",
    )(*operands)


def core_half(index):
    return pl.ds(pl.multiple_of(index * (FEATURES // 2), FEATURES // 2), FEATURES // 2)


def curvature_operands(micro, section, pair, w_out_t, slope, order, opening_lhs, norms, grads, lhs, rhs):
    @pl.when(section[0] == 0)
    def _():
        lhs[:ROWS] = opening_lhs[micro * ROWS : (micro + 1) * ROWS]
        lhs[ROWS:] = jnp.zeros((ROWS, FEATURES), jnp.bfloat16)

        def bottom(chunk, carry):
            low_grad, low_grad_t = hidden_grads(pair, w_out_t, slope, chunk)
            rhs[:, columns(chunk)] = jnp.concatenate([low_grad_t, low_grad], axis=0)
            return carry

        lax.fori_loop(0, CHUNKS, bottom, 0, unroll=UNROLL)

    for layer in range(1, LAYERS):

        @pl.when(section[0] == layer)
        def _():
            both = norms[layer - 1][...].reshape(2 * ROWS, FEATURES).astype(jnp.bfloat16)
            lhs[...] = jnp.dot(both, order[...], preferred_element_type=jnp.float32).astype(jnp.bfloat16)
            rhs[...] = grads[LAYERS - 1 - layer][...]


def half_product(lhs, rhs, half, now):
    return lax.dot_general(lhs[:, core_half(half)], rhs[:, now], CONTRACT_FIRST, preferred_element_type=jnp.float32)


def curvature_kernel(micro, earlier, final, *refs):
    section, core, pair, w_out_t, slope, order, opening_lhs = refs[:7]
    norms, refs = refs[7 : 6 + LAYERS], refs[6 + LAYERS :]
    grads, refs = refs[: LAYERS - 1], refs[LAYERS - 1 :]
    if earlier:
        away_in, refs = refs[0], refs[1:]
        stay_in, refs = refs[0], refs[1:]
    if final:
        away, lhs, rhs = refs
    else:
        away, stay, lhs, rhs = refs
    curvature_operands(micro, section, pair, w_out_t, slope, order, opening_lhs, norms, grads, lhs, rhs)

    def step(chunk, carry):
        now = columns(chunk)
        leaving = half_product(lhs, rhs, 1 - core[0], now)
        if earlier:
            leaving = leaving + away_in[:, now]
        away[:, now] = leaving.astype(away.dtype)
        if not final:
            staying = half_product(lhs, rhs, core[0], now)
            if earlier:
                staying = staying + stay_in[:, now]
            stay[:, now] = staying
        return carry

    lax.fori_loop(0, CHUNKS, step, 0, unroll=UNROLL)


def rest_kernel(core, lhs, rhs, stay_in, stay):
    def step(chunk, carry):
        now = columns(chunk)
        stay[:, now] = stay_in[:, now] + half_product(lhs, rhs, core[0], now)
        return carry

    lax.fori_loop(0, CHUNKS, step, 0, unroll=UNROLL)


def curvature_call(micro, section, core, pair, w_out_t, slope, order, opening_lhs, norms, grads, sums, final):
    half = (FEATURES // 2, HIDDEN)
    operands = [section, core, pair, w_out_t, slope, order, opening_lhs, *norms, *grads, *sums]
    lhs = jax.ShapeDtypeStruct((2 * ROWS, FEATURES), jnp.bfloat16)
    rhs = jax.ShapeDtypeStruct((2 * ROWS, HIDDEN), jnp.bfloat16)
    away = jax.ShapeDtypeStruct(half, jnp.bfloat16 if final else jnp.float32)
    stay = jax.ShapeDtypeStruct(half, jnp.float32)
    return pl.pallas_call(
        functools.partial(curvature_kernel, micro, bool(sums), final),
        out_shape=[away, lhs, rhs] if final else [away, stay],
        in_specs=[SMEM, SMEM] + [WHOLE] * (len(operands) - 2),
        out_specs=[WHOLE] * (3 if final else 2),
        scratch_shapes=[] if final else [pltpu.VMEM(each.shape, each.dtype) for each in (lhs, rhs)],
        compiler_params=PARAMS,
        name="curvature_away" if final else "curvature_part",
    )(*operands)


def rest_call(core, lhs, rhs, stay_in):
    return pl.pallas_call(
        rest_kernel,
        out_shape=jax.ShapeDtypeStruct(stay_in.shape, jnp.float32),
        in_specs=[SMEM] + [WHOLE] * 3,
        out_specs=WHOLE,
        compiler_params=PARAMS,
        name="curvature_rest",
    )(core, lhs, rhs, stay_in)


def shards(inputs, targets, w_in, w_out, probes):
    section = jnp.reshape(lax.axis_index(SECTION), (1,)).astype(jnp.int32)
    core = jnp.reshape(lax.axis_index("c"), (1,)).astype(jnp.int32)
    probe = probes[0]

    def opening(block):
        block, inputs_now = lax.optimization_barrier((block, inputs))
        return block, opening_call(inputs_now, probe)

    full_in, order, opening_lhs, opening_t = gathered(w_in[0], True, opening)
    (full_out,) = gathered(w_out[0], False)
    full_out = (
        full_out.reshape(2, 4, 2, 2, 2, 32, FEATURES).transpose(4, 3, 2, 1, 0, 5, 6).reshape(HIDDEN, FEATURES)
    )
    goal = routed(targets, goal_route)
    pairs, slopes, kept, grads = [None] * MICRO, [], [], []
    for micro in range(MICRO):
        kept.append([])
        grads.append([])
    for tick in range(LAYERS):
        for micro in range(MICRO):
            if tick == 0:
                pairs[micro], slope = first_call(micro, section, inputs, opening_lhs, opening_t, full_in, full_out)
                slopes.append(slope)
            else:
                goal_now = goal[micro * ROWS : (micro + 1) * ROWS]
                pairs[micro], *stores = forward_call(
                    tick, section, pairs[micro], full_in, probe, full_out, order, goal_now
                )
                kept[micro].append(stores)
            if tick < LAYERS - 1:
                pairs[micro] = routed(pairs[micro], up_from(tick))
        if tick == TURN_TICK:
            turned = turned_call(full_in, probe, full_out, order, kept[-1][-1][0])
    for tick in range(LAYERS - 1):
        for micro in range(MICRO):
            pairs[micro], low_grads = backward_call(
                tick, section, pairs[micro], *turned, kept[micro][LAYERS - 2 - tick]
            )
            grads[micro].append(low_grads)
            pairs[micro] = routed(pairs[micro], down_from(LAYERS - 1 - tick))
    sums = ()
    for micro in range(MICRO):
        sums_in = sums
        sums = curvature_call(
            micro,
            section,
            core,
            pairs[micro],
            turned[2],
            slopes[micro],
            order,
            opening_lhs,
            [stores[0] for stores in kept[micro]],
            grads[micro],
            sums_in,
            micro == MICRO - 1,
        )
    away, lhs, rhs = sums
    other = routed(away, swap_core)
    stay = rest_call(core, lhs, rhs, sums_in[1])
    summed = (stay + other.astype(jnp.float32)).astype(jnp.bfloat16).reshape(4, 64, HIDDEN)
    y = lax.axis_index("y")

    def piece(owner):
        return lax.dynamic_index_in_dim(summed, owner, 0, keepdims=False)

    arrived = [
        routed(piece(y ^ 1), swap_even),
        routed(piece(y ^ 3), swap_odd),
        routed(piece(y ^ 2), swap_far),
    ]
    summed = sum([each.astype(jnp.float32) for each in arrived], piece(y).astype(jnp.float32)).astype(jnp.bfloat16)
    summed = lax.all_to_all(summed.reshape(8, 8, HIDDEN), ("b1", "b2", "b4"), 0, 0, tiled=True)
    summed = jnp.sum(summed.astype(jnp.float32), axis=0)
    probe_own = lax.dynamic_slice_in_dim(probe, lax.axis_index(DP) * 8, 8, 0)
    return (probe_own.astype(jnp.float32) * summed)[None]


def solution(mesh):
    fine = Mesh(mesh.devices.reshape(SIZES), NAMES)
    return jax.shard_map(
        shards,
        mesh=fine,
        in_specs=(
            P(DP, None),
            P(DP, None),
            P(SECTION, DP, None),
            P(SECTION, DP, None),
            P(SECTION, None, None),
        ),
        out_specs=P(SECTION, DP, None),
        check_vma=False,
    )
```

```python
import functools
import itertools

import jax
import jax.numpy as jnp
from jax import lax
from jax.experimental import pallas as pl
from jax.experimental.pallas import tpu as pltpu
from jax.sharding import Mesh, PartitionSpec as P

EPSILON = 1e-05
SQRT_HALF = 0.7071067811865476
INV_ROOT_TWO_PI = 0.3989422804014327
CONTRACT_FIRST = (((0,), (0,)), ((), ()))

NAMES = ("zh", "x", "b4", "b2", "b1", "y", "c")
SIZES = (2, 4, 2, 2, 2, 4, 2)
SECTION = ("zh", "x")
DP = ("b4", "b2", "b1", "y", "c")
LAYERS = 8
FEATURES = 512
HIDDEN = 2048
MICRO = 2
ROWS = 128 // MICRO
UNROLL = 1
TURN_TICK = 3
TOKENS = 8192
CHUNK = 1024
CHUNKS = HIDDEN // CHUNK
VMEM_BYTES = 4 * 1024 * 1024
WHOLE = pl.BlockSpec(memory_space=pltpu.VMEM)
SMEM = pl.BlockSpec(memory_space=pltpu.SMEM)


def flat(place):
    index = 0
    for size, at in zip(SIZES, place):
        index = index * size + at
    return index


def routed(value, route):
    pairs = []
    for place in itertools.product(*(range(size) for size in SIZES)):
        there = route(*place)
        if there is not None:
            pairs.append((flat(place), flat(there)))
    return lax.ppermute(value, NAMES, pairs)


def swap_b4(zh, x, b4, b2, b1, y, c):
    return (zh, x, 1 - b4, b2, b1, y, c)


def goal_route(zh, x, b4, b2, b1, y, c):
    return (zh, x, 1 - b4, 1 - b2, 1 - b1, y, c) if (zh, x) == (1, 3) else None


def swap_b2(zh, x, b4, b2, b1, y, c):
    return (zh, x, b4, 1 - b2, b1, y, c)


def swap_b1(zh, x, b4, b2, b1, y, c):
    return (zh, x, b4, b2, 1 - b1, y, c)


def swap_even(zh, x, b4, b2, b1, y, c):
    return (zh, x, b4, b2, b1, y ^ 1, c)


def swap_odd(zh, x, b4, b2, b1, y, c):
    return (zh, x, b4, b2, b1, y ^ 3, c)


def swap_core(zh, x, b4, b2, b1, y, c):
    return (zh, x, b4, b2, b1, y, 1 - c)


def up_from(section):
    def route(zh, x, b4, b2, b1, y, c):
        if x != section % 4 or (x == 3 and zh == 1):
            return None
        if x == 3:
            return (1, 0, 1 - b4, 1 - b2, 1 - b1, y, c)
        return (zh, x + 1, b4, b2, b1, y, c)

    return route


def down_from(section):
    def route(zh, x, b4, b2, b1, y, c):
        if x != section % 4 or (x == 0 and zh == 0):
            return None
        if x == 0:
            return (0, 3, 1 - b4, 1 - b2, 1 - b1, y, c)
        return (zh, x - 1, b4, b2, b1, y, c)

    return route


def merged(own, other, bit):
    first = bit == 0
    return jnp.concatenate([jnp.where(first, own, other), jnp.where(first, other, own)], axis=0)


def merged_outer(own, other):
    y = lax.axis_index("y")
    outer = (y == 0) | (y == 3)
    rows = own.shape[0] // 2
    own_a, own_b, oth_a, oth_b = own[:rows], own[rows:], other[:rows], other[rows:]
    return jnp.concatenate(
        [
            jnp.where(outer, own_a, oth_a),
            jnp.where(outer, oth_a, own_a),
            jnp.where(outer, oth_b, own_b),
            jnp.where(outer, own_b, oth_b),
        ],
        axis=0,
    )


def gathered(block, even_first, beside=None):
    results = ()
    block = merged(block, routed(block, swap_b4), lax.axis_index("b4"))
    block = merged(block, routed(block, swap_b2), lax.axis_index("b2"))
    block = merged(block, routed(block, swap_b1), lax.axis_index("b1"))
    y = lax.axis_index("y")
    if even_first:
        if beside is not None:
            block, results = beside(block)
        block = merged(block, routed(block, swap_even), y % 2)
        block, *results = lax.optimization_barrier((block, *results))
        block = merged(block, routed(block, swap_odd), y // 2)
    else:
        block = merged(block, routed(block, swap_odd), y // 2)
        block = merged_outer(block, routed(block, swap_even))
    return block, routed(block, swap_core), *results


def row_mean(values):
    return jnp.mean(values, axis=-1, keepdims=True)


def columns(chunk):
    return pl.ds(pl.multiple_of(chunk * CHUNK, CHUNK), CHUNK)


def opening_kernel(this_core, inputs, probe, order, lhs, preact_t):
    position = lax.broadcasted_iota(jnp.int32, (FEATURES, FEATURES), 1)
    natural = lax.broadcasted_iota(jnp.int32, (FEATURES, FEATURES), 0)
    core, y = (position // 256) ^ this_core[0], (position // 64) % 4
    b1, b2, b4, row = (position // 32) % 2, (position // 16) % 2, (position // 8) % 2, position % 8
    at = (b4 * 4 + b2 * 2 + b1) * 64 + y * 16 + core * 8 + row
    order[...] = jnp.where(natural == at, 1.0, 0.0).astype(jnp.bfloat16)
    inflow = inputs[...].astype(jnp.float32)
    centred = inflow - row_mean(inflow)
    normed = (centred * lax.rsqrt(row_mean(centred * centred) + EPSILON)).astype(jnp.bfloat16)
    lhs[...] = jnp.dot(normed, order[...], preferred_element_type=jnp.float32).astype(jnp.bfloat16)

    def step(chunk, carry):
        preact_t[:, columns(chunk)] = jnp.dot(normed, probe[:, columns(chunk)], preferred_element_type=jnp.float32)
        return carry

    lax.fori_loop(0, CHUNKS, step, 0)


def opening_call(core, inputs, probe):
    rows = inputs.shape[0]
    return pl.pallas_call(
        opening_kernel,
        out_shape=[
            jax.ShapeDtypeStruct((FEATURES, FEATURES), jnp.bfloat16),
            jax.ShapeDtypeStruct((rows, FEATURES), jnp.bfloat16),
            jax.ShapeDtypeStruct((rows, HIDDEN), jnp.float32),
        ],
        in_specs=[SMEM] + [WHOLE] * 2,
        out_specs=[WHOLE] * 3,
        compiler_params=PARAMS,
        name="opening",
    )(core, inputs, probe)


def gelu_slopes(preact, preact_t, slope_out, chunk):
    normal_cdf = 0.5 * (1.0 + lax.erf(preact * SQRT_HALF))
    density = INV_ROOT_TWO_PI * jnp.exp(-0.5 * preact * preact)
    slope = normal_cdf + preact * density
    slope_out[0, :, columns(chunk)] = slope
    slope_out[1, :, columns(chunk)] = density * (2.0 - preact * preact) * preact_t
    return jnp.concatenate([preact * normal_cdf, slope * preact_t], axis=0).astype(jnp.bfloat16)


def halves_product(lhs, own_in, other_in, now):
    return jnp.dot(lhs[:, OWN_HALF], own_in[:, now], preferred_element_type=jnp.float32) + jnp.dot(
        lhs[:, OTHER_HALF], other_in[:, now], preferred_element_type=jnp.float32
    )


def first_kernel(micro, section, inputs, opening_lhs, opening_t, own_in, other_in, w_out, pair_out, slope_out, acc):
    rows = slice(micro * ROWS, (micro + 1) * ROWS)

    @pl.when(section[0] == 0)
    def _():
        acc[:ROWS] = inputs[rows].astype(jnp.float32)
        acc[ROWS:] = jnp.zeros((ROWS, FEATURES), jnp.float32)

        def step(chunk, carry):
            preact = halves_product(opening_lhs[rows], own_in, other_in, columns(chunk))
            hidden = gelu_slopes(preact, opening_t[rows, columns(chunk)], slope_out, chunk)
            acc[...] += jnp.dot(hidden, w_out[columns(chunk), :], preferred_element_type=jnp.float32)
            return carry

        lax.fori_loop(0, CHUNKS, step, 0, unroll=UNROLL)
        pair_out[0] = acc[:ROWS].astype(jnp.bfloat16)
        pair_out[1] = acc[ROWS:].astype(jnp.bfloat16)


def forward_kernel(tick, *refs):
    last = tick == LAYERS - 1
    section, pair, own_in, other_in, probe, w_out, order = refs[:7]
    refs = refs[7:]
    if last:
        goal, refs = refs[0], refs[1:]
    pair_out, norm, stat, slope_out, natural, lhs, acc = refs

    @pl.when(section[0] == tick)
    def _():
        inflow = pair[0].astype(jnp.float32)
        inflow_t = pair[1].astype(jnp.float32)
        centred = inflow - row_mean(inflow)
        rscale = lax.rsqrt(row_mean(centred * centred) + EPSILON)
        normed = centred * rscale
        tangent_dot = row_mean(normed * inflow_t)
        normed_t = rscale * (inflow_t - row_mean(inflow_t) - normed * tangent_dot)
        norm[0] = normed
        norm[1] = normed_t
        stat[0] = jnp.broadcast_to(rscale, (ROWS, 128))
        stat[1] = jnp.broadcast_to(tangent_dot, (ROWS, 128))
        acc[:ROWS] = inflow
        acc[ROWS:] = inflow_t
        natural[:ROWS] = normed.astype(jnp.bfloat16)
        natural[ROWS:] = normed_t.astype(jnp.bfloat16)
        lhs[...] = jnp.dot(natural[...], order[...], preferred_element_type=jnp.float32).astype(jnp.bfloat16)

        def step(chunk, carry):
            both = halves_product(lhs[...], own_in, other_in, columns(chunk))
            preact_t = both[ROWS:] + jnp.dot(
                natural[:ROWS], probe[:, columns(chunk)], preferred_element_type=jnp.float32
            )
            hidden = gelu_slopes(both[:ROWS], preact_t, slope_out, chunk)
            acc[...] += jnp.dot(hidden, w_out[columns(chunk), :], preferred_element_type=jnp.float32)
            return carry

        lax.fori_loop(0, CHUNKS, step, 0, unroll=UNROLL)
        if last:
            pair_out[0] = ((acc[:ROWS] - goal[...].astype(jnp.float32)) / TOKENS).astype(jnp.bfloat16)
            pair_out[1] = (acc[ROWS:] / TOKENS).astype(jnp.bfloat16)
        else:
            pair_out[0] = acc[:ROWS].astype(jnp.bfloat16)
            pair_out[1] = acc[ROWS:].astype(jnp.bfloat16)


NORM = jax.ShapeDtypeStruct((2, ROWS, FEATURES), jnp.float32)
STAT = jax.ShapeDtypeStruct((2, ROWS, 128), jnp.float32)
SLOPE = jax.ShapeDtypeStruct((2, ROWS, HIDDEN), jnp.float32)
PAIR = jax.ShapeDtypeStruct((2, ROWS, FEATURES), jnp.bfloat16)
GRADS = jax.ShapeDtypeStruct((2 * ROWS, HIDDEN), jnp.bfloat16)
PARAMS = pltpu.CompilerParams(vmem_limit_bytes=VMEM_BYTES)


def first_call(micro, section, inputs, opening_lhs, opening_t, own_in, other_in, w_out):
    return pl.pallas_call(
        functools.partial(first_kernel, micro),
        out_shape=[PAIR, SLOPE],
        in_specs=[SMEM] + [WHOLE] * 6,
        out_specs=[WHOLE] * 2,
        scratch_shapes=[pltpu.VMEM((2 * ROWS, FEATURES), jnp.float32)],
        compiler_params=PARAMS,
        name="layer_up_0",
    )(section, inputs, opening_lhs, opening_t, own_in, other_in, w_out)


def forward_call(tick, section, pair, own_in, other_in, probe, w_out, order, goal):
    operands = [section, pair, own_in, other_in, probe, w_out, order] + ([goal] if tick == LAYERS - 1 else [])
    return pl.pallas_call(
        functools.partial(forward_kernel, tick),
        out_shape=[PAIR, NORM, STAT, SLOPE],
        in_specs=[SMEM] + [WHOLE] * (len(operands) - 1),
        out_specs=[WHOLE] * 4,
        scratch_shapes=[
            pltpu.VMEM((2 * ROWS, FEATURES), jnp.bfloat16),
            pltpu.VMEM((2 * ROWS, FEATURES), jnp.bfloat16),
            pltpu.VMEM((2 * ROWS, FEATURES), jnp.float32),
        ],
        compiler_params=PARAMS,
        name=f"layer_up_{tick}",
    )(*operands)


def turned_kernel(own_in, other_in, probe, w_out, order, token, w_in_t, probe_t, w_out_t):
    by_place = (((0,), (1,)), ((), ()))

    def step(index, carry):
        now = pl.ds(pl.multiple_of(index * FEATURES, FEATURES), FEATURES)
        own = lax.dot_general(own_in[:, now], order[:, OWN_HALF], by_place, preferred_element_type=jnp.float32)
        other = lax.dot_general(other_in[:, now], order[:, OTHER_HALF], by_place, preferred_element_type=jnp.float32)
        w_in_t[now, :] = (own + other).astype(jnp.bfloat16)
        probe_t[now, :] = probe[:, now].T
        w_out_t[:, now] = w_out[now, :].T
        return carry

    lax.fori_loop(0, HIDDEN // FEATURES, step, 0)


def turned_call(own_in, other_in, probe, w_out, order, token):
    tall = jax.ShapeDtypeStruct((HIDDEN, FEATURES), jnp.bfloat16)
    wide = jax.ShapeDtypeStruct((FEATURES, HIDDEN), jnp.bfloat16)
    return pl.pallas_call(
        turned_kernel,
        out_shape=[tall, tall, wide],
        in_specs=[WHOLE] * 5 + [pl.BlockSpec(memory_space=pl.ANY)],
        out_specs=[WHOLE] * 3,
        compiler_params=PARAMS,
        name="turned_weights",
    )(own_in, other_in, probe, w_out, order, token)


def hidden_grads(pair, w_out_t, slope, chunk):
    both = jnp.dot(
        pair[...].reshape(2 * ROWS, FEATURES), w_out_t[:, columns(chunk)], preferred_element_type=jnp.float32
    )
    grad_hidden, grad_hidden_t = both[:ROWS], both[ROWS:]
    slope_chunk = slope[0, :, columns(chunk)]
    grad_pre = grad_hidden * slope_chunk
    grad_pre_t = grad_hidden_t * slope_chunk + grad_hidden * slope[1, :, columns(chunk)]
    return grad_pre.astype(jnp.bfloat16), grad_pre_t.astype(jnp.bfloat16)


def norm_apply(values, normed, rscale):
    return rscale * (values - row_mean(values) - normed * row_mean(normed * values))


def backward_kernel(tick, *refs):
    section, pair, w_in_t, probe_t, w_out_t, norm, stat, slope = refs[:8]
    pair_out, grads, acc, acc_t = refs[8:]

    @pl.when(section[0] == LAYERS - 1 - tick)
    def _():
        acc[...] = jnp.zeros_like(acc)
        acc_t[...] = jnp.zeros_like(acc_t)

        def step(chunk, carry):
            low_grad, low_grad_t = hidden_grads(pair, w_out_t, slope, chunk)
            both = jnp.concatenate([low_grad_t, low_grad], axis=0)
            grads[:, columns(chunk)] = both
            acc[...] += jnp.dot(both, w_in_t[columns(chunk), :], preferred_element_type=jnp.float32)
            acc_t[...] += jnp.dot(low_grad, probe_t[columns(chunk), :], preferred_element_type=jnp.float32)
            return carry

        lax.fori_loop(0, CHUNKS, step, 0, unroll=UNROLL)
        normed, normed_t = norm[0], norm[1]
        rscale, tangent_dot = stat[0][:, :1], stat[1][:, :1]
        grad_norm = acc[ROWS:]
        grad_norm_t = acc[:ROWS] + acc_t[...]
        through = norm_apply(grad_norm, normed, rscale)
        through_t = (
            norm_apply(grad_norm_t, normed, rscale)
            - rscale * tangent_dot * through
            - rscale * (normed_t * row_mean(normed * grad_norm) + normed * row_mean(normed_t * grad_norm))
        )
        pair_out[0] = (pair[0].astype(jnp.float32) + through).astype(jnp.bfloat16)
        pair_out[1] = (pair[1].astype(jnp.float32) + through_t).astype(jnp.bfloat16)


def backward_call(tick, section, pair, w_in_t, probe_t, w_out_t, kept):
    operands = [section, pair, w_in_t, probe_t, w_out_t, *kept]
    return pl.pallas_call(
        functools.partial(backward_kernel, tick),
        out_shape=[PAIR, GRADS],
        in_specs=[SMEM] + [WHOLE] * (len(operands) - 1),
        out_specs=[WHOLE] * 2,
        scratch_shapes=[
            pltpu.VMEM((2 * ROWS, FEATURES), jnp.float32),
            pltpu.VMEM((ROWS, FEATURES), jnp.float32),
        ],
        compiler_params=PARAMS,
        name=f"layer_down_{tick}",
    )(*operands)


OWN_HALF = slice(0, FEATURES // 2)
OTHER_HALF = slice(FEATURES // 2, FEATURES)


def curvature_operands(micro, section, pair, w_out_t, slope, order, opening_lhs, norms, grads, lhs, rhs):
    @pl.when(section[0] == 0)
    def _():
        lhs[:ROWS] = opening_lhs[micro * ROWS : (micro + 1) * ROWS]
        lhs[ROWS:] = jnp.zeros((ROWS, FEATURES), jnp.bfloat16)

        def bottom(chunk, carry):
            low_grad, low_grad_t = hidden_grads(pair, w_out_t, slope, chunk)
            rhs[:, columns(chunk)] = jnp.concatenate([low_grad_t, low_grad], axis=0)
            return carry

        lax.fori_loop(0, CHUNKS, bottom, 0, unroll=UNROLL)

    for layer in range(1, LAYERS):

        @pl.when(section[0] == layer)
        def _():
            both = norms[layer - 1][...].reshape(2 * ROWS, FEATURES).astype(jnp.bfloat16)
            lhs[...] = jnp.dot(both, order[...], preferred_element_type=jnp.float32).astype(jnp.bfloat16)
            rhs[...] = grads[LAYERS - 1 - layer][...]


def curvature_kernel(micro, final, *refs):
    section, pair, w_out_t, slope, order, opening_lhs = refs[:6]
    norms, refs = refs[6 : 5 + LAYERS], refs[5 + LAYERS :]
    grads, refs = refs[: LAYERS - 1], refs[LAYERS - 1 :]
    if final:
        away_in, stay_in, refs = refs[0], refs[1], refs[2:]
    away, stay, lhs, rhs = refs
    curvature_operands(micro, section, pair, w_out_t, slope, order, opening_lhs, norms, grads, lhs, rhs)

    def step(chunk, carry):
        now = columns(chunk)

        def product(half):
            return lax.dot_general(lhs[:, half], rhs[:, now], CONTRACT_FIRST, preferred_element_type=jnp.float32)

        if final:
            away[:, now] = (away_in[:, now] + product(OTHER_HALF)).astype(jnp.bfloat16)
            stay[:, now] = stay_in[:, now] + product(OWN_HALF)
        else:
            away[:, now] = product(OTHER_HALF)
            stay[:, now] = product(OWN_HALF)
        return carry

    lax.fori_loop(0, CHUNKS, step, 0, unroll=UNROLL)


def curvature_call(micro, section, pair, w_out_t, slope, order, opening_lhs, norms, grads, sums):
    half = (FEATURES // 2, HIDDEN)
    final = bool(sums)
    operands = [section, pair, w_out_t, slope, order, opening_lhs, *norms, *grads, *sums]
    return pl.pallas_call(
        functools.partial(curvature_kernel, micro, final),
        out_shape=[
            jax.ShapeDtypeStruct(half, jnp.bfloat16 if final else jnp.float32),
            jax.ShapeDtypeStruct(half, jnp.float32),
        ],
        in_specs=[SMEM] + [WHOLE] * (len(operands) - 1),
        out_specs=[WHOLE] * 2,
        scratch_shapes=[
            pltpu.VMEM((2 * ROWS, FEATURES), jnp.bfloat16),
            pltpu.VMEM((2 * ROWS, HIDDEN), jnp.bfloat16),
        ],
        compiler_params=PARAMS,
        name="curvature_last" if final else "curvature_first",
    )(*operands)


def shards(inputs, targets, w_in, w_out, probes):
    section = jnp.reshape(lax.axis_index(SECTION), (1,)).astype(jnp.int32)
    core = jnp.reshape(lax.axis_index("c"), (1,)).astype(jnp.int32)
    probe = probes[0]

    def opening(block):
        block, inputs_now = lax.optimization_barrier((block, inputs))
        return block, opening_call(core, inputs_now, probe)

    own_in, other_in, order, opening_lhs, opening_t = gathered(w_in[0], True, opening)
    full_out = merged(*gathered(w_out[0], False), lax.axis_index("c"))
    full_out = (
        full_out.reshape(2, 4, 2, 2, 2, 32, FEATURES).transpose(4, 3, 2, 1, 0, 5, 6).reshape(HIDDEN, FEATURES)
    )
    goal = routed(targets, goal_route)
    pairs, slopes, kept, grads = [None] * MICRO, [], [], []
    for micro in range(MICRO):
        kept.append([])
        grads.append([])
    for tick in range(LAYERS):
        for micro in range(MICRO):
            if tick == 0:
                pairs[micro], slope = first_call(
                    micro, section, inputs, opening_lhs, opening_t, own_in, other_in, full_out
                )
                slopes.append(slope)
            else:
                goal_now = goal[micro * ROWS : (micro + 1) * ROWS]
                pairs[micro], *stores = forward_call(
                    tick, section, pairs[micro], own_in, other_in, probe, full_out, order, goal_now
                )
                kept[micro].append(stores)
            if tick < LAYERS - 1:
                pairs[micro] = routed(pairs[micro], up_from(tick))
        if tick == TURN_TICK:
            turned = turned_call(own_in, other_in, probe, full_out, order, kept[-1][-1][0])
    for tick in range(LAYERS - 1):
        for micro in range(MICRO):
            pairs[micro], low_grads = backward_call(
                tick, section, pairs[micro], *turned, kept[micro][LAYERS - 2 - tick]
            )
            grads[micro].append(low_grads)
            pairs[micro] = routed(pairs[micro], down_from(LAYERS - 1 - tick))
    sums = ()
    for micro in range(MICRO):
        norms = [stores[0] for stores in kept[micro]]
        sums = curvature_call(
            micro, section, pairs[micro], turned[2], slopes[micro], order, opening_lhs, norms, grads[micro], sums
        )
    away, stay = sums
    other = routed(away, swap_core)
    summed = (stay + other.astype(jnp.float32)).astype(jnp.bfloat16)
    summed = lax.all_to_all(summed.reshape(4, 64, HIDDEN), "y", 0, 0, tiled=True)
    summed = jnp.sum(summed.astype(jnp.float32), axis=0).astype(jnp.bfloat16)
    summed = lax.all_to_all(summed.reshape(8, 8, HIDDEN), ("b1", "b2", "b4"), 0, 0, tiled=True)
    summed = jnp.sum(summed.astype(jnp.float32), axis=0)
    probe_own = lax.dynamic_slice_in_dim(probe, lax.axis_index(DP) * 8, 8, 0)
    return (probe_own.astype(jnp.float32) * summed)[None]


def solution(mesh):
    fine = Mesh(mesh.devices.reshape(SIZES), NAMES)
    return jax.shard_map(
        shards,
        mesh=fine,
        in_specs=(
            P(DP, None),
            P(DP, None),
            P(SECTION, DP, None),
            P(SECTION, DP, None),
            P(SECTION, None, None),
        ),
        out_specs=P(SECTION, DP, None),
        check_vma=False,
    )
```

```python
import functools
import itertools

import jax
import jax.numpy as jnp
from jax import lax
from jax.experimental import pallas as pl
from jax.experimental.pallas import tpu as pltpu
from jax.sharding import Mesh, PartitionSpec as P

EPSILON = 1e-05
SQRT_HALF = 0.7071067811865476
INV_ROOT_TWO_PI = 0.3989422804014327
CONTRACT_FIRST = (((0,), (0,)), ((), ()))

NAMES = ("zh", "x", "b4", "b2", "b1", "y", "c")
SIZES = (2, 4, 2, 2, 2, 4, 2)
SECTION = ("zh", "x")
DP = ("b4", "b2", "b1", "y", "c")
PLACES = 6
SECTION_AT = 5
LAYERS = 8
FEATURES = 512
HIDDEN = 2048
MICRO = 2
ROWS = 128 // MICRO
UNROLL = 1
TURN_TICK = 3
TOKENS = 8192
CHUNK = 1024
CHUNKS = HIDDEN // CHUNK
VMEM_BYTES = 4 * 1024 * 1024
WHOLE = pl.BlockSpec(memory_space=pltpu.VMEM)
SMEM = pl.BlockSpec(memory_space=pltpu.SMEM)


def flat(place):
    index = 0
    for size, at in zip(SIZES, place):
        index = index * size + at
    return index


def routed(value, route):
    pairs = []
    for place in itertools.product(*(range(size) for size in SIZES)):
        there = route(*place)
        if there is not None:
            pairs.append((flat(place), flat(there)))
    return lax.ppermute(value, NAMES, pairs)


def swap_b4(zh, x, b4, b2, b1, y, c):
    return (zh, x, 1 - b4, b2, b1, y, c)


def goal_route(zh, x, b4, b2, b1, y, c):
    return (zh, x, 1 - b4, 1 - b2, 1 - b1, y, c) if (zh, x) == (1, 3) else None


def swap_b2(zh, x, b4, b2, b1, y, c):
    return (zh, x, b4, 1 - b2, b1, y, c)


def swap_b1(zh, x, b4, b2, b1, y, c):
    return (zh, x, b4, b2, 1 - b1, y, c)


def swap_even(zh, x, b4, b2, b1, y, c):
    return (zh, x, b4, b2, b1, y ^ 1, c)


def swap_odd(zh, x, b4, b2, b1, y, c):
    return (zh, x, b4, b2, b1, y ^ 3, c)


def swap_core(zh, x, b4, b2, b1, y, c):
    return (zh, x, b4, b2, b1, y, 1 - c)


def up_from(section):
    def route(zh, x, b4, b2, b1, y, c):
        if x != section % 4 or (x == 3 and zh == 1):
            return None
        if x == 3:
            return (1, 0, 1 - b4, 1 - b2, 1 - b1, y, c)
        return (zh, x + 1, b4, b2, b1, y, c)

    return route


def down_from(section):
    def route(zh, x, b4, b2, b1, y, c):
        if x != section % 4 or (x == 0 and zh == 0):
            return None
        if x == 0:
            return (0, 3, 1 - b4, 1 - b2, 1 - b1, y, c)
        return (zh, x - 1, b4, b2, b1, y, c)

    return route


def doubled(block, route):
    return jnp.concatenate([block, routed(block, route)], axis=0)


def gathered(block, even_first):
    for route in (swap_b4, swap_b2, swap_b1) + ((swap_even, swap_odd) if even_first else (swap_odd, swap_even)):
        block = doubled(block, route)
    return block, routed(block, swap_core)


def natural_block(place, b4, b2, b1, y, c):
    z = (b4 ^ place[0]) * 4 + (b2 ^ place[1]) * 2 + (b1 ^ place[2])
    return z * 8 + (y ^ place[3]) * 2 + (c ^ place[4])


def settled_kernel(place_in, block_in, place, block):
    for index in range(PLACES):
        place[index] = place_in[index]
    block[...] = block_in[...]


def settled_call(place, block):
    return pl.pallas_call(
        settled_kernel,
        out_shape=[
            jax.ShapeDtypeStruct(place.shape, place.dtype),
            jax.ShapeDtypeStruct(block.shape, block.dtype),
        ],
        in_specs=[SMEM, WHOLE],
        out_specs=[SMEM, WHOLE],
        compiler_params=PARAMS,
        name="settled",
    )(place, block)


def placed_kernel(place, own_out, other_out, full_out):
    rows = HIDDEN // 64
    for core, half in enumerate((own_out, other_out)):
        for index in range(32):
            odd, even = index // 8 % 2, index // 16
            there = natural_block(place, index % 2, index // 2 % 2, index // 4 % 2, even ^ (odd * 3), core)
            full_out[pl.ds(pl.multiple_of(there * rows, rows), rows), :] = half[index * rows : (index + 1) * rows, :]


def placed_call(place, own_out, other_out):
    return pl.pallas_call(
        placed_kernel,
        out_shape=jax.ShapeDtypeStruct((HIDDEN, FEATURES), jnp.bfloat16),
        in_specs=[SMEM] + [WHOLE] * 2,
        out_specs=WHOLE,
        compiler_params=PARAMS,
        name="placed_w_out",
    )(place, own_out, other_out)


def row_mean(values):
    return jnp.mean(values, axis=-1, keepdims=True)


def columns(chunk):
    return pl.ds(pl.multiple_of(chunk * CHUNK, CHUNK), CHUNK)


def one_hot(natural_row):
    natural = lax.broadcasted_iota(jnp.int32, (FEATURES, FEATURES), 0)
    return jnp.where(natural == natural_row, 1.0, 0.0).astype(jnp.bfloat16)


def opening_kernel(place, inputs, probe, order, curvature_order, normed_out, preact_t):
    at = lax.broadcasted_iota(jnp.int32, (FEATURES, FEATURES), 1)
    row, b4, b2, b1 = at % 8, (at // 8) % 2, (at // 16) % 2, (at // 32) % 2
    even, odd, core = (at // 64) % 2, (at // 128) % 2, at // 256
    order[...] = one_hot(natural_block(place, b4, b2, b1, even ^ (odd * 3), core) * 8 + row)
    block = (b4 * 4 + b2 * 2 + b1) * 8 + ((at // 64) % 4) * 2 + (core ^ place[4])
    curvature_order[...] = one_hot(block * 8 + row)
    inflow = inputs[...].astype(jnp.float32)
    centred = inflow - row_mean(inflow)
    normed = (centred * lax.rsqrt(row_mean(centred * centred) + EPSILON)).astype(jnp.bfloat16)
    normed_out[...] = normed

    def step(chunk, carry):
        preact_t[:, columns(chunk)] = jnp.dot(normed, probe[:, columns(chunk)], preferred_element_type=jnp.float32)
        return carry

    lax.fori_loop(0, CHUNKS, step, 0)


def opening_call(place, inputs, probe):
    rows = inputs.shape[0]
    order = jax.ShapeDtypeStruct((FEATURES, FEATURES), jnp.bfloat16)
    return pl.pallas_call(
        opening_kernel,
        out_shape=[
            order,
            order,
            jax.ShapeDtypeStruct((rows, FEATURES), jnp.bfloat16),
            jax.ShapeDtypeStruct((rows, HIDDEN), jnp.float32),
        ],
        in_specs=[SMEM] + [WHOLE] * 2,
        out_specs=[WHOLE] * 4,
        compiler_params=PARAMS,
        name="opening",
    )(place, inputs, probe)


def gelu_slopes(preact, preact_t, slope_out, chunk):
    normal_cdf = 0.5 * (1.0 + lax.erf(preact * SQRT_HALF))
    density = INV_ROOT_TWO_PI * jnp.exp(-0.5 * preact * preact)
    slope = normal_cdf + preact * density
    slope_out[0, :, columns(chunk)] = slope
    slope_out[1, :, columns(chunk)] = density * (2.0 - preact * preact) * preact_t
    return jnp.concatenate([preact * normal_cdf, slope * preact_t], axis=0).astype(jnp.bfloat16)


def halves_product(lhs, own_in, other_in, now):
    return jnp.dot(lhs[:, OWN_HALF], own_in[:, now], preferred_element_type=jnp.float32) + jnp.dot(
        lhs[:, OTHER_HALF], other_in[:, now], preferred_element_type=jnp.float32
    )


def first_kernel(micro, place, inputs, opening_n, opening_t, order, own_in, other_in, w_out, pair_out, slope_out, lhs, acc):
    rows = slice(micro * ROWS, (micro + 1) * ROWS)

    @pl.when(place[SECTION_AT] == 0)
    def _():
        lhs[...] = jnp.dot(opening_n[rows], order[...], preferred_element_type=jnp.float32).astype(jnp.bfloat16)
        acc[:ROWS] = inputs[rows].astype(jnp.float32)
        acc[ROWS:] = jnp.zeros((ROWS, FEATURES), jnp.float32)

        def step(chunk, carry):
            preact = halves_product(lhs[...], own_in, other_in, columns(chunk))
            hidden = gelu_slopes(preact, opening_t[rows, columns(chunk)], slope_out, chunk)
            acc[...] += jnp.dot(hidden, w_out[columns(chunk), :], preferred_element_type=jnp.float32)
            return carry

        lax.fori_loop(0, CHUNKS, step, 0, unroll=UNROLL)
        pair_out[0] = acc[:ROWS].astype(jnp.bfloat16)
        pair_out[1] = acc[ROWS:].astype(jnp.bfloat16)


def forward_kernel(tick, *refs):
    last = tick == LAYERS - 1
    place, pair, own_in, other_in, probe, w_out, order = refs[:7]
    refs = refs[7:]
    if last:
        goal, refs = refs[0], refs[1:]
    pair_out, norm, stat, slope_out, natural, lhs, acc = refs

    @pl.when(place[SECTION_AT] == tick)
    def _():
        inflow = pair[0].astype(jnp.float32)
        inflow_t = pair[1].astype(jnp.float32)
        centred = inflow - row_mean(inflow)
        rscale = lax.rsqrt(row_mean(centred * centred) + EPSILON)
        normed = centred * rscale
        tangent_dot = row_mean(normed * inflow_t)
        normed_t = rscale * (inflow_t - row_mean(inflow_t) - normed * tangent_dot)
        norm[0] = normed
        norm[1] = normed_t
        stat[0] = jnp.broadcast_to(rscale, (ROWS, 128))
        stat[1] = jnp.broadcast_to(tangent_dot, (ROWS, 128))
        acc[:ROWS] = inflow
        acc[ROWS:] = inflow_t
        natural[:ROWS] = normed.astype(jnp.bfloat16)
        natural[ROWS:] = normed_t.astype(jnp.bfloat16)
        lhs[...] = jnp.dot(natural[...], order[...], preferred_element_type=jnp.float32).astype(jnp.bfloat16)

        def step(chunk, carry):
            both = halves_product(lhs[...], own_in, other_in, columns(chunk))
            preact_t = both[ROWS:] + jnp.dot(
                natural[:ROWS], probe[:, columns(chunk)], preferred_element_type=jnp.float32
            )
            hidden = gelu_slopes(both[:ROWS], preact_t, slope_out, chunk)
            acc[...] += jnp.dot(hidden, w_out[columns(chunk), :], preferred_element_type=jnp.float32)
            return carry

        lax.fori_loop(0, CHUNKS, step, 0, unroll=UNROLL)
        if last:
            pair_out[0] = ((acc[:ROWS] - goal[...].astype(jnp.float32)) / TOKENS).astype(jnp.bfloat16)
            pair_out[1] = (acc[ROWS:] / TOKENS).astype(jnp.bfloat16)
        else:
            pair_out[0] = acc[:ROWS].astype(jnp.bfloat16)
            pair_out[1] = acc[ROWS:].astype(jnp.bfloat16)


NORM = jax.ShapeDtypeStruct((2, ROWS, FEATURES), jnp.float32)
STAT = jax.ShapeDtypeStruct((2, ROWS, 128), jnp.float32)
SLOPE = jax.ShapeDtypeStruct((2, ROWS, HIDDEN), jnp.float32)
PAIR = jax.ShapeDtypeStruct((2, ROWS, FEATURES), jnp.bfloat16)
GRADS = jax.ShapeDtypeStruct((2 * ROWS, HIDDEN), jnp.bfloat16)
PARAMS = pltpu.CompilerParams(vmem_limit_bytes=VMEM_BYTES)


def first_call(micro, place, inputs, opening_n, opening_t, order, own_in, other_in, w_out):
    return pl.pallas_call(
        functools.partial(first_kernel, micro),
        out_shape=[PAIR, SLOPE],
        in_specs=[SMEM] + [WHOLE] * 7,
        out_specs=[WHOLE] * 2,
        scratch_shapes=[
            pltpu.VMEM((ROWS, FEATURES), jnp.bfloat16),
            pltpu.VMEM((2 * ROWS, FEATURES), jnp.float32),
        ],
        compiler_params=PARAMS,
        name="layer_up_0",
    )(place, inputs, opening_n, opening_t, order, own_in, other_in, w_out)


def forward_call(tick, place, pair, own_in, other_in, probe, w_out, order, goal):
    operands = [place, pair, own_in, other_in, probe, w_out, order] + ([goal] if tick == LAYERS - 1 else [])
    return pl.pallas_call(
        functools.partial(forward_kernel, tick),
        out_shape=[PAIR, NORM, STAT, SLOPE],
        in_specs=[SMEM] + [WHOLE] * (len(operands) - 1),
        out_specs=[WHOLE] * 4,
        scratch_shapes=[
            pltpu.VMEM((2 * ROWS, FEATURES), jnp.bfloat16),
            pltpu.VMEM((2 * ROWS, FEATURES), jnp.bfloat16),
            pltpu.VMEM((2 * ROWS, FEATURES), jnp.float32),
        ],
        compiler_params=PARAMS,
        name=f"layer_up_{tick}",
    )(*operands)


def turned_kernel(own_in, other_in, probe, w_out, order, token, w_in_t, probe_t, w_out_t):
    by_place = (((0,), (1,)), ((), ()))

    def step(index, carry):
        now = pl.ds(pl.multiple_of(index * FEATURES, FEATURES), FEATURES)
        own = lax.dot_general(own_in[:, now], order[:, OWN_HALF], by_place, preferred_element_type=jnp.float32)
        other = lax.dot_general(other_in[:, now], order[:, OTHER_HALF], by_place, preferred_element_type=jnp.float32)
        w_in_t[now, :] = (own + other).astype(jnp.bfloat16)
        probe_t[now, :] = probe[:, now].T
        w_out_t[:, now] = w_out[now, :].T
        return carry

    lax.fori_loop(0, HIDDEN // FEATURES, step, 0)


def turned_call(own_in, other_in, probe, w_out, order, token):
    tall = jax.ShapeDtypeStruct((HIDDEN, FEATURES), jnp.bfloat16)
    wide = jax.ShapeDtypeStruct((FEATURES, HIDDEN), jnp.bfloat16)
    return pl.pallas_call(
        turned_kernel,
        out_shape=[tall, tall, wide],
        in_specs=[WHOLE] * 5 + [pl.BlockSpec(memory_space=pl.ANY)],
        out_specs=[WHOLE] * 3,
        compiler_params=PARAMS,
        name="turned_weights",
    )(own_in, other_in, probe, w_out, order, token)


def hidden_grads(pair, w_out_t, slope, chunk):
    both = jnp.dot(
        pair[...].reshape(2 * ROWS, FEATURES), w_out_t[:, columns(chunk)], preferred_element_type=jnp.float32
    )
    grad_hidden, grad_hidden_t = both[:ROWS], both[ROWS:]
    slope_chunk = slope[0, :, columns(chunk)]
    grad_pre = grad_hidden * slope_chunk
    grad_pre_t = grad_hidden_t * slope_chunk + grad_hidden * slope[1, :, columns(chunk)]
    return grad_pre.astype(jnp.bfloat16), grad_pre_t.astype(jnp.bfloat16)


def norm_apply(values, normed, rscale):
    return rscale * (values - row_mean(values) - normed * row_mean(normed * values))


def backward_kernel(tick, *refs):
    place, pair, w_in_t, probe_t, w_out_t, norm, stat, slope = refs[:8]
    pair_out, grads, acc, acc_t = refs[8:]

    @pl.when(place[SECTION_AT] == LAYERS - 1 - tick)
    def _():
        acc[...] = jnp.zeros_like(acc)
        acc_t[...] = jnp.zeros_like(acc_t)

        def step(chunk, carry):
            low_grad, low_grad_t = hidden_grads(pair, w_out_t, slope, chunk)
            both = jnp.concatenate([low_grad_t, low_grad], axis=0)
            grads[:, columns(chunk)] = both
            acc[...] += jnp.dot(both, w_in_t[columns(chunk), :], preferred_element_type=jnp.float32)
            acc_t[...] += jnp.dot(low_grad, probe_t[columns(chunk), :], preferred_element_type=jnp.float32)
            return carry

        lax.fori_loop(0, CHUNKS, step, 0, unroll=UNROLL)
        normed, normed_t = norm[0], norm[1]
        rscale, tangent_dot = stat[0][:, :1], stat[1][:, :1]
        grad_norm = acc[ROWS:]
        grad_norm_t = acc[:ROWS] + acc_t[...]
        through = norm_apply(grad_norm, normed, rscale)
        through_t = (
            norm_apply(grad_norm_t, normed, rscale)
            - rscale * tangent_dot * through
            - rscale * (normed_t * row_mean(normed * grad_norm) + normed * row_mean(normed_t * grad_norm))
        )
        pair_out[0] = (pair[0].astype(jnp.float32) + through).astype(jnp.bfloat16)
        pair_out[1] = (pair[1].astype(jnp.float32) + through_t).astype(jnp.bfloat16)


def backward_call(tick, place, pair, w_in_t, probe_t, w_out_t, kept):
    operands = [place, pair, w_in_t, probe_t, w_out_t, *kept]
    return pl.pallas_call(
        functools.partial(backward_kernel, tick),
        out_shape=[PAIR, GRADS],
        in_specs=[SMEM] + [WHOLE] * (len(operands) - 1),
        out_specs=[WHOLE] * 2,
        scratch_shapes=[
            pltpu.VMEM((2 * ROWS, FEATURES), jnp.float32),
            pltpu.VMEM((ROWS, FEATURES), jnp.float32),
        ],
        compiler_params=PARAMS,
        name=f"layer_down_{tick}",
    )(*operands)


OWN_HALF = slice(0, FEATURES // 2)
OTHER_HALF = slice(FEATURES // 2, FEATURES)


def curvature_operands(micro, place, pair, w_out_t, slope, order, opening_n, norms, grads, lhs, rhs):
    @pl.when(place[SECTION_AT] == 0)
    def _():
        rows = slice(micro * ROWS, (micro + 1) * ROWS)
        lhs[:ROWS] = jnp.dot(opening_n[rows], order[...], preferred_element_type=jnp.float32).astype(jnp.bfloat16)
        lhs[ROWS:] = jnp.zeros((ROWS, FEATURES), jnp.bfloat16)

        def bottom(chunk, carry):
            low_grad, low_grad_t = hidden_grads(pair, w_out_t, slope, chunk)
            rhs[:, columns(chunk)] = jnp.concatenate([low_grad_t, low_grad], axis=0)
            return carry

        lax.fori_loop(0, CHUNKS, bottom, 0, unroll=UNROLL)

    for layer in range(1, LAYERS):

        @pl.when(place[SECTION_AT] == layer)
        def _():
            both = norms[layer - 1][...].reshape(2 * ROWS, FEATURES).astype(jnp.bfloat16)
            lhs[...] = jnp.dot(both, order[...], preferred_element_type=jnp.float32).astype(jnp.bfloat16)
            rhs[...] = grads[LAYERS - 1 - layer][...]


def curvature_kernel(micro, final, *refs):
    place, pair, w_out_t, slope, order, opening_n = refs[:6]
    norms, refs = refs[6 : 5 + LAYERS], refs[5 + LAYERS :]
    grads, refs = refs[: LAYERS - 1], refs[LAYERS - 1 :]
    if final:
        away_in, stay_in, refs = refs[0], refs[1], refs[2:]
    away, stay, lhs, rhs = refs
    curvature_operands(micro, place, pair, w_out_t, slope, order, opening_n, norms, grads, lhs, rhs)

    def step(chunk, carry):
        now = columns(chunk)

        def product(half):
            return lax.dot_general(lhs[:, half], rhs[:, now], CONTRACT_FIRST, preferred_element_type=jnp.float32)

        if final:
            away[:, now] = (away_in[:, now] + product(OTHER_HALF)).astype(jnp.bfloat16)
            stay[:, now] = stay_in[:, now] + product(OWN_HALF)
        else:
            away[:, now] = product(OTHER_HALF)
            stay[:, now] = product(OWN_HALF)
        return carry

    lax.fori_loop(0, CHUNKS, step, 0, unroll=UNROLL)


def curvature_call(micro, place, pair, w_out_t, slope, order, opening_n, norms, grads, sums):
    half = (FEATURES // 2, HIDDEN)
    final = bool(sums)
    operands = [place, pair, w_out_t, slope, order, opening_n, *norms, *grads, *sums]
    return pl.pallas_call(
        functools.partial(curvature_kernel, micro, final),
        out_shape=[
            jax.ShapeDtypeStruct(half, jnp.bfloat16 if final else jnp.float32),
            jax.ShapeDtypeStruct(half, jnp.float32),
        ],
        in_specs=[SMEM] + [WHOLE] * (len(operands) - 1),
        out_specs=[WHOLE] * 2,
        scratch_shapes=[
            pltpu.VMEM((2 * ROWS, FEATURES), jnp.bfloat16),
            pltpu.VMEM((2 * ROWS, HIDDEN), jnp.bfloat16),
        ],
        compiler_params=PARAMS,
        name="curvature_last" if final else "curvature_first",
    )(*operands)


def shards(inputs, targets, w_in, w_out, probes):
    place = jnp.stack([lax.axis_index(name) for name in (*DP, SECTION)]).astype(jnp.int32)
    place, out_block = settled_call(place, w_out[0])
    probe = probes[0]
    own_in, other_in = gathered(w_in[0], True)
    full_out = placed_call(place, *gathered(out_block, False))
    order, curvature_order, opening_n, opening_t = opening_call(place, inputs, probe)
    goal = routed(targets, goal_route)
    pairs, slopes, kept, grads = [None] * MICRO, [], [], []
    for micro in range(MICRO):
        kept.append([])
        grads.append([])
    for tick in range(LAYERS):
        for micro in range(MICRO):
            if tick == 0:
                pairs[micro], slope = first_call(
                    micro, place, inputs, opening_n, opening_t, order, own_in, other_in, full_out
                )
                slopes.append(slope)
            else:
                goal_now = goal[micro * ROWS : (micro + 1) * ROWS]
                pairs[micro], *stores = forward_call(
                    tick, place, pairs[micro], own_in, other_in, probe, full_out, order, goal_now
                )
                kept[micro].append(stores)
            if tick < LAYERS - 1:
                pairs[micro] = routed(pairs[micro], up_from(tick))
        if tick == TURN_TICK:
            turned = turned_call(own_in, other_in, probe, full_out, order, kept[-1][-1][0])
    for tick in range(LAYERS - 1):
        for micro in range(MICRO):
            pairs[micro], low_grads = backward_call(
                tick, place, pairs[micro], *turned, kept[micro][LAYERS - 2 - tick]
            )
            grads[micro].append(low_grads)
            pairs[micro] = routed(pairs[micro], down_from(LAYERS - 1 - tick))
    sums = ()
    for micro in range(MICRO):
        norms = [stores[0] for stores in kept[micro]]
        sums = curvature_call(
            micro, place, pairs[micro], turned[2], slopes[micro], curvature_order, opening_n, norms, grads[micro], sums
        )
    away, stay = sums
    other = routed(away, swap_core)
    summed = (stay + other.astype(jnp.float32)).astype(jnp.bfloat16)
    summed = lax.all_to_all(summed.reshape(4, 64, HIDDEN), "y", 0, 0, tiled=True)
    summed = jnp.sum(summed.astype(jnp.float32), axis=0).astype(jnp.bfloat16)
    summed = lax.all_to_all(summed.reshape(8, 8, HIDDEN), ("b1", "b2", "b4"), 0, 0, tiled=True)
    summed = jnp.sum(summed.astype(jnp.float32), axis=0)
    probe_own = lax.dynamic_slice_in_dim(probe, lax.axis_index(DP) * 8, 8, 0)
    return (probe_own.astype(jnp.float32) * summed)[None]


def solution(mesh):
    fine = Mesh(mesh.devices.reshape(SIZES), NAMES)
    return jax.shard_map(
        shards,
        mesh=fine,
        in_specs=(
            P(DP, None),
            P(DP, None),
            P(SECTION, DP, None),
            P(SECTION, DP, None),
            P(SECTION, None, None),
        ),
        out_specs=P(SECTION, DP, None),
        check_vma=False,
    )
```

```python
import functools
import itertools

import jax
import jax.numpy as jnp
from jax import lax
from jax.experimental import pallas as pl
from jax.experimental.pallas import tpu as pltpu
from jax.sharding import Mesh, PartitionSpec as P

EPSILON = 1e-05
SQRT_HALF = 0.7071067811865476
INV_ROOT_TWO_PI = 0.3989422804014327
CONTRACT_FIRST = (((0,), (0,)), ((), ()))

NAMES = ("zh", "x", "b4", "b2", "b1", "y", "c")
SIZES = (2, 4, 2, 2, 2, 4, 2)
SECTION = ("zh", "x")
DP = ("b4", "b2", "b1", "y", "c")
PLACES = 6
LAYERS = 8
FEATURES = 512
HIDDEN = 2048
MICRO = 2
ROWS = 128 // MICRO
UNROLL_UP = 1
UNROLL_DOWN = 2
UNROLL_LAST = 2
TURN_TICK = 3
TOKENS = 8192
CHUNK = 1024
CHUNKS = HIDDEN // CHUNK
VMEM_BYTES = 4 * 1024 * 1024
WHOLE = pl.BlockSpec(memory_space=pltpu.VMEM)
SMEM = pl.BlockSpec(memory_space=pltpu.SMEM)


def flat(place):
    index = 0
    for size, at in zip(SIZES, place):
        index = index * size + at
    return index


def routed(value, route):
    pairs = []
    for place in itertools.product(*(range(size) for size in SIZES)):
        there = route(*place)
        if there is not None:
            pairs.append((flat(place), flat(there)))
    return lax.ppermute(value, NAMES, pairs)


def swap_b4(zh, x, b4, b2, b1, y, c):
    return (zh, x, 1 - b4, b2, b1, y, c)


def goal_route(zh, x, b4, b2, b1, y, c):
    return (zh, x, 1 - b4, 1 - b2, 1 - b1, y, c) if (zh, x) == (1, 3) else None


def swap_b2(zh, x, b4, b2, b1, y, c):
    return (zh, x, b4, 1 - b2, b1, y, c)


def swap_b1(zh, x, b4, b2, b1, y, c):
    return (zh, x, b4, b2, 1 - b1, y, c)


def swap_even(zh, x, b4, b2, b1, y, c):
    return (zh, x, b4, b2, b1, y ^ 1, c)


def swap_odd(zh, x, b4, b2, b1, y, c):
    return (zh, x, b4, b2, b1, y ^ 3, c)


def swap_core(zh, x, b4, b2, b1, y, c):
    return (zh, x, b4, b2, b1, y, 1 - c)


def up_from(section):
    def route(zh, x, b4, b2, b1, y, c):
        if x != section % 4 or (x == 3 and zh == 1):
            return None
        if x == 3:
            return (1, 0, 1 - b4, 1 - b2, 1 - b1, y, c)
        return (zh, x + 1, b4, b2, b1, y, c)

    return route


def down_from(section):
    def route(zh, x, b4, b2, b1, y, c):
        if x != section % 4 or (x == 0 and zh == 0):
            return None
        if x == 0:
            return (0, 3, 1 - b4, 1 - b2, 1 - b1, y, c)
        return (zh, x - 1, b4, b2, b1, y, c)

    return route


def doubled(block, route):
    return jnp.concatenate([block, routed(block, route)], axis=0)


def gathered(block, even_first):
    for route in (swap_b4, swap_b2, swap_b1) + ((swap_even, swap_odd) if even_first else (swap_odd, swap_even)):
        block = doubled(block, route)
    return block, routed(block, swap_core)


def natural_block(place, b4, b2, b1, y, c):
    z = (b4 ^ place[0][0]) * 4 + (b2 ^ place[1][0]) * 2 + (b1 ^ place[2][0])
    return z * 8 + (y ^ place[3][0]) * 2 + (c ^ place[4][0])


def settled_kernel(*refs):
    block_in, block = refs[PLACES:]
    block[...] = block_in[...]


def settled_call(place, block):
    return pl.pallas_call(
        settled_kernel,
        out_shape=jax.ShapeDtypeStruct(block.shape, block.dtype),
        in_specs=[SMEM] * PLACES + [WHOLE],
        out_specs=WHOLE,
        compiler_params=PARAMS,
        name="settled",
    )(*place, block)


def placed_kernel(*refs):
    place = refs[:PLACES]
    own_out, other_out, full_out = refs[PLACES:]
    rows = HIDDEN // 64
    for core, half in enumerate((own_out, other_out)):
        for index in range(32):
            odd, even = index // 8 % 2, index // 16
            there = natural_block(place, index % 2, index // 2 % 2, index // 4 % 2, even ^ (odd * 3), core)
            full_out[pl.ds(pl.multiple_of(there * rows, rows), rows), :] = half[index * rows : (index + 1) * rows, :]


def placed_call(place, own_out, other_out):
    return pl.pallas_call(
        placed_kernel,
        out_shape=jax.ShapeDtypeStruct((HIDDEN, FEATURES), jnp.bfloat16),
        in_specs=[SMEM] * PLACES + [WHOLE] * 2,
        out_specs=WHOLE,
        compiler_params=PARAMS,
        name="placed_w_out",
    )(*place, own_out, other_out)


def row_mean(values):
    return jnp.mean(values, axis=-1, keepdims=True)


def columns(chunk):
    return pl.ds(pl.multiple_of(chunk * CHUNK, CHUNK), CHUNK)


def one_hot(natural_row):
    natural = lax.broadcasted_iota(jnp.int32, (FEATURES, FEATURES), 0)
    return jnp.where(natural == natural_row, 1.0, 0.0).astype(jnp.bfloat16)


def opening_kernel(*refs):
    place = refs[:PLACES]
    inputs, probe, order, curvature_order, normed_out, preact_t = refs[PLACES:]
    at = lax.broadcasted_iota(jnp.int32, (FEATURES, FEATURES), 1)
    row, b4, b2, b1 = at % 8, (at // 8) % 2, (at // 16) % 2, (at // 32) % 2
    even, odd, core = (at // 64) % 2, (at // 128) % 2, at // 256
    order[...] = one_hot(natural_block(place, b4, b2, b1, even ^ (odd * 3), core) * 8 + row)
    block = (b4 * 4 + b2 * 2 + b1) * 8 + ((at // 64) % 4) * 2 + (core ^ place[4][0])
    curvature_order[...] = one_hot(block * 8 + row)
    inflow = inputs[...].astype(jnp.float32)
    centred = inflow - row_mean(inflow)
    normed = (centred * lax.rsqrt(row_mean(centred * centred) + EPSILON)).astype(jnp.bfloat16)
    normed_out[...] = normed

    def step(chunk, carry):
        preact_t[:, columns(chunk)] = jnp.dot(normed, probe[:, columns(chunk)], preferred_element_type=jnp.float32)
        return carry

    lax.fori_loop(0, CHUNKS, step, 0)


def opening_call(place, inputs, probe):
    rows = inputs.shape[0]
    order = jax.ShapeDtypeStruct((FEATURES, FEATURES), jnp.bfloat16)
    return pl.pallas_call(
        opening_kernel,
        out_shape=[
            order,
            order,
            jax.ShapeDtypeStruct((rows, FEATURES), jnp.bfloat16),
            jax.ShapeDtypeStruct((rows, HIDDEN), jnp.float32),
        ],
        in_specs=[SMEM] * PLACES + [WHOLE] * 2,
        out_specs=[WHOLE] * 4,
        compiler_params=PARAMS,
        name="opening",
    )(*place, inputs, probe)


def gelu_slopes(preact, preact_t, slope_out, chunk):
    normal_cdf = 0.5 * (1.0 + lax.erf(preact * SQRT_HALF))
    density = INV_ROOT_TWO_PI * jnp.exp(-0.5 * preact * preact)
    slope = normal_cdf + preact * density
    slope_out[0, :, columns(chunk)] = slope
    slope_out[1, :, columns(chunk)] = density * (2.0 - preact * preact) * preact_t
    return jnp.concatenate([preact * normal_cdf, slope * preact_t], axis=0).astype(jnp.bfloat16)


def halves_product(lhs, own_in, other_in, now):
    return jnp.dot(lhs[:, OWN_HALF], own_in[:, now], preferred_element_type=jnp.float32) + jnp.dot(
        lhs[:, OTHER_HALF], other_in[:, now], preferred_element_type=jnp.float32
    )


def first_kernel(micro, section, inputs, opening_n, opening_t, order, own_in, other_in, w_out, pair_out, slope_out, lhs, acc):
    rows = slice(micro * ROWS, (micro + 1) * ROWS)

    @pl.when(section[0] == 0)
    def _():
        lhs[...] = jnp.dot(opening_n[rows], order[...], preferred_element_type=jnp.float32).astype(jnp.bfloat16)
        acc[:ROWS] = inputs[rows].astype(jnp.float32)
        acc[ROWS:] = jnp.zeros((ROWS, FEATURES), jnp.float32)

        def step(chunk, carry):
            preact = halves_product(lhs[...], own_in, other_in, columns(chunk))
            hidden = gelu_slopes(preact, opening_t[rows, columns(chunk)], slope_out, chunk)
            acc[...] += jnp.dot(hidden, w_out[columns(chunk), :], preferred_element_type=jnp.float32)
            return carry

        lax.fori_loop(0, CHUNKS, step, 0, unroll=UNROLL_LAST)
        pair_out[0] = acc[:ROWS].astype(jnp.bfloat16)
        pair_out[1] = acc[ROWS:].astype(jnp.bfloat16)


def forward_kernel(tick, *refs):
    last = tick == LAYERS - 1
    section, pair, own_in, other_in, probe, w_out, order = refs[:7]
    refs = refs[7:]
    if last:
        goal, refs = refs[0], refs[1:]
    pair_out, norm, stat, slope_out, natural, lhs, acc = refs

    @pl.when(section[0] == tick)
    def _():
        inflow = pair[0].astype(jnp.float32)
        inflow_t = pair[1].astype(jnp.float32)
        centred = inflow - row_mean(inflow)
        rscale = lax.rsqrt(row_mean(centred * centred) + EPSILON)
        normed = centred * rscale
        tangent_dot = row_mean(normed * inflow_t)
        normed_t = rscale * (inflow_t - row_mean(inflow_t) - normed * tangent_dot)
        norm[0] = normed
        norm[1] = normed_t
        stat[0] = jnp.broadcast_to(rscale, (ROWS, 128))
        stat[1] = jnp.broadcast_to(tangent_dot, (ROWS, 128))
        acc[:ROWS] = inflow
        acc[ROWS:] = inflow_t
        natural[:ROWS] = normed.astype(jnp.bfloat16)
        natural[ROWS:] = normed_t.astype(jnp.bfloat16)
        lhs[...] = jnp.dot(natural[...], order[...], preferred_element_type=jnp.float32).astype(jnp.bfloat16)

        def step(chunk, carry):
            both = halves_product(lhs[...], own_in, other_in, columns(chunk))
            preact_t = both[ROWS:] + jnp.dot(
                natural[:ROWS], probe[:, columns(chunk)], preferred_element_type=jnp.float32
            )
            hidden = gelu_slopes(both[:ROWS], preact_t, slope_out, chunk)
            acc[...] += jnp.dot(hidden, w_out[columns(chunk), :], preferred_element_type=jnp.float32)
            return carry

        lax.fori_loop(0, CHUNKS, step, 0, unroll=UNROLL_UP)
        if last:
            pair_out[0] = ((acc[:ROWS] - goal[...].astype(jnp.float32)) / TOKENS).astype(jnp.bfloat16)
            pair_out[1] = (acc[ROWS:] / TOKENS).astype(jnp.bfloat16)
        else:
            pair_out[0] = acc[:ROWS].astype(jnp.bfloat16)
            pair_out[1] = acc[ROWS:].astype(jnp.bfloat16)


NORM = jax.ShapeDtypeStruct((2, ROWS, FEATURES), jnp.float32)
STAT = jax.ShapeDtypeStruct((2, ROWS, 128), jnp.float32)
SLOPE = jax.ShapeDtypeStruct((2, ROWS, HIDDEN), jnp.float32)
PAIR = jax.ShapeDtypeStruct((2, ROWS, FEATURES), jnp.bfloat16)
GRADS = jax.ShapeDtypeStruct((2 * ROWS, HIDDEN), jnp.bfloat16)
PARAMS = pltpu.CompilerParams(vmem_limit_bytes=VMEM_BYTES)


def first_call(micro, section, inputs, opening_n, opening_t, order, own_in, other_in, w_out):
    return pl.pallas_call(
        functools.partial(first_kernel, micro),
        out_shape=[PAIR, SLOPE],
        in_specs=[SMEM] + [WHOLE] * 7,
        out_specs=[WHOLE] * 2,
        scratch_shapes=[
            pltpu.VMEM((ROWS, FEATURES), jnp.bfloat16),
            pltpu.VMEM((2 * ROWS, FEATURES), jnp.float32),
        ],
        compiler_params=PARAMS,
        name="layer_up_0",
    )(section, inputs, opening_n, opening_t, order, own_in, other_in, w_out)


def forward_call(tick, section, pair, own_in, other_in, probe, w_out, order, goal):
    operands = [section, pair, own_in, other_in, probe, w_out, order] + ([goal] if tick == LAYERS - 1 else [])
    return pl.pallas_call(
        functools.partial(forward_kernel, tick),
        out_shape=[PAIR, NORM, STAT, SLOPE],
        in_specs=[SMEM] + [WHOLE] * (len(operands) - 1),
        out_specs=[WHOLE] * 4,
        scratch_shapes=[
            pltpu.VMEM((2 * ROWS, FEATURES), jnp.bfloat16),
            pltpu.VMEM((2 * ROWS, FEATURES), jnp.bfloat16),
            pltpu.VMEM((2 * ROWS, FEATURES), jnp.float32),
        ],
        compiler_params=PARAMS,
        name=f"layer_up_{tick}",
    )(*operands)


def turned_kernel(own_in, other_in, probe, w_out, order, token, w_in_t, probe_t, w_out_t):
    by_place = (((0,), (1,)), ((), ()))

    def step(index, carry):
        now = pl.ds(pl.multiple_of(index * FEATURES, FEATURES), FEATURES)
        own = lax.dot_general(own_in[:, now], order[:, OWN_HALF], by_place, preferred_element_type=jnp.float32)
        other = lax.dot_general(other_in[:, now], order[:, OTHER_HALF], by_place, preferred_element_type=jnp.float32)
        w_in_t[now, :] = (own + other).astype(jnp.bfloat16)
        probe_t[now, :] = probe[:, now].T
        w_out_t[:, now] = w_out[now, :].T
        return carry

    lax.fori_loop(0, HIDDEN // FEATURES, step, 0)


def turned_call(own_in, other_in, probe, w_out, order, token):
    tall = jax.ShapeDtypeStruct((HIDDEN, FEATURES), jnp.bfloat16)
    wide = jax.ShapeDtypeStruct((FEATURES, HIDDEN), jnp.bfloat16)
    return pl.pallas_call(
        turned_kernel,
        out_shape=[tall, tall, wide],
        in_specs=[WHOLE] * 5 + [pl.BlockSpec(memory_space=pl.ANY)],
        out_specs=[WHOLE] * 3,
        compiler_params=PARAMS,
        name="turned_weights",
    )(own_in, other_in, probe, w_out, order, token)


def hidden_grads(pair, w_out_t, slope, chunk):
    both = jnp.dot(
        pair[...].reshape(2 * ROWS, FEATURES), w_out_t[:, columns(chunk)], preferred_element_type=jnp.float32
    )
    grad_hidden, grad_hidden_t = both[:ROWS], both[ROWS:]
    slope_chunk = slope[0, :, columns(chunk)]
    grad_pre = grad_hidden * slope_chunk
    grad_pre_t = grad_hidden_t * slope_chunk + grad_hidden * slope[1, :, columns(chunk)]
    return grad_pre.astype(jnp.bfloat16), grad_pre_t.astype(jnp.bfloat16)


def norm_apply(values, normed, rscale):
    return rscale * (values - row_mean(values) - normed * row_mean(normed * values))


def backward_kernel(tick, *refs):
    section, pair, w_in_t, probe_t, w_out_t, norm, stat, slope = refs[:8]
    pair_out, grads, acc, acc_t = refs[8:]

    @pl.when(section[0] == LAYERS - 1 - tick)
    def _():
        acc[...] = jnp.zeros_like(acc)
        acc_t[...] = jnp.zeros_like(acc_t)

        def step(chunk, carry):
            low_grad, low_grad_t = hidden_grads(pair, w_out_t, slope, chunk)
            both = jnp.concatenate([low_grad_t, low_grad], axis=0)
            grads[:, columns(chunk)] = both
            acc[...] += jnp.dot(both, w_in_t[columns(chunk), :], preferred_element_type=jnp.float32)
            acc_t[...] += jnp.dot(low_grad, probe_t[columns(chunk), :], preferred_element_type=jnp.float32)
            return carry

        lax.fori_loop(0, CHUNKS, step, 0, unroll=UNROLL_DOWN)
        normed, normed_t = norm[0], norm[1]
        rscale, tangent_dot = stat[0][:, :1], stat[1][:, :1]
        grad_norm = acc[ROWS:]
        grad_norm_t = acc[:ROWS] + acc_t[...]
        through = norm_apply(grad_norm, normed, rscale)
        through_t = (
            norm_apply(grad_norm_t, normed, rscale)
            - rscale * tangent_dot * through
            - rscale * (normed_t * row_mean(normed * grad_norm) + normed * row_mean(normed_t * grad_norm))
        )
        pair_out[0] = (pair[0].astype(jnp.float32) + through).astype(jnp.bfloat16)
        pair_out[1] = (pair[1].astype(jnp.float32) + through_t).astype(jnp.bfloat16)


def backward_call(tick, section, pair, w_in_t, probe_t, w_out_t, kept):
    operands = [section, pair, w_in_t, probe_t, w_out_t, *kept]
    return pl.pallas_call(
        functools.partial(backward_kernel, tick),
        out_shape=[PAIR, GRADS],
        in_specs=[SMEM] + [WHOLE] * (len(operands) - 1),
        out_specs=[WHOLE] * 2,
        scratch_shapes=[
            pltpu.VMEM((2 * ROWS, FEATURES), jnp.float32),
            pltpu.VMEM((ROWS, FEATURES), jnp.float32),
        ],
        compiler_params=PARAMS,
        name=f"layer_down_{tick}",
    )(*operands)


OWN_HALF = slice(0, FEATURES // 2)
OTHER_HALF = slice(FEATURES // 2, FEATURES)


def curvature_operands(micro, section, pair, w_out_t, slope, order, opening_n, norms, grads, lhs, rhs):
    @pl.when(section[0] == 0)
    def _():
        rows = slice(micro * ROWS, (micro + 1) * ROWS)
        lhs[:ROWS] = jnp.dot(opening_n[rows], order[...], preferred_element_type=jnp.float32).astype(jnp.bfloat16)
        lhs[ROWS:] = jnp.zeros((ROWS, FEATURES), jnp.bfloat16)

        def bottom(chunk, carry):
            low_grad, low_grad_t = hidden_grads(pair, w_out_t, slope, chunk)
            rhs[:, columns(chunk)] = jnp.concatenate([low_grad_t, low_grad], axis=0)
            return carry

        lax.fori_loop(0, CHUNKS, bottom, 0, unroll=UNROLL_LAST)

    for layer in range(1, LAYERS):

        @pl.when(section[0] == layer)
        def _():
            both = norms[layer - 1][...].reshape(2 * ROWS, FEATURES).astype(jnp.bfloat16)
            lhs[...] = jnp.dot(both, order[...], preferred_element_type=jnp.float32).astype(jnp.bfloat16)
            rhs[...] = grads[LAYERS - 1 - layer][...]


def curvature_kernel(micro, final, *refs):
    section, pair, w_out_t, slope, order, opening_n = refs[:6]
    norms, refs = refs[6 : 5 + LAYERS], refs[5 + LAYERS :]
    grads, refs = refs[: LAYERS - 1], refs[LAYERS - 1 :]
    if final:
        away_in, stay_in, refs = refs[0], refs[1], refs[2:]
    away, stay, lhs, rhs = refs
    curvature_operands(micro, section, pair, w_out_t, slope, order, opening_n, norms, grads, lhs, rhs)

    def step(chunk, carry):
        now = columns(chunk)

        def product(half):
            return lax.dot_general(lhs[:, half], rhs[:, now], CONTRACT_FIRST, preferred_element_type=jnp.float32)

        if final:
            away[:, now] = (away_in[:, now] + product(OTHER_HALF)).astype(jnp.bfloat16)
            stay[:, now] = stay_in[:, now] + product(OWN_HALF)
        else:
            away[:, now] = product(OTHER_HALF)
            stay[:, now] = product(OWN_HALF)
        return carry

    lax.fori_loop(0, CHUNKS, step, 0, unroll=UNROLL_LAST)


def curvature_call(micro, section, pair, w_out_t, slope, order, opening_n, norms, grads, sums):
    half = (FEATURES // 2, HIDDEN)
    final = bool(sums)
    operands = [section, pair, w_out_t, slope, order, opening_n, *norms, *grads, *sums]
    return pl.pallas_call(
        functools.partial(curvature_kernel, micro, final),
        out_shape=[
            jax.ShapeDtypeStruct(half, jnp.bfloat16 if final else jnp.float32),
            jax.ShapeDtypeStruct(half, jnp.float32),
        ],
        in_specs=[SMEM] + [WHOLE] * (len(operands) - 1),
        out_specs=[WHOLE] * 2,
        scratch_shapes=[
            pltpu.VMEM((2 * ROWS, FEATURES), jnp.bfloat16),
            pltpu.VMEM((2 * ROWS, HIDDEN), jnp.bfloat16),
        ],
        compiler_params=PARAMS,
        name="curvature_last" if final else "curvature_first",
    )(*operands)


def shards(inputs, targets, w_in, w_out, probes):
    place = [jnp.reshape(lax.axis_index(name), (1,)).astype(jnp.int32) for name in (*DP, SECTION)]
    section = place[-1]
    out_block = settled_call(place, w_out[0])
    probe = probes[0]
    own_in, other_in = gathered(w_in[0], True)
    full_out = placed_call(place, *gathered(out_block, False))
    order, curvature_order, opening_n, opening_t = opening_call(place, inputs, probe)
    goal = routed(targets, goal_route)
    pairs, slopes, kept, grads = [None] * MICRO, [], [], []
    for micro in range(MICRO):
        kept.append([])
        grads.append([])
    for tick in range(LAYERS):
        for micro in range(MICRO):
            if tick == 0:
                pairs[micro], slope = first_call(
                    micro, section, inputs, opening_n, opening_t, order, own_in, other_in, full_out
                )
                slopes.append(slope)
            else:
                goal_now = goal[micro * ROWS : (micro + 1) * ROWS]
                pairs[micro], *stores = forward_call(
                    tick, section, pairs[micro], own_in, other_in, probe, full_out, order, goal_now
                )
                kept[micro].append(stores)
            if tick < LAYERS - 1:
                pairs[micro] = routed(pairs[micro], up_from(tick))
        if tick == TURN_TICK:
            turned = turned_call(own_in, other_in, probe, full_out, order, kept[-1][-1][0])
    for tick in range(LAYERS - 1):
        for micro in range(MICRO):
            pairs[micro], low_grads = backward_call(
                tick, section, pairs[micro], *turned, kept[micro][LAYERS - 2 - tick]
            )
            grads[micro].append(low_grads)
            pairs[micro] = routed(pairs[micro], down_from(LAYERS - 1 - tick))
    sums = ()
    for micro in range(MICRO):
        norms = [stores[0] for stores in kept[micro]]
        sums = curvature_call(
            micro, section, pairs[micro], turned[2], slopes[micro], curvature_order, opening_n, norms, grads[micro], sums
        )
    away, stay = sums
    other = routed(away, swap_core)
    summed = (stay + other.astype(jnp.float32)).astype(jnp.bfloat16)
    summed = lax.all_to_all(summed.reshape(4, 64, HIDDEN), "y", 0, 0, tiled=True)
    summed = jnp.sum(summed.astype(jnp.float32), axis=0).astype(jnp.bfloat16)
    summed = lax.all_to_all(summed.reshape(8, 8, HIDDEN), ("b1", "b2", "b4"), 0, 0, tiled=True)
    summed = jnp.sum(summed.astype(jnp.float32), axis=0)
    probe_own = lax.dynamic_slice_in_dim(probe, lax.axis_index(DP) * 8, 8, 0)
    return (probe_own.astype(jnp.float32) * summed)[None]


def solution(mesh):
    fine = Mesh(mesh.devices.reshape(SIZES), NAMES)
    return jax.shard_map(
        shards,
        mesh=fine,
        in_specs=(
            P(DP, None),
            P(DP, None),
            P(SECTION, DP, None),
            P(SECTION, DP, None),
            P(SECTION, None, None),
        ),
        out_specs=P(SECTION, DP, None),
        check_vma=False,
    )
```

```python
import functools
import itertools

import jax
import jax.numpy as jnp
from jax import lax
from jax.experimental import pallas as pl
from jax.experimental.pallas import tpu as pltpu
from jax.sharding import Mesh, PartitionSpec as P

EPSILON = 1e-05
SQRT_HALF = 0.7071067811865476
INV_ROOT_TWO_PI = 0.3989422804014327
CONTRACT_FIRST = (((0,), (0,)), ((), ()))

NAMES = ("zh", "x", "b4", "b2", "b1", "y", "c")
SIZES = (2, 4, 2, 2, 2, 4, 2)
SECTION = ("zh", "x")
DP = ("b4", "b2", "b1", "y", "c")
PLACES = 6
LAYERS = 8
FEATURES = 512
HIDDEN = 2048
MICRO = 2
ROWS = 128 // MICRO
UNROLL_UP = 1
UNROLL_DOWN = 2
UNROLL_LAST = 2
TURN_TICK = 3
CROSS_TICK = 4
TOKENS = 8192
CHUNK = 1024
CHUNKS = HIDDEN // CHUNK
VMEM_BYTES = 4 * 1024 * 1024
WHOLE = pl.BlockSpec(memory_space=pltpu.VMEM)
SMEM = pl.BlockSpec(memory_space=pltpu.SMEM)


def flat(place):
    index = 0
    for size, at in zip(SIZES, place):
        index = index * size + at
    return index


def routed(value, route):
    pairs = []
    for place in itertools.product(*(range(size) for size in SIZES)):
        there = route(*place)
        if there is not None:
            pairs.append((flat(place), flat(there)))
    return lax.ppermute(value, NAMES, pairs)


def swap_b4(zh, x, b4, b2, b1, y, c):
    return (zh, x, 1 - b4, b2, b1, y, c)


def goal_route(zh, x, b4, b2, b1, y, c):
    return (zh, x, 1 - b4, 1 - b2, 1 - b1, y, c) if (zh, x) == (1, 3) else None


def swap_b2(zh, x, b4, b2, b1, y, c):
    return (zh, x, b4, 1 - b2, b1, y, c)


def swap_b1(zh, x, b4, b2, b1, y, c):
    return (zh, x, b4, b2, 1 - b1, y, c)


def swap_even(zh, x, b4, b2, b1, y, c):
    return (zh, x, b4, b2, b1, y ^ 1, c)


def swap_odd(zh, x, b4, b2, b1, y, c):
    return (zh, x, b4, b2, b1, y ^ 3, c)


def swap_core(zh, x, b4, b2, b1, y, c):
    return (zh, x, b4, b2, b1, y, 1 - c)


def up_from(section):
    def route(zh, x, b4, b2, b1, y, c):
        return (zh, x + 1, b4, b2, b1, y, c) if x == section % 4 else None

    return route


def down_from(section):
    def route(zh, x, b4, b2, b1, y, c):
        return (zh, x - 1, b4, b2, b1, y, c) if x == section % 4 else None

    return route


def up_across(zh, x, b4, b2, b1, y, c):
    if (zh, x) != (0, 3):
        return None
    return (0, 0, b4, b2, b1, y, 1) if c else (1, 0, 1 - b4, 1 - b2, 1 - b1, y, 0)


def up_relayed(zh, x, b4, b2, b1, y, c):
    return (1, 0, 1 - b4, 1 - b2, 1 - b1, y, 1) if (zh, x, c) == (0, 0, 1) else None


def down_across(zh, x, b4, b2, b1, y, c):
    if (zh, x) != (1, 0):
        return None
    return (0, 3, 1 - b4, 1 - b2, 1 - b1, y, 1) if c else (1, 3, b4, b2, b1, y, 0)


def down_relayed(zh, x, b4, b2, b1, y, c):
    return (0, 3, 1 - b4, 1 - b2, 1 - b1, y, 0) if (zh, x, c) == (1, 3, 0) else None


def doubled(block, route):
    return jnp.concatenate([block, routed(block, route)], axis=0)


def gathered(block, even_first):
    for route in (swap_b4, swap_b2, swap_b1) + ((swap_even, swap_odd) if even_first else (swap_odd, swap_even)):
        block = doubled(block, route)
    return block, routed(block, swap_core)


def natural_block(place, b4, b2, b1, y, c):
    z = (b4 ^ place[0][0]) * 4 + (b2 ^ place[1][0]) * 2 + (b1 ^ place[2][0])
    return z * 8 + (y ^ place[3][0]) * 2 + (c ^ place[4][0])


def settled_kernel(*refs):
    block_in, block = refs[PLACES:]
    block[...] = block_in[...]


def settled_call(place, block):
    return pl.pallas_call(
        settled_kernel,
        out_shape=jax.ShapeDtypeStruct(block.shape, block.dtype),
        in_specs=[SMEM] * PLACES + [WHOLE],
        out_specs=WHOLE,
        compiler_params=PARAMS,
        name="settled",
    )(*place, block)


def placed_kernel(*refs):
    place = refs[:PLACES]
    own_out, other_out, full_out = refs[PLACES:]
    rows = HIDDEN // 64
    for core, half in enumerate((own_out, other_out)):
        for index in range(32):
            odd, even = index // 8 % 2, index // 16
            there = natural_block(place, index % 2, index // 2 % 2, index // 4 % 2, even ^ (odd * 3), core)
            full_out[pl.ds(pl.multiple_of(there * rows, rows), rows), :] = half[index * rows : (index + 1) * rows, :]


def placed_call(place, own_out, other_out):
    return pl.pallas_call(
        placed_kernel,
        out_shape=jax.ShapeDtypeStruct((HIDDEN, FEATURES), jnp.bfloat16),
        in_specs=[SMEM] * PLACES + [WHOLE] * 2,
        out_specs=WHOLE,
        compiler_params=PARAMS,
        name="placed_w_out",
    )(*place, own_out, other_out)


def row_mean(values):
    return jnp.mean(values, axis=-1, keepdims=True)


def columns(chunk):
    return pl.ds(pl.multiple_of(chunk * CHUNK, CHUNK), CHUNK)


def one_hot(natural_row):
    natural = lax.broadcasted_iota(jnp.int32, (FEATURES, FEATURES), 0)
    return jnp.where(natural == natural_row, 1.0, 0.0).astype(jnp.bfloat16)


def opening_kernel(*refs):
    place = refs[:PLACES]
    inputs, probe, order, curvature_order, normed_out, preact_t = refs[PLACES:]
    at = lax.broadcasted_iota(jnp.int32, (FEATURES, FEATURES), 1)
    row, b4, b2, b1 = at % 8, (at // 8) % 2, (at // 16) % 2, (at // 32) % 2
    even, odd, core = (at // 64) % 2, (at // 128) % 2, at // 256
    order[...] = one_hot(natural_block(place, b4, b2, b1, even ^ (odd * 3), core) * 8 + row)
    block = (b4 * 4 + b2 * 2 + b1) * 8 + ((at // 64) % 4) * 2 + (core ^ place[4][0])
    curvature_order[...] = one_hot(block * 8 + row)
    inflow = inputs[...].astype(jnp.float32)
    centred = inflow - row_mean(inflow)
    normed = (centred * lax.rsqrt(row_mean(centred * centred) + EPSILON)).astype(jnp.bfloat16)
    normed_out[...] = normed

    def step(chunk, carry):
        preact_t[:, columns(chunk)] = jnp.dot(normed, probe[:, columns(chunk)], preferred_element_type=jnp.float32)
        return carry

    lax.fori_loop(0, CHUNKS, step, 0)


def opening_call(place, inputs, probe):
    rows = inputs.shape[0]
    order = jax.ShapeDtypeStruct((FEATURES, FEATURES), jnp.bfloat16)
    return pl.pallas_call(
        opening_kernel,
        out_shape=[
            order,
            order,
            jax.ShapeDtypeStruct((rows, FEATURES), jnp.bfloat16),
            jax.ShapeDtypeStruct((rows, HIDDEN), jnp.float32),
        ],
        in_specs=[SMEM] * PLACES + [WHOLE] * 2,
        out_specs=[WHOLE] * 4,
        compiler_params=PARAMS,
        name="opening",
    )(*place, inputs, probe)


def gelu_slopes(preact, preact_t, slope_out, chunk):
    normal_cdf = 0.5 * (1.0 + lax.erf(preact * SQRT_HALF))
    density = INV_ROOT_TWO_PI * jnp.exp(-0.5 * preact * preact)
    slope = normal_cdf + preact * density
    slope_out[0, :, columns(chunk)] = slope
    slope_out[1, :, columns(chunk)] = density * (2.0 - preact * preact) * preact_t
    return jnp.concatenate([preact * normal_cdf, slope * preact_t], axis=0).astype(jnp.bfloat16)


def halves_product(lhs, own_in, other_in, now):
    return jnp.dot(lhs[:, OWN_HALF], own_in[:, now], preferred_element_type=jnp.float32) + jnp.dot(
        lhs[:, OTHER_HALF], other_in[:, now], preferred_element_type=jnp.float32
    )


def first_kernel(micro, section, inputs, opening_n, opening_t, order, own_in, other_in, w_out, pair_out, slope_out, lhs, acc):
    rows = slice(micro * ROWS, (micro + 1) * ROWS)

    @pl.when(section[0] == 0)
    def _():
        lhs[...] = jnp.dot(opening_n[rows], order[...], preferred_element_type=jnp.float32).astype(jnp.bfloat16)
        acc[:ROWS] = inputs[rows].astype(jnp.float32)
        acc[ROWS:] = jnp.zeros((ROWS, FEATURES), jnp.float32)

        def step(chunk, carry):
            preact = halves_product(lhs[...], own_in, other_in, columns(chunk))
            hidden = gelu_slopes(preact, opening_t[rows, columns(chunk)], slope_out, chunk)
            acc[...] += jnp.dot(hidden, w_out[columns(chunk), :], preferred_element_type=jnp.float32)
            return carry

        lax.fori_loop(0, CHUNKS, step, 0, unroll=UNROLL_LAST)
        pair_out[0] = acc[:ROWS].astype(jnp.bfloat16)
        pair_out[1] = acc[ROWS:].astype(jnp.bfloat16)


def forward_kernel(tick, *refs):
    last = tick == LAYERS - 1
    section, own_in, other_in, probe, w_out, order = refs[:6]
    pairs, refs = (refs[6:8], refs[8:]) if tick == CROSS_TICK else (refs[6:7], refs[7:])
    if last:
        goal, refs = refs[0], refs[1:]
    pair_out, norm, stat, slope_out, natural, lhs, acc = refs

    @pl.when(section[0] == tick)
    def _():
        inflow = sum(pair[0].astype(jnp.float32) for pair in pairs)
        inflow_t = sum(pair[1].astype(jnp.float32) for pair in pairs)
        centred = inflow - row_mean(inflow)
        rscale = lax.rsqrt(row_mean(centred * centred) + EPSILON)
        normed = centred * rscale
        tangent_dot = row_mean(normed * inflow_t)
        normed_t = rscale * (inflow_t - row_mean(inflow_t) - normed * tangent_dot)
        norm[0] = normed
        norm[1] = normed_t
        stat[0] = jnp.broadcast_to(rscale, (ROWS, 128))
        stat[1] = jnp.broadcast_to(tangent_dot, (ROWS, 128))
        acc[:ROWS] = inflow
        acc[ROWS:] = inflow_t
        natural[:ROWS] = normed.astype(jnp.bfloat16)
        natural[ROWS:] = normed_t.astype(jnp.bfloat16)
        lhs[...] = jnp.dot(natural[...], order[...], preferred_element_type=jnp.float32).astype(jnp.bfloat16)

        def step(chunk, carry):
            both = halves_product(lhs[...], own_in, other_in, columns(chunk))
            preact_t = both[ROWS:] + jnp.dot(
                natural[:ROWS], probe[:, columns(chunk)], preferred_element_type=jnp.float32
            )
            hidden = gelu_slopes(both[:ROWS], preact_t, slope_out, chunk)
            acc[...] += jnp.dot(hidden, w_out[columns(chunk), :], preferred_element_type=jnp.float32)
            return carry

        lax.fori_loop(0, CHUNKS, step, 0, unroll=UNROLL_UP)
        if last:
            pair_out[0] = ((acc[:ROWS] - goal[...].astype(jnp.float32)) / TOKENS).astype(jnp.bfloat16)
            pair_out[1] = (acc[ROWS:] / TOKENS).astype(jnp.bfloat16)
        else:
            pair_out[0] = acc[:ROWS].astype(jnp.bfloat16)
            pair_out[1] = acc[ROWS:].astype(jnp.bfloat16)


NORM = jax.ShapeDtypeStruct((2, ROWS, FEATURES), jnp.float32)
STAT = jax.ShapeDtypeStruct((2, ROWS, 128), jnp.float32)
SLOPE = jax.ShapeDtypeStruct((2, ROWS, HIDDEN), jnp.float32)
PAIR = jax.ShapeDtypeStruct((2, ROWS, FEATURES), jnp.bfloat16)
GRADS = jax.ShapeDtypeStruct((2 * ROWS, HIDDEN), jnp.bfloat16)
PARAMS = pltpu.CompilerParams(vmem_limit_bytes=VMEM_BYTES)


def first_call(micro, section, inputs, opening_n, opening_t, order, own_in, other_in, w_out):
    return pl.pallas_call(
        functools.partial(first_kernel, micro),
        out_shape=[PAIR, SLOPE],
        in_specs=[SMEM] + [WHOLE] * 7,
        out_specs=[WHOLE] * 2,
        scratch_shapes=[
            pltpu.VMEM((ROWS, FEATURES), jnp.bfloat16),
            pltpu.VMEM((2 * ROWS, FEATURES), jnp.float32),
        ],
        compiler_params=PARAMS,
        name="layer_up_0",
    )(section, inputs, opening_n, opening_t, order, own_in, other_in, w_out)


def forward_call(tick, section, pairs, own_in, other_in, probe, w_out, order, goal):
    operands = [section, own_in, other_in, probe, w_out, order, *pairs] + ([goal] if tick == LAYERS - 1 else [])
    return pl.pallas_call(
        functools.partial(forward_kernel, tick),
        out_shape=[PAIR, NORM, STAT, SLOPE],
        in_specs=[SMEM] + [WHOLE] * (len(operands) - 1),
        out_specs=[WHOLE] * 4,
        scratch_shapes=[
            pltpu.VMEM((2 * ROWS, FEATURES), jnp.bfloat16),
            pltpu.VMEM((2 * ROWS, FEATURES), jnp.bfloat16),
            pltpu.VMEM((2 * ROWS, FEATURES), jnp.float32),
        ],
        compiler_params=PARAMS,
        name=f"layer_up_{tick}",
    )(*operands)


def turned_kernel(own_in, other_in, probe, w_out, order, token, w_in_t, probe_t, w_out_t):
    by_place = (((0,), (1,)), ((), ()))

    def step(index, carry):
        now = pl.ds(pl.multiple_of(index * FEATURES, FEATURES), FEATURES)
        own = lax.dot_general(own_in[:, now], order[:, OWN_HALF], by_place, preferred_element_type=jnp.float32)
        other = lax.dot_general(other_in[:, now], order[:, OTHER_HALF], by_place, preferred_element_type=jnp.float32)
        w_in_t[now, :] = (own + other).astype(jnp.bfloat16)
        probe_t[now, :] = probe[:, now].T
        w_out_t[:, now] = w_out[now, :].T
        return carry

    lax.fori_loop(0, HIDDEN // FEATURES, step, 0)


def turned_call(own_in, other_in, probe, w_out, order, token):
    tall = jax.ShapeDtypeStruct((HIDDEN, FEATURES), jnp.bfloat16)
    wide = jax.ShapeDtypeStruct((FEATURES, HIDDEN), jnp.bfloat16)
    return pl.pallas_call(
        turned_kernel,
        out_shape=[tall, tall, wide],
        in_specs=[WHOLE] * 5 + [pl.BlockSpec(memory_space=pl.ANY)],
        out_specs=[WHOLE] * 3,
        compiler_params=PARAMS,
        name="turned_weights",
    )(own_in, other_in, probe, w_out, order, token)


def hidden_grads(pair, w_out_t, slope, chunk):
    both = jnp.dot(
        pair[...].reshape(2 * ROWS, FEATURES), w_out_t[:, columns(chunk)], preferred_element_type=jnp.float32
    )
    grad_hidden, grad_hidden_t = both[:ROWS], both[ROWS:]
    slope_chunk = slope[0, :, columns(chunk)]
    grad_pre = grad_hidden * slope_chunk
    grad_pre_t = grad_hidden_t * slope_chunk + grad_hidden * slope[1, :, columns(chunk)]
    return grad_pre.astype(jnp.bfloat16), grad_pre_t.astype(jnp.bfloat16)


def norm_apply(values, normed, rscale):
    return rscale * (values - row_mean(values) - normed * row_mean(normed * values))


def backward_kernel(tick, *refs):
    section, pair, w_in_t, probe_t, w_out_t, norm, stat, slope = refs[:8]
    refs = refs[8:]
    if tick == CROSS_TICK:
        other_pair, pair_out, grads, acc, acc_t, whole = refs
    else:
        pair_out, grads, acc, acc_t = refs

    @pl.when(section[0] == LAYERS - 1 - tick)
    def _():
        adjoint = pair
        if tick == CROSS_TICK:
            adjoint = whole
            whole[...] = (pair[...].astype(jnp.float32) + other_pair[...].astype(jnp.float32)).astype(jnp.bfloat16)
        acc[...] = jnp.zeros_like(acc)
        acc_t[...] = jnp.zeros_like(acc_t)

        def step(chunk, carry):
            low_grad, low_grad_t = hidden_grads(adjoint, w_out_t, slope, chunk)
            both = jnp.concatenate([low_grad_t, low_grad], axis=0)
            grads[:, columns(chunk)] = both
            acc[...] += jnp.dot(both, w_in_t[columns(chunk), :], preferred_element_type=jnp.float32)
            acc_t[...] += jnp.dot(low_grad, probe_t[columns(chunk), :], preferred_element_type=jnp.float32)
            return carry

        lax.fori_loop(0, CHUNKS, step, 0, unroll=UNROLL_DOWN)
        normed, normed_t = norm[0], norm[1]
        rscale, tangent_dot = stat[0][:, :1], stat[1][:, :1]
        grad_norm = acc[ROWS:]
        grad_norm_t = acc[:ROWS] + acc_t[...]
        through = norm_apply(grad_norm, normed, rscale)
        through_t = (
            norm_apply(grad_norm_t, normed, rscale)
            - rscale * tangent_dot * through
            - rscale * (normed_t * row_mean(normed * grad_norm) + normed * row_mean(normed_t * grad_norm))
        )
        pair_out[0] = (adjoint[0].astype(jnp.float32) + through).astype(jnp.bfloat16)
        pair_out[1] = (adjoint[1].astype(jnp.float32) + through_t).astype(jnp.bfloat16)


def backward_call(tick, section, pairs, w_in_t, probe_t, w_out_t, kept):
    operands = [section, pairs[0], w_in_t, probe_t, w_out_t, *kept, *pairs[1:]]
    whole = [pltpu.VMEM(PAIR.shape, PAIR.dtype)] if tick == CROSS_TICK else []
    return pl.pallas_call(
        functools.partial(backward_kernel, tick),
        out_shape=[PAIR, GRADS],
        in_specs=[SMEM] + [WHOLE] * (len(operands) - 1),
        out_specs=[WHOLE] * 2,
        scratch_shapes=[
            pltpu.VMEM((2 * ROWS, FEATURES), jnp.float32),
            pltpu.VMEM((ROWS, FEATURES), jnp.float32),
            *whole,
        ],
        compiler_params=PARAMS,
        name=f"layer_down_{tick}",
    )(*operands)


OWN_HALF = slice(0, FEATURES // 2)
OTHER_HALF = slice(FEATURES // 2, FEATURES)


def curvature_operands(micro, section, pair, w_out_t, slope, order, opening_n, norms, grads, lhs, rhs):
    @pl.when(section[0] == 0)
    def _():
        rows = slice(micro * ROWS, (micro + 1) * ROWS)
        lhs[:ROWS] = jnp.dot(opening_n[rows], order[...], preferred_element_type=jnp.float32).astype(jnp.bfloat16)
        lhs[ROWS:] = jnp.zeros((ROWS, FEATURES), jnp.bfloat16)

        def bottom(chunk, carry):
            low_grad, low_grad_t = hidden_grads(pair, w_out_t, slope, chunk)
            rhs[:, columns(chunk)] = jnp.concatenate([low_grad_t, low_grad], axis=0)
            return carry

        lax.fori_loop(0, CHUNKS, bottom, 0, unroll=UNROLL_LAST)

    for layer in range(1, LAYERS):

        @pl.when(section[0] == layer)
        def _():
            both = norms[layer - 1][...].reshape(2 * ROWS, FEATURES).astype(jnp.bfloat16)
            lhs[...] = jnp.dot(both, order[...], preferred_element_type=jnp.float32).astype(jnp.bfloat16)
            rhs[...] = grads[LAYERS - 1 - layer][...]


def curvature_kernel(micro, final, *refs):
    section, pair, w_out_t, slope, order, opening_n = refs[:6]
    norms, refs = refs[6 : 5 + LAYERS], refs[5 + LAYERS :]
    grads, refs = refs[: LAYERS - 1], refs[LAYERS - 1 :]
    if final:
        away_in, stay_in, refs = refs[0], refs[1], refs[2:]
    away, stay, lhs, rhs = refs
    curvature_operands(micro, section, pair, w_out_t, slope, order, opening_n, norms, grads, lhs, rhs)

    def step(chunk, carry):
        now = columns(chunk)

        def product(half):
            return lax.dot_general(lhs[:, half], rhs[:, now], CONTRACT_FIRST, preferred_element_type=jnp.float32)

        if final:
            away[:, now] = (away_in[:, now] + product(OTHER_HALF)).astype(jnp.bfloat16)
            stay[:, now] = stay_in[:, now] + product(OWN_HALF)
        else:
            away[:, now] = product(OTHER_HALF)
            stay[:, now] = product(OWN_HALF)
        return carry

    lax.fori_loop(0, CHUNKS, step, 0, unroll=UNROLL_LAST)


def curvature_call(micro, section, pair, w_out_t, slope, order, opening_n, norms, grads, sums):
    half = (FEATURES // 2, HIDDEN)
    final = bool(sums)
    operands = [section, pair, w_out_t, slope, order, opening_n, *norms, *grads, *sums]
    return pl.pallas_call(
        functools.partial(curvature_kernel, micro, final),
        out_shape=[
            jax.ShapeDtypeStruct(half, jnp.bfloat16 if final else jnp.float32),
            jax.ShapeDtypeStruct(half, jnp.float32),
        ],
        in_specs=[SMEM] + [WHOLE] * (len(operands) - 1),
        out_specs=[WHOLE] * 2,
        scratch_shapes=[
            pltpu.VMEM((2 * ROWS, FEATURES), jnp.bfloat16),
            pltpu.VMEM((2 * ROWS, HIDDEN), jnp.bfloat16),
        ],
        compiler_params=PARAMS,
        name="curvature_last" if final else "curvature_first",
    )(*operands)


def shards(inputs, targets, w_in, w_out, probes):
    place = [jnp.reshape(lax.axis_index(name), (1,)).astype(jnp.int32) for name in (*DP, SECTION)]
    section = place[-1]
    in_block = settled_call(place, w_in[0])
    probe = probes[0]
    own_in, other_in = gathered(in_block, True)
    full_out = placed_call(place, *gathered(w_out[0], False))
    order, curvature_order, opening_n, opening_t = opening_call(place, inputs, probe)
    goal = routed(targets, goal_route)
    pairs, slopes, kept, grads = [None] * MICRO, [], [], []
    for micro in range(MICRO):
        kept.append([])
        grads.append([])
    for tick in range(LAYERS):
        for micro in range(MICRO):
            if tick == 0:
                pair, slope = first_call(
                    micro, section, inputs, opening_n, opening_t, order, own_in, other_in, full_out
                )
                slopes.append(slope)
            else:
                goal_now = goal[micro * ROWS : (micro + 1) * ROWS]
                pair, *stores = forward_call(
                    tick, section, pairs[micro], own_in, other_in, probe, full_out, order, goal_now
                )
                kept[micro].append(stores)
            if tick < LAYERS - 1:
                pairs[micro] = [routed(pair, up_across if tick + 1 == CROSS_TICK else up_from(tick))]
            else:
                pairs[micro] = [pair]
            if tick + 1 == CROSS_TICK:
                pairs[micro].append(routed(pairs[micro][0], up_relayed))
        if tick == TURN_TICK:
            turned = turned_call(own_in, other_in, probe, full_out, order, kept[-1][-1][0])
    for tick in range(LAYERS - 1):
        for micro in range(MICRO):
            pair, low_grads = backward_call(tick, section, pairs[micro], *turned, kept[micro][LAYERS - 2 - tick])
            grads[micro].append(low_grads)
            pairs[micro] = [routed(pair, down_across if tick + 1 == CROSS_TICK else down_from(LAYERS - 1 - tick))]
            if tick + 1 == CROSS_TICK:
                pairs[micro].append(routed(pairs[micro][0], down_relayed))
    sums = ()
    for micro in range(MICRO):
        norms = [stores[0] for stores in kept[micro]]
        sums = curvature_call(
            micro, section, pairs[micro][0], turned[2], slopes[micro], curvature_order, opening_n, norms, grads[micro], sums
        )
    away, stay = sums
    other = routed(away, swap_core)
    summed = (stay + other.astype(jnp.float32)).astype(jnp.bfloat16)
    summed = lax.all_to_all(summed.reshape(4, 64, HIDDEN), "y", 0, 0, tiled=True)
    summed = jnp.sum(summed.astype(jnp.float32), axis=0).astype(jnp.bfloat16)
    summed = lax.all_to_all(summed.reshape(8, 8, HIDDEN), ("b1", "b2", "b4"), 0, 0, tiled=True)
    summed = jnp.sum(summed.astype(jnp.float32), axis=0)
    probe_own = lax.dynamic_slice_in_dim(probe, lax.axis_index(DP) * 8, 8, 0)
    return (probe_own.astype(jnp.float32) * summed)[None]


def solution(mesh):
    fine = Mesh(mesh.devices.reshape(SIZES), NAMES)
    return jax.shard_map(
        shards,
        mesh=fine,
        in_specs=(
            P(DP, None),
            P(DP, None),
            P(SECTION, DP, None),
            P(SECTION, DP, None),
            P(SECTION, None, None),
        ),
        out_specs=P(SECTION, DP, None),
        check_vma=False,
    )
```

```python
import functools
import itertools

import jax
import jax.numpy as jnp
from jax import lax
from jax.experimental import pallas as pl
from jax.experimental.pallas import tpu as pltpu
from jax.sharding import Mesh, PartitionSpec as P

EPSILON = 1e-05
SQRT_HALF = 0.7071067811865476
INV_ROOT_TWO_PI = 0.3989422804014327
CONTRACT_FIRST = (((0,), (0,)), ((), ()))

NAMES = ("zh", "x", "b4", "b2", "b1", "y", "c")
SIZES = (2, 4, 2, 2, 2, 4, 2)
SECTION = ("zh", "x")
DP = ("b4", "b2", "b1", "y", "c")
PLACES = 6
LAYERS = 8
FEATURES = 512
HIDDEN = 2048
MICRO = 2
ROWS = 128 // MICRO
UNROLL_UP = 1
UNROLL_DOWN = 2
UNROLL_LAST = 2
TURN_TICK = 3
CROSS_TICK = 4
TOKENS = 8192
CHUNK = 1024
CHUNKS = HIDDEN // CHUNK
VMEM_BYTES = 4 * 1024 * 1024
WHOLE = pl.BlockSpec(memory_space=pltpu.VMEM)
SMEM = pl.BlockSpec(memory_space=pltpu.SMEM)


def flat(place):
    index = 0
    for size, at in zip(SIZES, place):
        index = index * size + at
    return index


def routed(value, route):
    pairs = []
    for place in itertools.product(*(range(size) for size in SIZES)):
        there = route(*place)
        if there is not None:
            pairs.append((flat(place), flat(there)))
    return lax.ppermute(value, NAMES, pairs)


def swap_b4(zh, x, b4, b2, b1, y, c):
    return (zh, x, 1 - b4, b2, b1, y, c)


def goal_route(zh, x, b4, b2, b1, y, c):
    return (zh, x, 1 - b4, 1 - b2, 1 - b1, y, c) if (zh, x) == (1, 3) else None


def swap_b2(zh, x, b4, b2, b1, y, c):
    return (zh, x, b4, 1 - b2, b1, y, c)


def swap_b1(zh, x, b4, b2, b1, y, c):
    return (zh, x, b4, b2, 1 - b1, y, c)


def swap_even(zh, x, b4, b2, b1, y, c):
    return (zh, x, b4, b2, b1, y ^ 1, c)


def swap_odd(zh, x, b4, b2, b1, y, c):
    return (zh, x, b4, b2, b1, y ^ 3, c)


def swap_core(zh, x, b4, b2, b1, y, c):
    return (zh, x, b4, b2, b1, y, 1 - c)


def up_from(section):
    def route(zh, x, b4, b2, b1, y, c):
        return (zh, x + 1, b4, b2, b1, y, c) if x == section % 4 else None

    return route


def down_from(section):
    def route(zh, x, b4, b2, b1, y, c):
        return (zh, x - 1, b4, b2, b1, y, c) if x == section % 4 else None

    return route


def up_across(zh, x, b4, b2, b1, y, c):
    if (zh, x) != (0, 3):
        return None
    return (0, 0, b4, b2, b1, y, 1) if c else (1, 0, 1 - b4, 1 - b2, 1 - b1, y, 0)


def up_relayed(zh, x, b4, b2, b1, y, c):
    return (1, 0, 1 - b4, 1 - b2, 1 - b1, y, 1) if (zh, x, c) == (0, 0, 1) else None


def down_across(zh, x, b4, b2, b1, y, c):
    if (zh, x) != (1, 0):
        return None
    return (1, 3, b4, b2, b1, y, 1) if c else (0, 3, 1 - b4, 1 - b2, 1 - b1, y, 0)


def down_relayed(zh, x, b4, b2, b1, y, c):
    return (0, 3, 1 - b4, 1 - b2, 1 - b1, y, 1) if (zh, x, c) == (1, 3, 1) else None


def doubled(block, route):
    return jnp.concatenate([block, routed(block, route)], axis=0)


def gathered(block, even_first):
    for route in (swap_b4, swap_b2, swap_b1) + ((swap_even, swap_odd) if even_first else (swap_odd, swap_even)):
        block = doubled(block, route)
    return block, routed(block, swap_core)


def natural_block(place, b4, b2, b1, y, c):
    z = (b4 ^ place[0][0]) * 4 + (b2 ^ place[1][0]) * 2 + (b1 ^ place[2][0])
    return z * 8 + (y ^ place[3][0]) * 2 + (c ^ place[4][0])


def settled_kernel(*refs):
    block_in, block = refs[PLACES:]
    block[...] = block_in[...]


def settled_call(place, block):
    return pl.pallas_call(
        settled_kernel,
        out_shape=jax.ShapeDtypeStruct(block.shape, block.dtype),
        in_specs=[SMEM] * PLACES + [WHOLE],
        out_specs=WHOLE,
        compiler_params=PARAMS,
        name="settled",
    )(*place, block)


def placed_kernel(*refs):
    place = refs[:PLACES]
    own_out, other_out, full_out = refs[PLACES:]
    rows = HIDDEN // 64
    for core, half in enumerate((own_out, other_out)):
        for index in range(32):
            odd, even = index // 8 % 2, index // 16
            there = natural_block(place, index % 2, index // 2 % 2, index // 4 % 2, even ^ (odd * 3), core)
            full_out[pl.ds(pl.multiple_of(there * rows, rows), rows), :] = half[index * rows : (index + 1) * rows, :]


def placed_call(place, own_out, other_out):
    return pl.pallas_call(
        placed_kernel,
        out_shape=jax.ShapeDtypeStruct((HIDDEN, FEATURES), jnp.bfloat16),
        in_specs=[SMEM] * PLACES + [WHOLE] * 2,
        out_specs=WHOLE,
        compiler_params=PARAMS,
        name="placed_w_out",
    )(*place, own_out, other_out)


def row_mean(values):
    return jnp.mean(values, axis=-1, keepdims=True)


def columns(chunk):
    return pl.ds(pl.multiple_of(chunk * CHUNK, CHUNK), CHUNK)


def one_hot(natural_row):
    natural = lax.broadcasted_iota(jnp.int32, (FEATURES, FEATURES), 0)
    return jnp.where(natural == natural_row, 1.0, 0.0).astype(jnp.bfloat16)


def opening_kernel(*refs):
    place = refs[:PLACES]
    inputs, probe, order, curvature_order, normed_out, preact_t = refs[PLACES:]
    at = lax.broadcasted_iota(jnp.int32, (FEATURES, FEATURES), 1)
    row, b4, b2, b1 = at % 8, (at // 8) % 2, (at // 16) % 2, (at // 32) % 2
    even, odd, core = (at // 64) % 2, (at // 128) % 2, at // 256
    order[...] = one_hot(natural_block(place, b4, b2, b1, even ^ (odd * 3), core) * 8 + row)
    block = (b4 * 4 + b2 * 2 + b1) * 8 + ((at // 64) % 4) * 2 + (core ^ place[4][0])
    curvature_order[...] = one_hot(block * 8 + row)
    inflow = inputs[...].astype(jnp.float32)
    centred = inflow - row_mean(inflow)
    normed = (centred * lax.rsqrt(row_mean(centred * centred) + EPSILON)).astype(jnp.bfloat16)
    normed_out[...] = normed

    def step(chunk, carry):
        preact_t[:, columns(chunk)] = jnp.dot(normed, probe[:, columns(chunk)], preferred_element_type=jnp.float32)
        return carry

    lax.fori_loop(0, CHUNKS, step, 0)


def opening_call(place, inputs, probe):
    rows = inputs.shape[0]
    order = jax.ShapeDtypeStruct((FEATURES, FEATURES), jnp.bfloat16)
    return pl.pallas_call(
        opening_kernel,
        out_shape=[
            order,
            order,
            jax.ShapeDtypeStruct((rows, FEATURES), jnp.bfloat16),
            jax.ShapeDtypeStruct((rows, HIDDEN), jnp.float32),
        ],
        in_specs=[SMEM] * PLACES + [WHOLE] * 2,
        out_specs=[WHOLE] * 4,
        compiler_params=PARAMS,
        name="opening",
    )(*place, inputs, probe)


def gelu_slopes(preact, preact_t, slope_out, chunk):
    normal_cdf = 0.5 * (1.0 + lax.erf(preact * SQRT_HALF))
    density = INV_ROOT_TWO_PI * jnp.exp(-0.5 * preact * preact)
    slope = normal_cdf + preact * density
    slope_out[0, :, columns(chunk)] = slope
    slope_out[1, :, columns(chunk)] = density * (2.0 - preact * preact) * preact_t
    return jnp.concatenate([preact * normal_cdf, slope * preact_t], axis=0).astype(jnp.bfloat16)


def halves_product(lhs, own_in, other_in, now):
    return jnp.dot(lhs[:, OWN_HALF], own_in[:, now], preferred_element_type=jnp.float32) + jnp.dot(
        lhs[:, OTHER_HALF], other_in[:, now], preferred_element_type=jnp.float32
    )


def first_kernel(micro, section, inputs, opening_n, opening_t, order, own_in, other_in, w_out, pair_out, slope_out, lhs, acc):
    rows = slice(micro * ROWS, (micro + 1) * ROWS)

    @pl.when(section[0] == 0)
    def _():
        lhs[...] = jnp.dot(opening_n[rows], order[...], preferred_element_type=jnp.float32).astype(jnp.bfloat16)
        acc[:ROWS] = inputs[rows].astype(jnp.float32)
        acc[ROWS:] = jnp.zeros((ROWS, FEATURES), jnp.float32)

        def step(chunk, carry):
            preact = halves_product(lhs[...], own_in, other_in, columns(chunk))
            hidden = gelu_slopes(preact, opening_t[rows, columns(chunk)], slope_out, chunk)
            acc[...] += jnp.dot(hidden, w_out[columns(chunk), :], preferred_element_type=jnp.float32)
            return carry

        lax.fori_loop(0, CHUNKS, step, 0, unroll=UNROLL_LAST)
        pair_out[0] = acc[:ROWS].astype(jnp.bfloat16)
        pair_out[1] = acc[ROWS:].astype(jnp.bfloat16)


def forward_kernel(tick, *refs):
    last = tick == LAYERS - 1
    section, own_in, other_in, probe, w_out, order = refs[:6]
    pairs, refs = (refs[6:8], refs[8:]) if tick == CROSS_TICK else (refs[6:7], refs[7:])
    if last:
        goal, refs = refs[0], refs[1:]
    pair_out, norm, stat, slope_out, natural, lhs, acc = refs

    @pl.when(section[0] == tick)
    def _():
        inflow = sum(pair[0].astype(jnp.float32) for pair in pairs)
        inflow_t = sum(pair[1].astype(jnp.float32) for pair in pairs)
        centred = inflow - row_mean(inflow)
        rscale = lax.rsqrt(row_mean(centred * centred) + EPSILON)
        normed = centred * rscale
        tangent_dot = row_mean(normed * inflow_t)
        normed_t = rscale * (inflow_t - row_mean(inflow_t) - normed * tangent_dot)
        norm[0] = normed
        norm[1] = normed_t
        stat[0] = jnp.broadcast_to(rscale, (ROWS, 128))
        stat[1] = jnp.broadcast_to(tangent_dot, (ROWS, 128))
        acc[:ROWS] = inflow
        acc[ROWS:] = inflow_t
        natural[:ROWS] = normed.astype(jnp.bfloat16)
        natural[ROWS:] = normed_t.astype(jnp.bfloat16)
        lhs[...] = jnp.dot(natural[...], order[...], preferred_element_type=jnp.float32).astype(jnp.bfloat16)

        def step(chunk, carry):
            both = halves_product(lhs[...], own_in, other_in, columns(chunk))
            preact_t = both[ROWS:] + jnp.dot(
                natural[:ROWS], probe[:, columns(chunk)], preferred_element_type=jnp.float32
            )
            hidden = gelu_slopes(both[:ROWS], preact_t, slope_out, chunk)
            acc[...] += jnp.dot(hidden, w_out[columns(chunk), :], preferred_element_type=jnp.float32)
            return carry

        lax.fori_loop(0, CHUNKS, step, 0, unroll=UNROLL_UP)
        if last:
            pair_out[0] = ((acc[:ROWS] - goal[...].astype(jnp.float32)) / TOKENS).astype(jnp.bfloat16)
            pair_out[1] = (acc[ROWS:] / TOKENS).astype(jnp.bfloat16)
        else:
            pair_out[0] = acc[:ROWS].astype(jnp.bfloat16)
            pair_out[1] = acc[ROWS:].astype(jnp.bfloat16)


NORM = jax.ShapeDtypeStruct((2, ROWS, FEATURES), jnp.float32)
STAT = jax.ShapeDtypeStruct((2, ROWS, 128), jnp.float32)
SLOPE = jax.ShapeDtypeStruct((2, ROWS, HIDDEN), jnp.float32)
PAIR = jax.ShapeDtypeStruct((2, ROWS, FEATURES), jnp.bfloat16)
GRADS = jax.ShapeDtypeStruct((2 * ROWS, HIDDEN), jnp.bfloat16)
PARAMS = pltpu.CompilerParams(vmem_limit_bytes=VMEM_BYTES)


def first_call(micro, section, inputs, opening_n, opening_t, order, own_in, other_in, w_out):
    return pl.pallas_call(
        functools.partial(first_kernel, micro),
        out_shape=[PAIR, SLOPE],
        in_specs=[SMEM] + [WHOLE] * 7,
        out_specs=[WHOLE] * 2,
        scratch_shapes=[
            pltpu.VMEM((ROWS, FEATURES), jnp.bfloat16),
            pltpu.VMEM((2 * ROWS, FEATURES), jnp.float32),
        ],
        compiler_params=PARAMS,
        name="layer_up_0",
    )(section, inputs, opening_n, opening_t, order, own_in, other_in, w_out)


def forward_call(tick, section, pairs, own_in, other_in, probe, w_out, order, goal):
    operands = [section, own_in, other_in, probe, w_out, order, *pairs] + ([goal] if tick == LAYERS - 1 else [])
    return pl.pallas_call(
        functools.partial(forward_kernel, tick),
        out_shape=[PAIR, NORM, STAT, SLOPE],
        in_specs=[SMEM] + [WHOLE] * (len(operands) - 1),
        out_specs=[WHOLE] * 4,
        scratch_shapes=[
            pltpu.VMEM((2 * ROWS, FEATURES), jnp.bfloat16),
            pltpu.VMEM((2 * ROWS, FEATURES), jnp.bfloat16),
            pltpu.VMEM((2 * ROWS, FEATURES), jnp.float32),
        ],
        compiler_params=PARAMS,
        name=f"layer_up_{tick}",
    )(*operands)


def turned_kernel(own_in, other_in, probe, w_out, order, token, w_in_t, probe_t, w_out_t):
    by_place = (((0,), (1,)), ((), ()))

    def step(index, carry):
        now = pl.ds(pl.multiple_of(index * FEATURES, FEATURES), FEATURES)
        own = lax.dot_general(own_in[:, now], order[:, OWN_HALF], by_place, preferred_element_type=jnp.float32)
        other = lax.dot_general(other_in[:, now], order[:, OTHER_HALF], by_place, preferred_element_type=jnp.float32)
        w_in_t[now, :] = (own + other).astype(jnp.bfloat16)
        probe_t[now, :] = probe[:, now].T
        w_out_t[:, now] = w_out[now, :].T
        return carry

    lax.fori_loop(0, HIDDEN // FEATURES, step, 0)


def turned_call(own_in, other_in, probe, w_out, order, token):
    tall = jax.ShapeDtypeStruct((HIDDEN, FEATURES), jnp.bfloat16)
    wide = jax.ShapeDtypeStruct((FEATURES, HIDDEN), jnp.bfloat16)
    return pl.pallas_call(
        turned_kernel,
        out_shape=[tall, tall, wide],
        in_specs=[WHOLE] * 5 + [pl.BlockSpec(memory_space=pl.ANY)],
        out_specs=[WHOLE] * 3,
        compiler_params=PARAMS,
        name="turned_weights",
    )(own_in, other_in, probe, w_out, order, token)


def hidden_grads(pair, w_out_t, slope, chunk):
    both = jnp.dot(
        pair[...].reshape(2 * ROWS, FEATURES), w_out_t[:, columns(chunk)], preferred_element_type=jnp.float32
    )
    grad_hidden, grad_hidden_t = both[:ROWS], both[ROWS:]
    slope_chunk = slope[0, :, columns(chunk)]
    grad_pre = grad_hidden * slope_chunk
    grad_pre_t = grad_hidden_t * slope_chunk + grad_hidden * slope[1, :, columns(chunk)]
    return grad_pre.astype(jnp.bfloat16), grad_pre_t.astype(jnp.bfloat16)


def norm_apply(values, normed, rscale):
    return rscale * (values - row_mean(values) - normed * row_mean(normed * values))


def backward_kernel(tick, *refs):
    section, pair, w_in_t, probe_t, w_out_t, norm, stat, slope = refs[:8]
    refs = refs[8:]
    if tick == CROSS_TICK:
        other_pair, pair_out, grads, acc, acc_t, whole = refs
    else:
        pair_out, grads, acc, acc_t = refs

    @pl.when(section[0] == LAYERS - 1 - tick)
    def _():
        adjoint = pair
        if tick == CROSS_TICK:
            adjoint = whole
            whole[...] = (pair[...].astype(jnp.float32) + other_pair[...].astype(jnp.float32)).astype(jnp.bfloat16)
        acc[...] = jnp.zeros_like(acc)
        acc_t[...] = jnp.zeros_like(acc_t)

        def step(chunk, carry):
            low_grad, low_grad_t = hidden_grads(adjoint, w_out_t, slope, chunk)
            both = jnp.concatenate([low_grad_t, low_grad], axis=0)
            grads[:, columns(chunk)] = both
            acc[...] += jnp.dot(both, w_in_t[columns(chunk), :], preferred_element_type=jnp.float32)
            acc_t[...] += jnp.dot(low_grad, probe_t[columns(chunk), :], preferred_element_type=jnp.float32)
            return carry

        lax.fori_loop(0, CHUNKS, step, 0, unroll=UNROLL_DOWN)
        normed, normed_t = norm[0], norm[1]
        rscale, tangent_dot = stat[0][:, :1], stat[1][:, :1]
        grad_norm = acc[ROWS:]
        grad_norm_t = acc[:ROWS] + acc_t[...]
        through = norm_apply(grad_norm, normed, rscale)
        through_t = (
            norm_apply(grad_norm_t, normed, rscale)
            - rscale * tangent_dot * through
            - rscale * (normed_t * row_mean(normed * grad_norm) + normed * row_mean(normed_t * grad_norm))
        )
        pair_out[0] = (adjoint[0].astype(jnp.float32) + through).astype(jnp.bfloat16)
        pair_out[1] = (adjoint[1].astype(jnp.float32) + through_t).astype(jnp.bfloat16)


def backward_call(tick, section, pairs, w_in_t, probe_t, w_out_t, kept):
    operands = [section, pairs[0], w_in_t, probe_t, w_out_t, *kept, *pairs[1:]]
    whole = [pltpu.VMEM(PAIR.shape, PAIR.dtype)] if tick == CROSS_TICK else []
    return pl.pallas_call(
        functools.partial(backward_kernel, tick),
        out_shape=[PAIR, GRADS],
        in_specs=[SMEM] + [WHOLE] * (len(operands) - 1),
        out_specs=[WHOLE] * 2,
        scratch_shapes=[
            pltpu.VMEM((2 * ROWS, FEATURES), jnp.float32),
            pltpu.VMEM((ROWS, FEATURES), jnp.float32),
            *whole,
        ],
        compiler_params=PARAMS,
        name=f"layer_down_{tick}",
    )(*operands)


OWN_HALF = slice(0, FEATURES // 2)
OTHER_HALF = slice(FEATURES // 2, FEATURES)


def curvature_operands(micro, section, pair, w_out_t, slope, order, opening_n, norms, grads, lhs, rhs):
    @pl.when(section[0] == 0)
    def _():
        rows = slice(micro * ROWS, (micro + 1) * ROWS)
        lhs[:ROWS] = jnp.dot(opening_n[rows], order[...], preferred_element_type=jnp.float32).astype(jnp.bfloat16)
        lhs[ROWS:] = jnp.zeros((ROWS, FEATURES), jnp.bfloat16)

        def bottom(chunk, carry):
            low_grad, low_grad_t = hidden_grads(pair, w_out_t, slope, chunk)
            rhs[:, columns(chunk)] = jnp.concatenate([low_grad_t, low_grad], axis=0)
            return carry

        lax.fori_loop(0, CHUNKS, bottom, 0, unroll=UNROLL_LAST)

    for layer in range(1, LAYERS):

        @pl.when(section[0] == layer)
        def _():
            both = norms[layer - 1][...].reshape(2 * ROWS, FEATURES).astype(jnp.bfloat16)
            lhs[...] = jnp.dot(both, order[...], preferred_element_type=jnp.float32).astype(jnp.bfloat16)
            rhs[...] = grads[LAYERS - 1 - layer][...]


def curvature_kernel(micro, final, *refs):
    section, pair, w_out_t, slope, order, opening_n = refs[:6]
    norms, refs = refs[6 : 5 + LAYERS], refs[5 + LAYERS :]
    grads, refs = refs[: LAYERS - 1], refs[LAYERS - 1 :]
    if final:
        away_in, stay_in, refs = refs[0], refs[1], refs[2:]
    away, stay, lhs, rhs = refs
    curvature_operands(micro, section, pair, w_out_t, slope, order, opening_n, norms, grads, lhs, rhs)

    def step(chunk, carry):
        now = columns(chunk)

        def product(half):
            return lax.dot_general(lhs[:, half], rhs[:, now], CONTRACT_FIRST, preferred_element_type=jnp.float32)

        if final:
            away[:, now] = (away_in[:, now] + product(OTHER_HALF)).astype(jnp.bfloat16)
            stay[:, now] = stay_in[:, now] + product(OWN_HALF)
        else:
            away[:, now] = product(OTHER_HALF)
            stay[:, now] = product(OWN_HALF)
        return carry

    lax.fori_loop(0, CHUNKS, step, 0, unroll=UNROLL_LAST)


def curvature_call(micro, section, pair, w_out_t, slope, order, opening_n, norms, grads, sums):
    half = (FEATURES // 2, HIDDEN)
    final = bool(sums)
    operands = [section, pair, w_out_t, slope, order, opening_n, *norms, *grads, *sums]
    return pl.pallas_call(
        functools.partial(curvature_kernel, micro, final),
        out_shape=[
            jax.ShapeDtypeStruct(half, jnp.bfloat16 if final else jnp.float32),
            jax.ShapeDtypeStruct(half, jnp.float32),
        ],
        in_specs=[SMEM] + [WHOLE] * (len(operands) - 1),
        out_specs=[WHOLE] * 2,
        scratch_shapes=[
            pltpu.VMEM((2 * ROWS, FEATURES), jnp.bfloat16),
            pltpu.VMEM((2 * ROWS, HIDDEN), jnp.bfloat16),
        ],
        compiler_params=PARAMS,
        name="curvature_last" if final else "curvature_first",
    )(*operands)


def shards(inputs, targets, w_in, w_out, probes):
    place = [jnp.reshape(lax.axis_index(name), (1,)).astype(jnp.int32) for name in (*DP, SECTION)]
    section = place[-1]
    out_block = settled_call(place, w_out[0])
    probe = probes[0]
    own_in, other_in = gathered(w_in[0], True)
    full_out = placed_call(place, *gathered(out_block, False))
    order, curvature_order, opening_n, opening_t = opening_call(place, inputs, probe)
    goal = routed(targets, goal_route)
    pairs, slopes, kept, grads = [None] * MICRO, [], [], []
    for micro in range(MICRO):
        kept.append([])
        grads.append([])
    for tick in range(LAYERS):
        for micro in range(MICRO):
            if tick == 0:
                pair, slope = first_call(
                    micro, section, inputs, opening_n, opening_t, order, own_in, other_in, full_out
                )
                slopes.append(slope)
            else:
                goal_now = goal[micro * ROWS : (micro + 1) * ROWS]
                pair, *stores = forward_call(
                    tick, section, pairs[micro], own_in, other_in, probe, full_out, order, goal_now
                )
                kept[micro].append(stores)
            if tick < LAYERS - 1:
                pairs[micro] = [routed(pair, up_across if tick + 1 == CROSS_TICK else up_from(tick))]
            else:
                pairs[micro] = [pair]
            if tick + 1 == CROSS_TICK:
                pairs[micro].append(routed(pairs[micro][0], up_relayed))
        if tick == TURN_TICK:
            turned = turned_call(own_in, other_in, probe, full_out, order, kept[-1][-1][0])
    for tick in range(LAYERS - 1):
        for micro in range(MICRO):
            pair, low_grads = backward_call(tick, section, pairs[micro], *turned, kept[micro][LAYERS - 2 - tick])
            grads[micro].append(low_grads)
            pairs[micro] = [routed(pair, down_across if tick + 1 == CROSS_TICK else down_from(LAYERS - 1 - tick))]
            if tick + 1 == CROSS_TICK:
                pairs[micro].append(routed(pairs[micro][0], down_relayed))
    sums = ()
    for micro in range(MICRO):
        norms = [stores[0] for stores in kept[micro]]
        sums = curvature_call(
            micro, section, pairs[micro][0], turned[2], slopes[micro], curvature_order, opening_n, norms, grads[micro], sums
        )
    away, stay = sums
    other = routed(away, swap_core)
    summed = (stay + other.astype(jnp.float32)).astype(jnp.bfloat16)
    summed = lax.all_to_all(summed.reshape(4, 64, HIDDEN), "y", 0, 0, tiled=True)
    summed = jnp.sum(summed.astype(jnp.float32), axis=0).astype(jnp.bfloat16)
    summed = lax.all_to_all(summed.reshape(8, 8, HIDDEN), ("b1", "b2", "b4"), 0, 0, tiled=True)
    summed = jnp.sum(summed.astype(jnp.float32), axis=0)
    probe_own = lax.dynamic_slice_in_dim(probe, lax.axis_index(DP) * 8, 8, 0)
    return (probe_own.astype(jnp.float32) * summed)[None]


def solution(mesh):
    fine = Mesh(mesh.devices.reshape(SIZES), NAMES)
    return jax.shard_map(
        shards,
        mesh=fine,
        in_specs=(
            P(DP, None),
            P(DP, None),
            P(SECTION, DP, None),
            P(SECTION, DP, None),
            P(SECTION, None, None),
        ),
        out_specs=P(SECTION, DP, None),
        check_vma=False,
    )
```

```python
import functools
import itertools

import jax
import jax.numpy as jnp
from jax import lax
from jax.experimental import pallas as pl
from jax.experimental.pallas import tpu as pltpu
from jax.sharding import Mesh, PartitionSpec as P

EPSILON = 1e-05
SQRT_HALF = 0.7071067811865476
INV_ROOT_TWO_PI = 0.3989422804014327
CONTRACT_FIRST = (((0,), (0,)), ((), ()))

NAMES = ("zh", "x", "b4", "b2", "b1", "y", "c")
SIZES = (2, 4, 2, 2, 2, 4, 2)
SECTION = ("zh", "x")
DP = ("b4", "b2", "b1", "y", "c")
PLACES = 6
LAYERS = 8
FEATURES = 512
HIDDEN = 2048
MICRO = 2
ROWS = 128 // MICRO
UNROLL_UP = 1
UNROLL_DOWN = 2
UNROLL_LAST = 2
TURN_TICK = 3
CROSS_TICK = 4
TOKENS = 8192
CHUNK = 1024
CHUNKS = HIDDEN // CHUNK
VMEM_BYTES = 4 * 1024 * 1024
WHOLE = pl.BlockSpec(memory_space=pltpu.VMEM)
SMEM = pl.BlockSpec(memory_space=pltpu.SMEM)


def flat(place):
    index = 0
    for size, at in zip(SIZES, place):
        index = index * size + at
    return index


def routed(value, route):
    pairs = []
    for place in itertools.product(*(range(size) for size in SIZES)):
        there = route(*place)
        if there is not None:
            pairs.append((flat(place), flat(there)))
    return lax.ppermute(value, NAMES, pairs)


def swap_b4(zh, x, b4, b2, b1, y, c):
    return (zh, x, 1 - b4, b2, b1, y, c)


def goal_route(zh, x, b4, b2, b1, y, c):
    return (zh, x, 1 - b4, 1 - b2, 1 - b1, y, c) if (zh, x) == (1, 3) else None


def swap_b2(zh, x, b4, b2, b1, y, c):
    return (zh, x, b4, 1 - b2, b1, y, c)


def swap_b1(zh, x, b4, b2, b1, y, c):
    return (zh, x, b4, b2, 1 - b1, y, c)


def swap_even(zh, x, b4, b2, b1, y, c):
    return (zh, x, b4, b2, b1, y ^ 1, c)


def swap_odd(zh, x, b4, b2, b1, y, c):
    return (zh, x, b4, b2, b1, y ^ 3, c)


def swap_core(zh, x, b4, b2, b1, y, c):
    return (zh, x, b4, b2, b1, y, 1 - c)


def up_from(section):
    def route(zh, x, b4, b2, b1, y, c):
        return (zh, x + 1, b4, b2, b1, y, 1 - c) if x == section % 4 else None

    return route


def down_from(section):
    def route(zh, x, b4, b2, b1, y, c):
        return (zh, x - 1, b4, b2, b1, y, 1 - c) if x == section % 4 else None

    return route


def up_across(zh, x, b4, b2, b1, y, c):
    if (zh, x) != (0, 3):
        return None
    return (0, 0, b4, b2, b1, y, 1) if c else (1, 0, 1 - b4, 1 - b2, 1 - b1, y, 0)


def up_relayed(zh, x, b4, b2, b1, y, c):
    return (1, 0, 1 - b4, 1 - b2, 1 - b1, y, 1) if (zh, x, c) == (0, 0, 1) else None


def down_across(zh, x, b4, b2, b1, y, c):
    if (zh, x) != (1, 0):
        return None
    return (1, 3, b4, b2, b1, y, 1) if c else (0, 3, 1 - b4, 1 - b2, 1 - b1, y, 0)


def down_relayed(zh, x, b4, b2, b1, y, c):
    return (0, 3, 1 - b4, 1 - b2, 1 - b1, y, 1) if (zh, x, c) == (1, 3, 1) else None


def doubled(block, route):
    return jnp.concatenate([block, routed(block, route)], axis=0)


def gathered(block, even_first):
    for route in (swap_b4, swap_b2, swap_b1) + ((swap_even, swap_odd) if even_first else (swap_odd, swap_even)):
        block = doubled(block, route)
    return block, routed(block, swap_core)


def natural_block(place, b4, b2, b1, y, c):
    z = (b4 ^ place[0][0]) * 4 + (b2 ^ place[1][0]) * 2 + (b1 ^ place[2][0])
    return z * 8 + (y ^ place[3][0]) * 2 + (c ^ place[4][0])


def settled_kernel(*refs):
    block_in, block = refs[PLACES:]
    block[...] = block_in[...]


def settled_call(place, block):
    return pl.pallas_call(
        settled_kernel,
        out_shape=jax.ShapeDtypeStruct(block.shape, block.dtype),
        in_specs=[SMEM] * PLACES + [WHOLE],
        out_specs=WHOLE,
        compiler_params=PARAMS,
        name="settled",
    )(*place, block)


def placed_kernel(*refs):
    place = refs[:PLACES]
    own_out, other_out, full_out = refs[PLACES:]
    rows = HIDDEN // 64
    for core, half in enumerate((own_out, other_out)):
        for index in range(32):
            odd, even = index // 8 % 2, index // 16
            there = natural_block(place, index % 2, index // 2 % 2, index // 4 % 2, even ^ (odd * 3), core)
            full_out[pl.ds(pl.multiple_of(there * rows, rows), rows), :] = half[index * rows : (index + 1) * rows, :]


def placed_call(place, own_out, other_out):
    return pl.pallas_call(
        placed_kernel,
        out_shape=jax.ShapeDtypeStruct((HIDDEN, FEATURES), jnp.bfloat16),
        in_specs=[SMEM] * PLACES + [WHOLE] * 2,
        out_specs=WHOLE,
        compiler_params=PARAMS,
        name="placed_w_out",
    )(*place, own_out, other_out)


def row_mean(values):
    return jnp.mean(values, axis=-1, keepdims=True)


def columns(chunk):
    return pl.ds(pl.multiple_of(chunk * CHUNK, CHUNK), CHUNK)


def one_hot(natural_row):
    natural = lax.broadcasted_iota(jnp.int32, (FEATURES, FEATURES), 0)
    return jnp.where(natural == natural_row, 1.0, 0.0).astype(jnp.bfloat16)


def opening_kernel(*refs):
    place = refs[:PLACES]
    inputs, probe, order, curvature_order, normed_out, preact_t = refs[PLACES:]
    at = lax.broadcasted_iota(jnp.int32, (FEATURES, FEATURES), 1)
    row, b4, b2, b1 = at % 8, (at // 8) % 2, (at // 16) % 2, (at // 32) % 2
    even, odd, core = (at // 64) % 2, (at // 128) % 2, at // 256
    order[...] = one_hot(natural_block(place, b4, b2, b1, even ^ (odd * 3), core) * 8 + row)
    block = (b4 * 4 + b2 * 2 + b1) * 8 + ((at // 64) % 4) * 2 + (core ^ place[4][0])
    curvature_order[...] = one_hot(block * 8 + row)
    inflow = inputs[...].astype(jnp.float32)
    centred = inflow - row_mean(inflow)
    normed = (centred * lax.rsqrt(row_mean(centred * centred) + EPSILON)).astype(jnp.bfloat16)
    normed_out[...] = normed

    def step(chunk, carry):
        preact_t[:, columns(chunk)] = jnp.dot(normed, probe[:, columns(chunk)], preferred_element_type=jnp.float32)
        return carry

    lax.fori_loop(0, CHUNKS, step, 0)


def opening_call(place, inputs, probe):
    rows = inputs.shape[0]
    order = jax.ShapeDtypeStruct((FEATURES, FEATURES), jnp.bfloat16)
    return pl.pallas_call(
        opening_kernel,
        out_shape=[
            order,
            order,
            jax.ShapeDtypeStruct((rows, FEATURES), jnp.bfloat16),
            jax.ShapeDtypeStruct((rows, HIDDEN), jnp.float32),
        ],
        in_specs=[SMEM] * PLACES + [WHOLE] * 2,
        out_specs=[WHOLE] * 4,
        compiler_params=PARAMS,
        name="opening",
    )(*place, inputs, probe)


def gelu_slopes(preact, preact_t, slope_out, chunk):
    normal_cdf = 0.5 * (1.0 + lax.erf(preact * SQRT_HALF))
    density = INV_ROOT_TWO_PI * jnp.exp(-0.5 * preact * preact)
    slope = normal_cdf + preact * density
    slope_out[0, :, columns(chunk)] = slope
    slope_out[1, :, columns(chunk)] = density * (2.0 - preact * preact) * preact_t
    return jnp.concatenate([preact * normal_cdf, slope * preact_t], axis=0).astype(jnp.bfloat16)


def halves_product(lhs, own_in, other_in, now):
    return jnp.dot(lhs[:, OWN_HALF], own_in[:, now], preferred_element_type=jnp.float32) + jnp.dot(
        lhs[:, OTHER_HALF], other_in[:, now], preferred_element_type=jnp.float32
    )


def first_kernel(micro, section, inputs, opening_n, opening_t, order, own_in, other_in, w_out, pair_out, slope_out, lhs, acc):
    rows = slice(micro * ROWS, (micro + 1) * ROWS)

    @pl.when(section[0] == 0)
    def _():
        lhs[...] = jnp.dot(opening_n[rows], order[...], preferred_element_type=jnp.float32).astype(jnp.bfloat16)
        acc[:ROWS] = inputs[rows].astype(jnp.float32)
        acc[ROWS:] = jnp.zeros((ROWS, FEATURES), jnp.float32)

        def step(chunk, carry):
            preact = halves_product(lhs[...], own_in, other_in, columns(chunk))
            hidden = gelu_slopes(preact, opening_t[rows, columns(chunk)], slope_out, chunk)
            acc[...] += jnp.dot(hidden, w_out[columns(chunk), :], preferred_element_type=jnp.float32)
            return carry

        lax.fori_loop(0, CHUNKS, step, 0, unroll=UNROLL_LAST)
        pair_out[0] = acc[:ROWS].astype(jnp.bfloat16)
        pair_out[1] = acc[ROWS:].astype(jnp.bfloat16)


def forward_kernel(tick, *refs):
    last = tick == LAYERS - 1
    section, own_in, other_in, probe, w_out, order = refs[:6]
    pairs, refs = (refs[6:8], refs[8:]) if tick == CROSS_TICK else (refs[6:7], refs[7:])
    if last:
        goal, refs = refs[0], refs[1:]
    pair_out, norm, stat, slope_out, natural, lhs, acc = refs

    @pl.when(section[0] == tick)
    def _():
        inflow = sum(pair[0].astype(jnp.float32) for pair in pairs)
        inflow_t = sum(pair[1].astype(jnp.float32) for pair in pairs)
        centred = inflow - row_mean(inflow)
        rscale = lax.rsqrt(row_mean(centred * centred) + EPSILON)
        normed = centred * rscale
        tangent_dot = row_mean(normed * inflow_t)
        normed_t = rscale * (inflow_t - row_mean(inflow_t) - normed * tangent_dot)
        norm[0] = normed
        norm[1] = normed_t
        stat[0] = jnp.broadcast_to(rscale, (ROWS, 128))
        stat[1] = jnp.broadcast_to(tangent_dot, (ROWS, 128))
        acc[:ROWS] = inflow
        acc[ROWS:] = inflow_t
        natural[:ROWS] = normed.astype(jnp.bfloat16)
        natural[ROWS:] = normed_t.astype(jnp.bfloat16)
        lhs[...] = jnp.dot(natural[...], order[...], preferred_element_type=jnp.float32).astype(jnp.bfloat16)

        def step(chunk, carry):
            both = halves_product(lhs[...], own_in, other_in, columns(chunk))
            preact_t = both[ROWS:] + jnp.dot(
                natural[:ROWS], probe[:, columns(chunk)], preferred_element_type=jnp.float32
            )
            hidden = gelu_slopes(both[:ROWS], preact_t, slope_out, chunk)
            acc[...] += jnp.dot(hidden, w_out[columns(chunk), :], preferred_element_type=jnp.float32)
            return carry

        lax.fori_loop(0, CHUNKS, step, 0, unroll=UNROLL_UP)
        if last:
            pair_out[0] = ((acc[:ROWS] - goal[...].astype(jnp.float32)) / TOKENS).astype(jnp.bfloat16)
            pair_out[1] = (acc[ROWS:] / TOKENS).astype(jnp.bfloat16)
        else:
            pair_out[0] = acc[:ROWS].astype(jnp.bfloat16)
            pair_out[1] = acc[ROWS:].astype(jnp.bfloat16)


NORM = jax.ShapeDtypeStruct((2, ROWS, FEATURES), jnp.float32)
STAT = jax.ShapeDtypeStruct((2, ROWS, 128), jnp.float32)
SLOPE = jax.ShapeDtypeStruct((2, ROWS, HIDDEN), jnp.float32)
PAIR = jax.ShapeDtypeStruct((2, ROWS, FEATURES), jnp.bfloat16)
GRADS = jax.ShapeDtypeStruct((2 * ROWS, HIDDEN), jnp.bfloat16)
PARAMS = pltpu.CompilerParams(vmem_limit_bytes=VMEM_BYTES)


def first_call(micro, section, inputs, opening_n, opening_t, order, own_in, other_in, w_out):
    return pl.pallas_call(
        functools.partial(first_kernel, micro),
        out_shape=[PAIR, SLOPE],
        in_specs=[SMEM] + [WHOLE] * 7,
        out_specs=[WHOLE] * 2,
        scratch_shapes=[
            pltpu.VMEM((ROWS, FEATURES), jnp.bfloat16),
            pltpu.VMEM((2 * ROWS, FEATURES), jnp.float32),
        ],
        compiler_params=PARAMS,
        name="layer_up_0",
    )(section, inputs, opening_n, opening_t, order, own_in, other_in, w_out)


def forward_call(tick, section, pairs, own_in, other_in, probe, w_out, order, goal):
    operands = [section, own_in, other_in, probe, w_out, order, *pairs] + ([goal] if tick == LAYERS - 1 else [])
    return pl.pallas_call(
        functools.partial(forward_kernel, tick),
        out_shape=[PAIR, NORM, STAT, SLOPE],
        in_specs=[SMEM] + [WHOLE] * (len(operands) - 1),
        out_specs=[WHOLE] * 4,
        scratch_shapes=[
            pltpu.VMEM((2 * ROWS, FEATURES), jnp.bfloat16),
            pltpu.VMEM((2 * ROWS, FEATURES), jnp.bfloat16),
            pltpu.VMEM((2 * ROWS, FEATURES), jnp.float32),
        ],
        compiler_params=PARAMS,
        name=f"layer_up_{tick}",
    )(*operands)


def turned_kernel(own_in, other_in, probe, w_out, order, token, w_in_t, probe_t, w_out_t):
    by_place = (((0,), (1,)), ((), ()))

    def step(index, carry):
        now = pl.ds(pl.multiple_of(index * FEATURES, FEATURES), FEATURES)
        own = lax.dot_general(own_in[:, now], order[:, OWN_HALF], by_place, preferred_element_type=jnp.float32)
        other = lax.dot_general(other_in[:, now], order[:, OTHER_HALF], by_place, preferred_element_type=jnp.float32)
        w_in_t[now, :] = (own + other).astype(jnp.bfloat16)
        probe_t[now, :] = probe[:, now].T
        w_out_t[:, now] = w_out[now, :].T
        return carry

    lax.fori_loop(0, HIDDEN // FEATURES, step, 0)


def turned_call(own_in, other_in, probe, w_out, order, token):
    tall = jax.ShapeDtypeStruct((HIDDEN, FEATURES), jnp.bfloat16)
    wide = jax.ShapeDtypeStruct((FEATURES, HIDDEN), jnp.bfloat16)
    return pl.pallas_call(
        turned_kernel,
        out_shape=[tall, tall, wide],
        in_specs=[WHOLE] * 5 + [pl.BlockSpec(memory_space=pl.ANY)],
        out_specs=[WHOLE] * 3,
        compiler_params=PARAMS,
        name="turned_weights",
    )(own_in, other_in, probe, w_out, order, token)


def hidden_grads(pair, w_out_t, slope, chunk):
    both = jnp.dot(
        pair[...].reshape(2 * ROWS, FEATURES), w_out_t[:, columns(chunk)], preferred_element_type=jnp.float32
    )
    grad_hidden, grad_hidden_t = both[:ROWS], both[ROWS:]
    slope_chunk = slope[0, :, columns(chunk)]
    grad_pre = grad_hidden * slope_chunk
    grad_pre_t = grad_hidden_t * slope_chunk + grad_hidden * slope[1, :, columns(chunk)]
    return grad_pre.astype(jnp.bfloat16), grad_pre_t.astype(jnp.bfloat16)


def norm_apply(values, normed, rscale):
    return rscale * (values - row_mean(values) - normed * row_mean(normed * values))


def backward_kernel(tick, *refs):
    section, pair, w_in_t, probe_t, w_out_t, norm, stat, slope = refs[:8]
    refs = refs[8:]
    if tick == CROSS_TICK:
        other_pair, pair_out, grads, acc, acc_t, whole = refs
    else:
        pair_out, grads, acc, acc_t = refs

    @pl.when(section[0] == LAYERS - 1 - tick)
    def _():
        adjoint = pair
        if tick == CROSS_TICK:
            adjoint = whole
            whole[...] = (pair[...].astype(jnp.float32) + other_pair[...].astype(jnp.float32)).astype(jnp.bfloat16)
        acc[...] = jnp.zeros_like(acc)
        acc_t[...] = jnp.zeros_like(acc_t)

        def step(chunk, carry):
            low_grad, low_grad_t = hidden_grads(adjoint, w_out_t, slope, chunk)
            both = jnp.concatenate([low_grad_t, low_grad], axis=0)
            grads[:, columns(chunk)] = both
            acc[...] += jnp.dot(both, w_in_t[columns(chunk), :], preferred_element_type=jnp.float32)
            acc_t[...] += jnp.dot(low_grad, probe_t[columns(chunk), :], preferred_element_type=jnp.float32)
            return carry

        lax.fori_loop(0, CHUNKS, step, 0, unroll=UNROLL_DOWN)
        normed, normed_t = norm[0], norm[1]
        rscale, tangent_dot = stat[0][:, :1], stat[1][:, :1]
        grad_norm = acc[ROWS:]
        grad_norm_t = acc[:ROWS] + acc_t[...]
        through = norm_apply(grad_norm, normed, rscale)
        through_t = (
            norm_apply(grad_norm_t, normed, rscale)
            - rscale * tangent_dot * through
            - rscale * (normed_t * row_mean(normed * grad_norm) + normed * row_mean(normed_t * grad_norm))
        )
        pair_out[0] = (adjoint[0].astype(jnp.float32) + through).astype(jnp.bfloat16)
        pair_out[1] = (adjoint[1].astype(jnp.float32) + through_t).astype(jnp.bfloat16)


def backward_call(tick, section, pairs, w_in_t, probe_t, w_out_t, kept):
    operands = [section, pairs[0], w_in_t, probe_t, w_out_t, *kept, *pairs[1:]]
    whole = [pltpu.VMEM(PAIR.shape, PAIR.dtype)] if tick == CROSS_TICK else []
    return pl.pallas_call(
        functools.partial(backward_kernel, tick),
        out_shape=[PAIR, GRADS],
        in_specs=[SMEM] + [WHOLE] * (len(operands) - 1),
        out_specs=[WHOLE] * 2,
        scratch_shapes=[
            pltpu.VMEM((2 * ROWS, FEATURES), jnp.float32),
            pltpu.VMEM((ROWS, FEATURES), jnp.float32),
            *whole,
        ],
        compiler_params=PARAMS,
        name=f"layer_down_{tick}",
    )(*operands)


OWN_HALF = slice(0, FEATURES // 2)
OTHER_HALF = slice(FEATURES // 2, FEATURES)


def curvature_operands(micro, section, pair, w_out_t, slope, order, opening_n, norms, grads, lhs, rhs):
    @pl.when(section[0] == 0)
    def _():
        rows = slice(micro * ROWS, (micro + 1) * ROWS)
        lhs[:ROWS] = jnp.dot(opening_n[rows], order[...], preferred_element_type=jnp.float32).astype(jnp.bfloat16)
        lhs[ROWS:] = jnp.zeros((ROWS, FEATURES), jnp.bfloat16)

        def bottom(chunk, carry):
            low_grad, low_grad_t = hidden_grads(pair, w_out_t, slope, chunk)
            rhs[:, columns(chunk)] = jnp.concatenate([low_grad_t, low_grad], axis=0)
            return carry

        lax.fori_loop(0, CHUNKS, bottom, 0, unroll=UNROLL_LAST)

    for layer in range(1, LAYERS):

        @pl.when(section[0] == layer)
        def _():
            both = norms[layer - 1][...].reshape(2 * ROWS, FEATURES).astype(jnp.bfloat16)
            lhs[...] = jnp.dot(both, order[...], preferred_element_type=jnp.float32).astype(jnp.bfloat16)
            rhs[...] = grads[LAYERS - 1 - layer][...]


def curvature_kernel(micro, final, *refs):
    section, pair, w_out_t, slope, order, opening_n = refs[:6]
    norms, refs = refs[6 : 5 + LAYERS], refs[5 + LAYERS :]
    grads, refs = refs[: LAYERS - 1], refs[LAYERS - 1 :]
    if final:
        away_in, stay_in, refs = refs[0], refs[1], refs[2:]
    away, stay, lhs, rhs = refs
    curvature_operands(micro, section, pair, w_out_t, slope, order, opening_n, norms, grads, lhs, rhs)

    def step(chunk, carry):
        now = columns(chunk)

        def product(half):
            return lax.dot_general(lhs[:, half], rhs[:, now], CONTRACT_FIRST, preferred_element_type=jnp.float32)

        if final:
            away[:, now] = (away_in[:, now] + product(OTHER_HALF)).astype(jnp.bfloat16)
            stay[:, now] = stay_in[:, now] + product(OWN_HALF)
        else:
            away[:, now] = product(OTHER_HALF)
            stay[:, now] = product(OWN_HALF)
        return carry

    lax.fori_loop(0, CHUNKS, step, 0, unroll=UNROLL_LAST)


def curvature_call(micro, section, pair, w_out_t, slope, order, opening_n, norms, grads, sums):
    half = (FEATURES // 2, HIDDEN)
    final = bool(sums)
    operands = [section, pair, w_out_t, slope, order, opening_n, *norms, *grads, *sums]
    return pl.pallas_call(
        functools.partial(curvature_kernel, micro, final),
        out_shape=[
            jax.ShapeDtypeStruct(half, jnp.bfloat16 if final else jnp.float32),
            jax.ShapeDtypeStruct(half, jnp.float32),
        ],
        in_specs=[SMEM] + [WHOLE] * (len(operands) - 1),
        out_specs=[WHOLE] * 2,
        scratch_shapes=[
            pltpu.VMEM((2 * ROWS, FEATURES), jnp.bfloat16),
            pltpu.VMEM((2 * ROWS, HIDDEN), jnp.bfloat16),
        ],
        compiler_params=PARAMS,
        name="curvature_last" if final else "curvature_first",
    )(*operands)


def shards(inputs, targets, w_in, w_out, probes):
    place = [jnp.reshape(lax.axis_index(name), (1,)).astype(jnp.int32) for name in (*DP, SECTION)]
    section = place[-1]
    out_block = settled_call(place, w_out[0])
    probe = probes[0]
    own_in, other_in = gathered(w_in[0], True)
    full_out = placed_call(place, *gathered(out_block, False))
    order, curvature_order, opening_n, opening_t = opening_call(place, inputs, probe)
    goal = routed(targets, goal_route)
    pairs, slopes, kept, grads = [None] * MICRO, [], [], []
    for micro in range(MICRO):
        kept.append([])
        grads.append([])
    for tick in range(LAYERS):
        for micro in range(MICRO):
            if tick == 0:
                pair, slope = first_call(
                    micro, section, inputs, opening_n, opening_t, order, own_in, other_in, full_out
                )
                slopes.append(slope)
            else:
                goal_now = goal[micro * ROWS : (micro + 1) * ROWS]
                pair, *stores = forward_call(
                    tick, section, pairs[micro], own_in, other_in, probe, full_out, order, goal_now
                )
                kept[micro].append(stores)
            if tick < LAYERS - 1:
                pairs[micro] = [routed(pair, up_across if tick + 1 == CROSS_TICK else up_from(tick))]
            else:
                pairs[micro] = [pair]
            if tick + 1 == CROSS_TICK:
                pairs[micro].append(routed(pairs[micro][0], up_relayed))
        if tick == TURN_TICK:
            turned = turned_call(own_in, other_in, probe, full_out, order, kept[-1][-1][0])
    for tick in range(LAYERS - 1):
        for micro in range(MICRO):
            pair, low_grads = backward_call(tick, section, pairs[micro], *turned, kept[micro][LAYERS - 2 - tick])
            grads[micro].append(low_grads)
            pairs[micro] = [routed(pair, down_across if tick + 1 == CROSS_TICK else down_from(LAYERS - 1 - tick))]
            if tick + 1 == CROSS_TICK:
                pairs[micro].append(routed(pairs[micro][0], down_relayed))
    sums = ()
    for micro in range(MICRO):
        norms = [stores[0] for stores in kept[micro]]
        sums = curvature_call(
            micro, section, pairs[micro][0], turned[2], slopes[micro], curvature_order, opening_n, norms, grads[micro], sums
        )
    away, stay = sums
    other = routed(away, swap_core)
    summed = (stay + other.astype(jnp.float32)).astype(jnp.bfloat16)
    summed = lax.all_to_all(summed.reshape(4, 64, HIDDEN), "y", 0, 0, tiled=True)
    summed = jnp.sum(summed.astype(jnp.float32), axis=0).astype(jnp.bfloat16)
    summed = lax.all_to_all(summed.reshape(8, 8, HIDDEN), ("b1", "b2", "b4"), 0, 0, tiled=True)
    summed = jnp.sum(summed.astype(jnp.float32), axis=0)
    probe_own = lax.dynamic_slice_in_dim(probe, lax.axis_index(DP) * 8, 8, 0)
    return (probe_own.astype(jnp.float32) * summed)[None]


def solution(mesh):
    fine = Mesh(mesh.devices.reshape(SIZES), NAMES)
    return jax.shard_map(
        shards,
        mesh=fine,
        in_specs=(
            P(DP, None),
            P(DP, None),
            P(SECTION, DP, None),
            P(SECTION, DP, None),
            P(SECTION, None, None),
        ),
        out_specs=P(SECTION, DP, None),
        check_vma=False,
    )
```

```python
import functools
import itertools

import jax
import jax.numpy as jnp
from jax import lax
from jax.experimental import pallas as pl
from jax.experimental.pallas import tpu as pltpu
from jax.sharding import Mesh, PartitionSpec as P

EPSILON = 1e-05
SQRT_HALF = 0.7071067811865476
INV_ROOT_TWO_PI = 0.3989422804014327
CONTRACT_FIRST = (((0,), (0,)), ((), ()))

NAMES = ("zh", "x", "b4", "b2", "b1", "y", "c")
SIZES = (2, 4, 2, 2, 2, 4, 2)
SECTION = ("zh", "x")
DP = ("b4", "b2", "b1", "y", "c")
PLACES = 6
LAYERS = 8
FEATURES = 512
HIDDEN = 2048
MICRO = 2
ROWS = 128 // MICRO
UNROLL_UP = 1
UNROLL_DOWN = 2
UNROLL_LAST = 2
TURN_TICK = 3
TOKENS = 8192
CHUNK = 1024
CHUNKS = HIDDEN // CHUNK
VMEM_BYTES = 4 * 1024 * 1024
WHOLE = pl.BlockSpec(memory_space=pltpu.VMEM)
SMEM = pl.BlockSpec(memory_space=pltpu.SMEM)


def flat(place):
    index = 0
    for size, at in zip(SIZES, place):
        index = index * size + at
    return index


def routed(value, route):
    pairs = []
    for place in itertools.product(*(range(size) for size in SIZES)):
        there = route(*place)
        if there is not None:
            pairs.append((flat(place), flat(there)))
    return lax.ppermute(value, NAMES, pairs)


def swap_b4(zh, x, b4, b2, b1, y, c):
    return (zh, x, 1 - b4, b2, b1, y, c)


def goal_route(zh, x, b4, b2, b1, y, c):
    return (zh, x, 1 - b4, 1 - b2, 1 - b1, y, c) if (zh, x) == (1, 3) else None


def swap_b2(zh, x, b4, b2, b1, y, c):
    return (zh, x, b4, 1 - b2, b1, y, c)


def swap_b1(zh, x, b4, b2, b1, y, c):
    return (zh, x, b4, b2, 1 - b1, y, c)


def swap_even(zh, x, b4, b2, b1, y, c):
    return (zh, x, b4, b2, b1, y ^ 1, c)


def swap_odd(zh, x, b4, b2, b1, y, c):
    return (zh, x, b4, b2, b1, y ^ 3, c)


def swap_core(zh, x, b4, b2, b1, y, c):
    return (zh, x, b4, b2, b1, y, 1 - c)


def up_from(section):
    def route(zh, x, b4, b2, b1, y, c):
        return (zh, x + 1, b4, b2, b1, y, c) if x == section % 4 else None

    return route


def down_from(section):
    def route(zh, x, b4, b2, b1, y, c):
        return (zh, x - 1, b4, b2, b1, y, c) if x == section % 4 else None

    return route


def crossing(half, x_from, x_to):
    def first(zh, x, b4, b2, b1, y, c):
        if (zh, x) != (half, x_from):
            return None
        return (zh, x_to, b4, b2, b1, y, c) if c else (1 - zh, x, 1 - b4, 1 - b2, 1 - b1, y, c)

    def second(zh, x, b4, b2, b1, y, c):
        if (zh, x, c) == (1 - half, x_from, 0):
            return (zh, x_to, b4, b2, b1, y, c)
        if (zh, x, c) == (half, x_to, 1):
            return (1 - zh, x, 1 - b4, 1 - b2, 1 - b1, y, c)
        return None

    return lambda pair: routed(routed(pair, first), second)


def doubled(block, route):
    return jnp.concatenate([block, routed(block, route)], axis=0)


def gathered(block, even_first):
    for route in (swap_b4, swap_b2, swap_b1) + ((swap_even, swap_odd) if even_first else (swap_odd, swap_even)):
        block = doubled(block, route)
    return block, routed(block, swap_core)


def natural_block(place, b4, b2, b1, y, c):
    z = (b4 ^ place[0][0]) * 4 + (b2 ^ place[1][0]) * 2 + (b1 ^ place[2][0])
    return z * 8 + (y ^ place[3][0]) * 2 + (c ^ place[4][0])


def settled_kernel(*refs):
    block_in, block = refs[PLACES:]
    block[...] = block_in[...]


def settled_call(place, block):
    return pl.pallas_call(
        settled_kernel,
        out_shape=jax.ShapeDtypeStruct(block.shape, block.dtype),
        in_specs=[SMEM] * PLACES + [WHOLE],
        out_specs=WHOLE,
        compiler_params=PARAMS,
        name="settled",
    )(*place, block)


def placed_kernel(*refs):
    place = refs[:PLACES]
    own_out, other_out, full_out = refs[PLACES:]
    rows = HIDDEN // 64
    for core, half in enumerate((own_out, other_out)):
        for index in range(32):
            odd, even = index // 8 % 2, index // 16
            there = natural_block(place, index % 2, index // 2 % 2, index // 4 % 2, even ^ (odd * 3), core)
            full_out[pl.ds(pl.multiple_of(there * rows, rows), rows), :] = half[index * rows : (index + 1) * rows, :]


def placed_call(place, own_out, other_out):
    return pl.pallas_call(
        placed_kernel,
        out_shape=jax.ShapeDtypeStruct((HIDDEN, FEATURES), jnp.bfloat16),
        in_specs=[SMEM] * PLACES + [WHOLE] * 2,
        out_specs=WHOLE,
        compiler_params=PARAMS,
        name="placed_w_out",
    )(*place, own_out, other_out)


def row_mean(values):
    return jnp.mean(values, axis=-1, keepdims=True)


def columns(chunk):
    return pl.ds(pl.multiple_of(chunk * CHUNK, CHUNK), CHUNK)


def one_hot(natural_row):
    natural = lax.broadcasted_iota(jnp.int32, (FEATURES, FEATURES), 0)
    return jnp.where(natural == natural_row, 1.0, 0.0).astype(jnp.bfloat16)


def opening_kernel(*refs):
    place = refs[:PLACES]
    inputs, probe, order, curvature_order, normed_out, preact_t = refs[PLACES:]
    at = lax.broadcasted_iota(jnp.int32, (FEATURES, FEATURES), 1)
    row, b4, b2, b1 = at % 8, (at // 8) % 2, (at // 16) % 2, (at // 32) % 2
    even, odd, core = (at // 64) % 2, (at // 128) % 2, at // 256
    order[...] = one_hot(natural_block(place, b4, b2, b1, even ^ (odd * 3), core) * 8 + row)
    block = (b4 * 4 + b2 * 2 + b1) * 8 + ((at // 64) % 4) * 2 + (core ^ place[4][0])
    curvature_order[...] = one_hot(block * 8 + row)
    inflow = inputs[...].astype(jnp.float32)
    centred = inflow - row_mean(inflow)
    normed = (centred * lax.rsqrt(row_mean(centred * centred) + EPSILON)).astype(jnp.bfloat16)
    normed_out[...] = normed

    def step(chunk, carry):
        preact_t[:, columns(chunk)] = jnp.dot(normed, probe[:, columns(chunk)], preferred_element_type=jnp.float32)
        return carry

    lax.fori_loop(0, CHUNKS, step, 0)


def opening_call(place, inputs, probe):
    rows = inputs.shape[0]
    order = jax.ShapeDtypeStruct((FEATURES, FEATURES), jnp.bfloat16)
    return pl.pallas_call(
        opening_kernel,
        out_shape=[
            order,
            order,
            jax.ShapeDtypeStruct((rows, FEATURES), jnp.bfloat16),
            jax.ShapeDtypeStruct((rows, HIDDEN), jnp.float32),
        ],
        in_specs=[SMEM] * PLACES + [WHOLE] * 2,
        out_specs=[WHOLE] * 4,
        compiler_params=PARAMS,
        name="opening",
    )(*place, inputs, probe)


def gelu_slopes(preact, preact_t, slope_out, chunk):
    normal_cdf = 0.5 * (1.0 + lax.erf(preact * SQRT_HALF))
    density = INV_ROOT_TWO_PI * jnp.exp(-0.5 * preact * preact)
    slope = normal_cdf + preact * density
    slope_out[0, :, columns(chunk)] = slope
    slope_out[1, :, columns(chunk)] = density * (2.0 - preact * preact) * preact_t
    return jnp.concatenate([preact * normal_cdf, slope * preact_t], axis=0).astype(jnp.bfloat16)


def halves_product(lhs, own_in, other_in, now):
    return jnp.dot(lhs[:, OWN_HALF], own_in[:, now], preferred_element_type=jnp.float32) + jnp.dot(
        lhs[:, OTHER_HALF], other_in[:, now], preferred_element_type=jnp.float32
    )


def first_kernel(micro, section, inputs, opening_n, opening_t, order, own_in, other_in, w_out, pair_out, slope_out, lhs, acc):
    rows = slice(micro * ROWS, (micro + 1) * ROWS)

    @pl.when(section[0] == 0)
    def _():
        lhs[...] = jnp.dot(opening_n[rows], order[...], preferred_element_type=jnp.float32).astype(jnp.bfloat16)
        acc[:ROWS] = inputs[rows].astype(jnp.float32)
        acc[ROWS:] = jnp.zeros((ROWS, FEATURES), jnp.float32)

        def step(chunk, carry):
            preact = halves_product(lhs[...], own_in, other_in, columns(chunk))
            hidden = gelu_slopes(preact, opening_t[rows, columns(chunk)], slope_out, chunk)
            acc[...] += jnp.dot(hidden, w_out[columns(chunk), :], preferred_element_type=jnp.float32)
            return carry

        lax.fori_loop(0, CHUNKS, step, 0, unroll=UNROLL_LAST)
        pair_out[0] = acc[:ROWS].astype(jnp.bfloat16)
        pair_out[1] = acc[ROWS:].astype(jnp.bfloat16)


def forward_kernel(tick, *refs):
    last = tick == LAYERS - 1
    section, pair, own_in, other_in, probe, w_out, order = refs[:7]
    refs = refs[7:]
    if last:
        goal, refs = refs[0], refs[1:]
    pair_out, norm, stat, slope_out, natural, lhs, acc = refs

    @pl.when(section[0] == tick)
    def _():
        inflow = pair[0].astype(jnp.float32)
        inflow_t = pair[1].astype(jnp.float32)
        centred = inflow - row_mean(inflow)
        rscale = lax.rsqrt(row_mean(centred * centred) + EPSILON)
        normed = centred * rscale
        tangent_dot = row_mean(normed * inflow_t)
        normed_t = rscale * (inflow_t - row_mean(inflow_t) - normed * tangent_dot)
        norm[0] = normed
        norm[1] = normed_t
        stat[0] = jnp.broadcast_to(rscale, (ROWS, 128))
        stat[1] = jnp.broadcast_to(tangent_dot, (ROWS, 128))
        acc[:ROWS] = inflow
        acc[ROWS:] = inflow_t
        natural[:ROWS] = normed.astype(jnp.bfloat16)
        natural[ROWS:] = normed_t.astype(jnp.bfloat16)
        lhs[...] = jnp.dot(natural[...], order[...], preferred_element_type=jnp.float32).astype(jnp.bfloat16)

        def step(chunk, carry):
            both = halves_product(lhs[...], own_in, other_in, columns(chunk))
            preact_t = both[ROWS:] + jnp.dot(
                natural[:ROWS], probe[:, columns(chunk)], preferred_element_type=jnp.float32
            )
            hidden = gelu_slopes(both[:ROWS], preact_t, slope_out, chunk)
            acc[...] += jnp.dot(hidden, w_out[columns(chunk), :], preferred_element_type=jnp.float32)
            return carry

        lax.fori_loop(0, CHUNKS, step, 0, unroll=UNROLL_UP)
        if last:
            pair_out[0] = ((acc[:ROWS] - goal[...].astype(jnp.float32)) / TOKENS).astype(jnp.bfloat16)
            pair_out[1] = (acc[ROWS:] / TOKENS).astype(jnp.bfloat16)
        else:
            pair_out[0] = acc[:ROWS].astype(jnp.bfloat16)
            pair_out[1] = acc[ROWS:].astype(jnp.bfloat16)


NORM = jax.ShapeDtypeStruct((2, ROWS, FEATURES), jnp.float32)
STAT = jax.ShapeDtypeStruct((2, ROWS, 128), jnp.float32)
SLOPE = jax.ShapeDtypeStruct((2, ROWS, HIDDEN), jnp.float32)
PAIR = jax.ShapeDtypeStruct((2, ROWS, FEATURES), jnp.bfloat16)
GRADS = jax.ShapeDtypeStruct((2 * ROWS, HIDDEN), jnp.bfloat16)
PARAMS = pltpu.CompilerParams(vmem_limit_bytes=VMEM_BYTES)


def first_call(micro, section, inputs, opening_n, opening_t, order, own_in, other_in, w_out):
    return pl.pallas_call(
        functools.partial(first_kernel, micro),
        out_shape=[PAIR, SLOPE],
        in_specs=[SMEM] + [WHOLE] * 7,
        out_specs=[WHOLE] * 2,
        scratch_shapes=[
            pltpu.VMEM((ROWS, FEATURES), jnp.bfloat16),
            pltpu.VMEM((2 * ROWS, FEATURES), jnp.float32),
        ],
        compiler_params=PARAMS,
        name="layer_up_0",
    )(section, inputs, opening_n, opening_t, order, own_in, other_in, w_out)


def forward_call(tick, section, pair, own_in, other_in, probe, w_out, order, goal):
    operands = [section, pair, own_in, other_in, probe, w_out, order] + ([goal] if tick == LAYERS - 1 else [])
    return pl.pallas_call(
        functools.partial(forward_kernel, tick),
        out_shape=[PAIR, NORM, STAT, SLOPE],
        in_specs=[SMEM] + [WHOLE] * (len(operands) - 1),
        out_specs=[WHOLE] * 4,
        scratch_shapes=[
            pltpu.VMEM((2 * ROWS, FEATURES), jnp.bfloat16),
            pltpu.VMEM((2 * ROWS, FEATURES), jnp.bfloat16),
            pltpu.VMEM((2 * ROWS, FEATURES), jnp.float32),
        ],
        compiler_params=PARAMS,
        name=f"layer_up_{tick}",
    )(*operands)


def turned_kernel(own_in, other_in, probe, w_out, order, token, w_in_t, probe_t, w_out_t):
    by_place = (((0,), (1,)), ((), ()))

    def step(index, carry):
        now = pl.ds(pl.multiple_of(index * FEATURES, FEATURES), FEATURES)
        own = lax.dot_general(own_in[:, now], order[:, OWN_HALF], by_place, preferred_element_type=jnp.float32)
        other = lax.dot_general(other_in[:, now], order[:, OTHER_HALF], by_place, preferred_element_type=jnp.float32)
        w_in_t[now, :] = (own + other).astype(jnp.bfloat16)
        probe_t[now, :] = probe[:, now].T
        w_out_t[:, now] = w_out[now, :].T
        return carry

    lax.fori_loop(0, HIDDEN // FEATURES, step, 0)


def turned_call(own_in, other_in, probe, w_out, order, token):
    tall = jax.ShapeDtypeStruct((HIDDEN, FEATURES), jnp.bfloat16)
    wide = jax.ShapeDtypeStruct((FEATURES, HIDDEN), jnp.bfloat16)
    return pl.pallas_call(
        turned_kernel,
        out_shape=[tall, tall, wide],
        in_specs=[WHOLE] * 5 + [pl.BlockSpec(memory_space=pl.ANY)],
        out_specs=[WHOLE] * 3,
        compiler_params=PARAMS,
        name="turned_weights",
    )(own_in, other_in, probe, w_out, order, token)


def hidden_grads(pair, w_out_t, slope, chunk):
    both = jnp.dot(
        pair[...].reshape(2 * ROWS, FEATURES), w_out_t[:, columns(chunk)], preferred_element_type=jnp.float32
    )
    grad_hidden, grad_hidden_t = both[:ROWS], both[ROWS:]
    slope_chunk = slope[0, :, columns(chunk)]
    grad_pre = grad_hidden * slope_chunk
    grad_pre_t = grad_hidden_t * slope_chunk + grad_hidden * slope[1, :, columns(chunk)]
    return grad_pre.astype(jnp.bfloat16), grad_pre_t.astype(jnp.bfloat16)


def norm_apply(values, normed, rscale):
    return rscale * (values - row_mean(values) - normed * row_mean(normed * values))


def backward_kernel(tick, *refs):
    section, pair, w_in_t, probe_t, w_out_t, norm, stat, slope = refs[:8]
    pair_out, grads, acc, acc_t = refs[8:]

    @pl.when(section[0] == LAYERS - 1 - tick)
    def _():
        acc[...] = jnp.zeros_like(acc)
        acc_t[...] = jnp.zeros_like(acc_t)

        def step(chunk, carry):
            low_grad, low_grad_t = hidden_grads(pair, w_out_t, slope, chunk)
            both = jnp.concatenate([low_grad_t, low_grad], axis=0)
            grads[:, columns(chunk)] = both
            acc[...] += jnp.dot(both, w_in_t[columns(chunk), :], preferred_element_type=jnp.float32)
            acc_t[...] += jnp.dot(low_grad, probe_t[columns(chunk), :], preferred_element_type=jnp.float32)
            return carry

        lax.fori_loop(0, CHUNKS, step, 0, unroll=UNROLL_DOWN)
        normed, normed_t = norm[0], norm[1]
        rscale, tangent_dot = stat[0][:, :1], stat[1][:, :1]
        grad_norm = acc[ROWS:]
        grad_norm_t = acc[:ROWS] + acc_t[...]
        through = norm_apply(grad_norm, normed, rscale)
        through_t = (
            norm_apply(grad_norm_t, normed, rscale)
            - rscale * tangent_dot * through
            - rscale * (normed_t * row_mean(normed * grad_norm) + normed * row_mean(normed_t * grad_norm))
        )
        pair_out[0] = (pair[0].astype(jnp.float32) + through).astype(jnp.bfloat16)
        pair_out[1] = (pair[1].astype(jnp.float32) + through_t).astype(jnp.bfloat16)


def backward_call(tick, section, pair, w_in_t, probe_t, w_out_t, kept):
    operands = [section, pair, w_in_t, probe_t, w_out_t, *kept]
    return pl.pallas_call(
        functools.partial(backward_kernel, tick),
        out_shape=[PAIR, GRADS],
        in_specs=[SMEM] + [WHOLE] * (len(operands) - 1),
        out_specs=[WHOLE] * 2,
        scratch_shapes=[
            pltpu.VMEM((2 * ROWS, FEATURES), jnp.float32),
            pltpu.VMEM((ROWS, FEATURES), jnp.float32),
        ],
        compiler_params=PARAMS,
        name=f"layer_down_{tick}",
    )(*operands)


OWN_HALF = slice(0, FEATURES // 2)
OTHER_HALF = slice(FEATURES // 2, FEATURES)


def curvature_operands(micro, section, pair, w_out_t, slope, order, opening_n, norms, grads, lhs, rhs):
    @pl.when(section[0] == 0)
    def _():
        rows = slice(micro * ROWS, (micro + 1) * ROWS)
        lhs[:ROWS] = jnp.dot(opening_n[rows], order[...], preferred_element_type=jnp.float32).astype(jnp.bfloat16)
        lhs[ROWS:] = jnp.zeros((ROWS, FEATURES), jnp.bfloat16)

        def bottom(chunk, carry):
            low_grad, low_grad_t = hidden_grads(pair, w_out_t, slope, chunk)
            rhs[:, columns(chunk)] = jnp.concatenate([low_grad_t, low_grad], axis=0)
            return carry

        lax.fori_loop(0, CHUNKS, bottom, 0, unroll=UNROLL_LAST)

    for layer in range(1, LAYERS):

        @pl.when(section[0] == layer)
        def _():
            both = norms[layer - 1][...].reshape(2 * ROWS, FEATURES).astype(jnp.bfloat16)
            lhs[...] = jnp.dot(both, order[...], preferred_element_type=jnp.float32).astype(jnp.bfloat16)
            rhs[...] = grads[LAYERS - 1 - layer][...]


def curvature_kernel(micro, final, *refs):
    section, pair, w_out_t, slope, order, opening_n = refs[:6]
    norms, refs = refs[6 : 5 + LAYERS], refs[5 + LAYERS :]
    grads, refs = refs[: LAYERS - 1], refs[LAYERS - 1 :]
    if final:
        away_in, stay_in, refs = refs[0], refs[1], refs[2:]
    away, stay, lhs, rhs = refs
    curvature_operands(micro, section, pair, w_out_t, slope, order, opening_n, norms, grads, lhs, rhs)

    def step(chunk, carry):
        now = columns(chunk)

        def product(half):
            return lax.dot_general(lhs[:, half], rhs[:, now], CONTRACT_FIRST, preferred_element_type=jnp.float32)

        if final:
            away[:, now] = (away_in[:, now] + product(OTHER_HALF)).astype(jnp.bfloat16)
            stay[:, now] = stay_in[:, now] + product(OWN_HALF)
        else:
            away[:, now] = product(OTHER_HALF)
            stay[:, now] = product(OWN_HALF)
        return carry

    lax.fori_loop(0, CHUNKS, step, 0, unroll=UNROLL_LAST)


def curvature_call(micro, section, pair, w_out_t, slope, order, opening_n, norms, grads, sums):
    half = (FEATURES // 2, HIDDEN)
    final = bool(sums)
    operands = [section, pair, w_out_t, slope, order, opening_n, *norms, *grads, *sums]
    return pl.pallas_call(
        functools.partial(curvature_kernel, micro, final),
        out_shape=[
            jax.ShapeDtypeStruct(half, jnp.bfloat16 if final else jnp.float32),
            jax.ShapeDtypeStruct(half, jnp.float32),
        ],
        in_specs=[SMEM] + [WHOLE] * (len(operands) - 1),
        out_specs=[WHOLE] * 2,
        scratch_shapes=[
            pltpu.VMEM((2 * ROWS, FEATURES), jnp.bfloat16),
            pltpu.VMEM((2 * ROWS, HIDDEN), jnp.bfloat16),
        ],
        compiler_params=PARAMS,
        name="curvature_last" if final else "curvature_first",
    )(*operands)


def shards(inputs, targets, w_in, w_out, probes):
    place = [jnp.reshape(lax.axis_index(name), (1,)).astype(jnp.int32) for name in (*DP, SECTION)]
    section = place[-1]
    out_block = settled_call(place, w_out[0])
    probe = probes[0]
    own_in, other_in = gathered(w_in[0], True)
    full_out = placed_call(place, *gathered(out_block, False))
    order, curvature_order, opening_n, opening_t = opening_call(place, inputs, probe)
    goal = routed(targets, goal_route)
    pairs, slopes, kept, grads = [None] * MICRO, [], [], []
    for micro in range(MICRO):
        kept.append([])
        grads.append([])
    for tick in range(LAYERS):
        for micro in range(MICRO):
            if tick == 0:
                pairs[micro], slope = first_call(
                    micro, section, inputs, opening_n, opening_t, order, own_in, other_in, full_out
                )
                slopes.append(slope)
            else:
                goal_now = goal[micro * ROWS : (micro + 1) * ROWS]
                pairs[micro], *stores = forward_call(
                    tick, section, pairs[micro], own_in, other_in, probe, full_out, order, goal_now
                )
                kept[micro].append(stores)
            if tick + 1 == LAYERS // 2:
                pairs[micro] = crossing(0, 3, 0)(pairs[micro])
            elif tick < LAYERS - 1:
                pairs[micro] = routed(pairs[micro], up_from(tick))
        if tick == TURN_TICK:
            turned = turned_call(own_in, other_in, probe, full_out, order, kept[-1][-1][0])
    for tick in range(LAYERS - 1):
        for micro in range(MICRO):
            pairs[micro], low_grads = backward_call(
                tick, section, pairs[micro], *turned, kept[micro][LAYERS - 2 - tick]
            )
            grads[micro].append(low_grads)
            if tick + 1 == LAYERS // 2:
                pairs[micro] = crossing(1, 0, 3)(pairs[micro])
            else:
                pairs[micro] = routed(pairs[micro], down_from(LAYERS - 1 - tick))
    sums = ()
    for micro in range(MICRO):
        norms = [stores[0] for stores in kept[micro]]
        sums = curvature_call(
            micro, section, pairs[micro], turned[2], slopes[micro], curvature_order, opening_n, norms, grads[micro], sums
        )
    away, stay = sums
    other = routed(away, swap_core)
    summed = (stay + other.astype(jnp.float32)).astype(jnp.bfloat16)
    summed = lax.all_to_all(summed.reshape(4, 64, HIDDEN), "y", 0, 0, tiled=True)
    summed = jnp.sum(summed.astype(jnp.float32), axis=0).astype(jnp.bfloat16)
    summed = lax.all_to_all(summed.reshape(8, 8, HIDDEN), ("b1", "b2", "b4"), 0, 0, tiled=True)
    summed = jnp.sum(summed.astype(jnp.float32), axis=0)
    probe_own = lax.dynamic_slice_in_dim(probe, lax.axis_index(DP) * 8, 8, 0)
    return (probe_own.astype(jnp.float32) * summed)[None]


def solution(mesh):
    fine = Mesh(mesh.devices.reshape(SIZES), NAMES)
    return jax.shard_map(
        shards,
        mesh=fine,
        in_specs=(
            P(DP, None),
            P(DP, None),
            P(SECTION, DP, None),
            P(SECTION, DP, None),
            P(SECTION, None, None),
        ),
        out_specs=P(SECTION, DP, None),
        check_vma=False,
    )
```

```python
import functools
import itertools

import jax
import jax.numpy as jnp
from jax import lax
from jax.experimental import pallas as pl
from jax.experimental.pallas import tpu as pltpu
from jax.sharding import Mesh, PartitionSpec as P

EPSILON = 1e-05
SQRT_HALF = 0.7071067811865476
INV_ROOT_TWO_PI = 0.3989422804014327
CONTRACT_FIRST = (((0,), (0,)), ((), ()))

NAMES = ("zh", "x", "b4", "b2", "b1", "y", "c")
SIZES = (2, 4, 2, 2, 2, 4, 2)
SECTION = ("zh", "x")
DP = ("b4", "b2", "b1", "y", "c")
PLACES = 6
LAYERS = 8
FEATURES = 512
HIDDEN = 2048
MICRO = 2
ROWS = 128 // MICRO
UNROLL_UP = 2
UNROLL_DOWN = 2
UNROLL_LAST = 1
TURN_TICK = 3
CROSS_TICK = 4
TOKENS = 8192
CHUNK = 1024
CHUNKS = HIDDEN // CHUNK
VMEM_BYTES = 4 * 1024 * 1024
WHOLE = pl.BlockSpec(memory_space=pltpu.VMEM)
SMEM = pl.BlockSpec(memory_space=pltpu.SMEM)


def flat(place):
    index = 0
    for size, at in zip(SIZES, place):
        index = index * size + at
    return index


def routed(value, route):
    pairs = []
    for place in itertools.product(*(range(size) for size in SIZES)):
        there = route(*place)
        if there is not None:
            pairs.append((flat(place), flat(there)))
    return lax.ppermute(value, NAMES, pairs)


def swap_b4(zh, x, b4, b2, b1, y, c):
    return (zh, x, 1 - b4, b2, b1, y, c)


def goal_route(zh, x, b4, b2, b1, y, c):
    return (zh, x, 1 - b4, 1 - b2, 1 - b1, y, c) if (zh, x) == (1, 3) else None


def swap_b2(zh, x, b4, b2, b1, y, c):
    return (zh, x, b4, 1 - b2, b1, y, c)


def swap_b1(zh, x, b4, b2, b1, y, c):
    return (zh, x, b4, b2, 1 - b1, y, c)


def swap_even(zh, x, b4, b2, b1, y, c):
    return (zh, x, b4, b2, b1, y ^ 1, c)


def swap_odd(zh, x, b4, b2, b1, y, c):
    return (zh, x, b4, b2, b1, y ^ 3, c)


def swap_core(zh, x, b4, b2, b1, y, c):
    return (zh, x, b4, b2, b1, y, 1 - c)


def up_from(section):
    def route(zh, x, b4, b2, b1, y, c):
        return (zh, x + 1, b4, b2, b1, y, c) if x == section % 4 else None

    return route


def down_from(section):
    def route(zh, x, b4, b2, b1, y, c):
        return (zh, x - 1, b4, b2, b1, y, c) if x == section % 4 else None

    return route


def up_across(zh, x, b4, b2, b1, y, c):
    if (zh, x) != (0, 3):
        return None
    return (0, 0, b4, b2, b1, y, 1) if c else (1, 0, 1 - b4, 1 - b2, 1 - b1, y, 0)


def up_relayed(zh, x, b4, b2, b1, y, c):
    return (1, 0, 1 - b4, 1 - b2, 1 - b1, y, 1) if (zh, x, c) == (0, 0, 1) else None


def down_across(zh, x, b4, b2, b1, y, c):
    if (zh, x) != (1, 0):
        return None
    return (1, 3, b4, b2, b1, y, 1) if c else (0, 3, 1 - b4, 1 - b2, 1 - b1, y, 0)


def down_relayed(zh, x, b4, b2, b1, y, c):
    return (0, 3, 1 - b4, 1 - b2, 1 - b1, y, 1) if (zh, x, c) == (1, 3, 1) else None


def doubled(block, route):
    return jnp.concatenate([block, routed(block, route)], axis=0)


def gathered(block, even_first):
    for route in (swap_b4, swap_b2, swap_b1) + ((swap_even, swap_odd) if even_first else (swap_odd, swap_even)):
        block = doubled(block, route)
    return block, routed(block, swap_core)


def natural_block(place, b4, b2, b1, y, c):
    z = (b4 ^ place[0][0]) * 4 + (b2 ^ place[1][0]) * 2 + (b1 ^ place[2][0])
    return z * 8 + (y ^ place[3][0]) * 2 + (c ^ place[4][0])


def settled_kernel(*refs):
    block_in, block = refs[PLACES:]
    block[...] = block_in[...]


def settled_call(place, block):
    return pl.pallas_call(
        settled_kernel,
        out_shape=jax.ShapeDtypeStruct(block.shape, block.dtype),
        in_specs=[SMEM] * PLACES + [WHOLE],
        out_specs=WHOLE,
        compiler_params=PARAMS,
        name="settled",
    )(*place, block)


def placed_kernel(*refs):
    place = refs[:PLACES]
    own_out, other_out, full_out = refs[PLACES:]
    rows = HIDDEN // 64
    for core, half in enumerate((own_out, other_out)):
        for index in range(32):
            odd, even = index // 8 % 2, index // 16
            there = natural_block(place, index % 2, index // 2 % 2, index // 4 % 2, even ^ (odd * 3), core)
            full_out[pl.ds(pl.multiple_of(there * rows, rows), rows), :] = half[index * rows : (index + 1) * rows, :]


def placed_call(place, own_out, other_out):
    return pl.pallas_call(
        placed_kernel,
        out_shape=jax.ShapeDtypeStruct((HIDDEN, FEATURES), jnp.bfloat16),
        in_specs=[SMEM] * PLACES + [WHOLE] * 2,
        out_specs=WHOLE,
        compiler_params=PARAMS,
        name="placed_w_out",
    )(*place, own_out, other_out)


def row_mean(values):
    return jnp.mean(values, axis=-1, keepdims=True)


def columns(chunk):
    return pl.ds(pl.multiple_of(chunk * CHUNK, CHUNK), CHUNK)


def one_hot(natural_row):
    natural = lax.broadcasted_iota(jnp.int32, (FEATURES, FEATURES), 0)
    return jnp.where(natural == natural_row, 1.0, 0.0).astype(jnp.bfloat16)


def opening_kernel(*refs):
    place = refs[:PLACES]
    inputs, probe, order, curvature_order, normed_out, preact_t = refs[PLACES:]
    at = lax.broadcasted_iota(jnp.int32, (FEATURES, FEATURES), 1)
    row, b4, b2, b1 = at % 8, (at // 8) % 2, (at // 16) % 2, (at // 32) % 2
    even, odd, core = (at // 64) % 2, (at // 128) % 2, at // 256
    order[...] = one_hot(natural_block(place, b4, b2, b1, even ^ (odd * 3), core) * 8 + row)
    block = (b4 * 4 + b2 * 2 + b1) * 8 + ((at // 64) % 4) * 2 + (core ^ place[4][0])
    curvature_order[...] = one_hot(block * 8 + row)
    inflow = inputs[...].astype(jnp.float32)
    centred = inflow - row_mean(inflow)
    normed = (centred * lax.rsqrt(row_mean(centred * centred) + EPSILON)).astype(jnp.bfloat16)
    normed_out[...] = normed

    def step(chunk, carry):
        preact_t[:, columns(chunk)] = jnp.dot(normed, probe[:, columns(chunk)], preferred_element_type=jnp.float32)
        return carry

    lax.fori_loop(0, CHUNKS, step, 0)


def opening_call(place, inputs, probe):
    rows = inputs.shape[0]
    order = jax.ShapeDtypeStruct((FEATURES, FEATURES), jnp.bfloat16)
    return pl.pallas_call(
        opening_kernel,
        out_shape=[
            order,
            order,
            jax.ShapeDtypeStruct((rows, FEATURES), jnp.bfloat16),
            jax.ShapeDtypeStruct((rows, HIDDEN), jnp.float32),
        ],
        in_specs=[SMEM] * PLACES + [WHOLE] * 2,
        out_specs=[WHOLE] * 4,
        compiler_params=PARAMS,
        name="opening",
    )(*place, inputs, probe)


def gelu_slopes(preact, preact_t, slope_out, chunk):
    normal_cdf = 0.5 * (1.0 + lax.erf(preact * SQRT_HALF))
    density = INV_ROOT_TWO_PI * jnp.exp(-0.5 * preact * preact)
    slope = normal_cdf + preact * density
    slope_out[0, :, columns(chunk)] = slope
    slope_out[1, :, columns(chunk)] = density * (2.0 - preact * preact) * preact_t
    return jnp.concatenate([preact * normal_cdf, slope * preact_t], axis=0).astype(jnp.bfloat16)


def halves_product(lhs, own_in, other_in, now):
    return jnp.dot(lhs[:, OWN_HALF], own_in[:, now], preferred_element_type=jnp.float32) + jnp.dot(
        lhs[:, OTHER_HALF], other_in[:, now], preferred_element_type=jnp.float32
    )


def first_kernel(micro, section, inputs, opening_n, opening_t, order, own_in, other_in, w_out, pair_out, slope_out, lhs, acc):
    rows = slice(micro * ROWS, (micro + 1) * ROWS)

    @pl.when(section[0] == 0)
    def _():
        lhs[...] = jnp.dot(opening_n[rows], order[...], preferred_element_type=jnp.float32).astype(jnp.bfloat16)
        acc[:ROWS] = inputs[rows].astype(jnp.float32)
        acc[ROWS:] = jnp.zeros((ROWS, FEATURES), jnp.float32)

        def step(chunk, carry):
            preact = halves_product(lhs[...], own_in, other_in, columns(chunk))
            hidden = gelu_slopes(preact, opening_t[rows, columns(chunk)], slope_out, chunk)
            acc[...] += jnp.dot(hidden, w_out[columns(chunk), :], preferred_element_type=jnp.float32)
            return carry

        lax.fori_loop(0, CHUNKS, step, 0, unroll=UNROLL_LAST)
        pair_out[0] = acc[:ROWS].astype(jnp.bfloat16)
        pair_out[1] = acc[ROWS:].astype(jnp.bfloat16)


def forward_kernel(tick, *refs):
    last = tick == LAYERS - 1
    section, own_in, other_in, probe, w_out, order = refs[:6]
    pairs, refs = (refs[6:8], refs[8:]) if tick == CROSS_TICK else (refs[6:7], refs[7:])
    if last:
        goal, refs = refs[0], refs[1:]
    pair_out, norm, stat, slope_out, natural, lhs, acc = refs

    @pl.when(section[0] == tick)
    def _():
        inflow = sum(pair[0].astype(jnp.float32) for pair in pairs)
        inflow_t = sum(pair[1].astype(jnp.float32) for pair in pairs)
        centred = inflow - row_mean(inflow)
        rscale = lax.rsqrt(row_mean(centred * centred) + EPSILON)
        normed = centred * rscale
        tangent_dot = row_mean(normed * inflow_t)
        normed_t = rscale * (inflow_t - row_mean(inflow_t) - normed * tangent_dot)
        norm[0] = normed
        norm[1] = normed_t
        stat[0] = jnp.broadcast_to(rscale, (ROWS, 128))
        stat[1] = jnp.broadcast_to(tangent_dot, (ROWS, 128))
        acc[:ROWS] = inflow
        acc[ROWS:] = inflow_t
        natural[:ROWS] = normed.astype(jnp.bfloat16)
        natural[ROWS:] = normed_t.astype(jnp.bfloat16)
        lhs[...] = jnp.dot(natural[...], order[...], preferred_element_type=jnp.float32).astype(jnp.bfloat16)

        def step(chunk, carry):
            both = halves_product(lhs[...], own_in, other_in, columns(chunk))
            preact_t = both[ROWS:] + jnp.dot(
                natural[:ROWS], probe[:, columns(chunk)], preferred_element_type=jnp.float32
            )
            hidden = gelu_slopes(both[:ROWS], preact_t, slope_out, chunk)
            acc[...] += jnp.dot(hidden, w_out[columns(chunk), :], preferred_element_type=jnp.float32)
            return carry

        lax.fori_loop(0, CHUNKS, step, 0, unroll=UNROLL_UP)
        if last:
            pair_out[0] = ((acc[:ROWS] - goal[...].astype(jnp.float32)) / TOKENS).astype(jnp.bfloat16)
            pair_out[1] = (acc[ROWS:] / TOKENS).astype(jnp.bfloat16)
        else:
            pair_out[0] = acc[:ROWS].astype(jnp.bfloat16)
            pair_out[1] = acc[ROWS:].astype(jnp.bfloat16)


NORM = jax.ShapeDtypeStruct((2, ROWS, FEATURES), jnp.float32)
STAT = jax.ShapeDtypeStruct((2, ROWS, 128), jnp.float32)
SLOPE = jax.ShapeDtypeStruct((2, ROWS, HIDDEN), jnp.float32)
PAIR = jax.ShapeDtypeStruct((2, ROWS, FEATURES), jnp.bfloat16)
GRADS = jax.ShapeDtypeStruct((2 * ROWS, HIDDEN), jnp.bfloat16)
PARAMS = pltpu.CompilerParams(vmem_limit_bytes=VMEM_BYTES)


def first_call(micro, section, inputs, opening_n, opening_t, order, own_in, other_in, w_out):
    return pl.pallas_call(
        functools.partial(first_kernel, micro),
        out_shape=[PAIR, SLOPE],
        in_specs=[SMEM] + [WHOLE] * 7,
        out_specs=[WHOLE] * 2,
        scratch_shapes=[
            pltpu.VMEM((ROWS, FEATURES), jnp.bfloat16),
            pltpu.VMEM((2 * ROWS, FEATURES), jnp.float32),
        ],
        compiler_params=PARAMS,
        name="layer_up_0",
    )(section, inputs, opening_n, opening_t, order, own_in, other_in, w_out)


def forward_call(tick, section, pairs, own_in, other_in, probe, w_out, order, goal):
    operands = [section, own_in, other_in, probe, w_out, order, *pairs] + ([goal] if tick == LAYERS - 1 else [])
    return pl.pallas_call(
        functools.partial(forward_kernel, tick),
        out_shape=[PAIR, NORM, STAT, SLOPE],
        in_specs=[SMEM] + [WHOLE] * (len(operands) - 1),
        out_specs=[WHOLE] * 4,
        scratch_shapes=[
            pltpu.VMEM((2 * ROWS, FEATURES), jnp.bfloat16),
            pltpu.VMEM((2 * ROWS, FEATURES), jnp.bfloat16),
            pltpu.VMEM((2 * ROWS, FEATURES), jnp.float32),
        ],
        compiler_params=PARAMS,
        name=f"layer_up_{tick}",
    )(*operands)


def turned_kernel(own_in, other_in, probe, w_out, order, token, w_in_t, probe_t, w_out_t):
    by_place = (((0,), (1,)), ((), ()))

    def step(index, carry):
        now = pl.ds(pl.multiple_of(index * FEATURES, FEATURES), FEATURES)
        own = lax.dot_general(own_in[:, now], order[:, OWN_HALF], by_place, preferred_element_type=jnp.float32)
        other = lax.dot_general(other_in[:, now], order[:, OTHER_HALF], by_place, preferred_element_type=jnp.float32)
        w_in_t[now, :] = (own + other).astype(jnp.bfloat16)
        probe_t[now, :] = probe[:, now].T
        w_out_t[:, now] = w_out[now, :].T
        return carry

    lax.fori_loop(0, HIDDEN // FEATURES, step, 0)


def turned_call(own_in, other_in, probe, w_out, order, token):
    tall = jax.ShapeDtypeStruct((HIDDEN, FEATURES), jnp.bfloat16)
    wide = jax.ShapeDtypeStruct((FEATURES, HIDDEN), jnp.bfloat16)
    return pl.pallas_call(
        turned_kernel,
        out_shape=[tall, tall, wide],
        in_specs=[WHOLE] * 5 + [pl.BlockSpec(memory_space=pl.ANY)],
        out_specs=[WHOLE] * 3,
        compiler_params=PARAMS,
        name="turned_weights",
    )(own_in, other_in, probe, w_out, order, token)


def hidden_grads(pair, w_out_t, slope, chunk):
    both = jnp.dot(
        pair[...].reshape(2 * ROWS, FEATURES), w_out_t[:, columns(chunk)], preferred_element_type=jnp.float32
    )
    grad_hidden, grad_hidden_t = both[:ROWS], both[ROWS:]
    slope_chunk = slope[0, :, columns(chunk)]
    grad_pre = grad_hidden * slope_chunk
    grad_pre_t = grad_hidden_t * slope_chunk + grad_hidden * slope[1, :, columns(chunk)]
    return grad_pre.astype(jnp.bfloat16), grad_pre_t.astype(jnp.bfloat16)


def norm_apply(values, normed, rscale):
    return rscale * (values - row_mean(values) - normed * row_mean(normed * values))


def backward_kernel(tick, *refs):
    section, pair, w_in_t, probe_t, w_out_t, norm, stat, slope = refs[:8]
    refs = refs[8:]
    if tick == CROSS_TICK:
        other_pair, pair_out, grads, acc, acc_t, whole = refs
    else:
        pair_out, grads, acc, acc_t = refs

    @pl.when(section[0] == LAYERS - 1 - tick)
    def _():
        adjoint = pair
        if tick == CROSS_TICK:
            adjoint = whole
            whole[...] = (pair[...].astype(jnp.float32) + other_pair[...].astype(jnp.float32)).astype(jnp.bfloat16)
        acc[...] = jnp.zeros_like(acc)
        acc_t[...] = jnp.zeros_like(acc_t)

        def step(chunk, carry):
            low_grad, low_grad_t = hidden_grads(adjoint, w_out_t, slope, chunk)
            both = jnp.concatenate([low_grad_t, low_grad], axis=0)
            grads[:, columns(chunk)] = both
            acc[...] += jnp.dot(both, w_in_t[columns(chunk), :], preferred_element_type=jnp.float32)
            acc_t[...] += jnp.dot(low_grad, probe_t[columns(chunk), :], preferred_element_type=jnp.float32)
            return carry

        lax.fori_loop(0, CHUNKS, step, 0, unroll=UNROLL_DOWN)
        normed, normed_t = norm[0], norm[1]
        rscale, tangent_dot = stat[0][:, :1], stat[1][:, :1]
        grad_norm = acc[ROWS:]
        grad_norm_t = acc[:ROWS] + acc_t[...]
        through = norm_apply(grad_norm, normed, rscale)
        through_t = (
            norm_apply(grad_norm_t, normed, rscale)
            - rscale * tangent_dot * through
            - rscale * (normed_t * row_mean(normed * grad_norm) + normed * row_mean(normed_t * grad_norm))
        )
        pair_out[0] = (adjoint[0].astype(jnp.float32) + through).astype(jnp.bfloat16)
        pair_out[1] = (adjoint[1].astype(jnp.float32) + through_t).astype(jnp.bfloat16)


def backward_call(tick, section, pairs, w_in_t, probe_t, w_out_t, kept):
    operands = [section, pairs[0], w_in_t, probe_t, w_out_t, *kept, *pairs[1:]]
    whole = [pltpu.VMEM(PAIR.shape, PAIR.dtype)] if tick == CROSS_TICK else []
    return pl.pallas_call(
        functools.partial(backward_kernel, tick),
        out_shape=[PAIR, GRADS],
        in_specs=[SMEM] + [WHOLE] * (len(operands) - 1),
        out_specs=[WHOLE] * 2,
        scratch_shapes=[
            pltpu.VMEM((2 * ROWS, FEATURES), jnp.float32),
            pltpu.VMEM((ROWS, FEATURES), jnp.float32),
            *whole,
        ],
        compiler_params=PARAMS,
        name=f"layer_down_{tick}",
    )(*operands)


OWN_HALF = slice(0, FEATURES // 2)
OTHER_HALF = slice(FEATURES // 2, FEATURES)


def curvature_operands(micro, section, pair, w_out_t, slope, order, opening_n, norms, grads, lhs, rhs):
    @pl.when(section[0] == 0)
    def _():
        rows = slice(micro * ROWS, (micro + 1) * ROWS)
        lhs[:ROWS] = jnp.dot(opening_n[rows], order[...], preferred_element_type=jnp.float32).astype(jnp.bfloat16)
        lhs[ROWS:] = jnp.zeros((ROWS, FEATURES), jnp.bfloat16)

        def bottom(chunk, carry):
            low_grad, low_grad_t = hidden_grads(pair, w_out_t, slope, chunk)
            rhs[:, columns(chunk)] = jnp.concatenate([low_grad_t, low_grad], axis=0)
            return carry

        lax.fori_loop(0, CHUNKS, bottom, 0, unroll=UNROLL_LAST)

    for layer in range(1, LAYERS):

        @pl.when(section[0] == layer)
        def _():
            both = norms[layer - 1][...].reshape(2 * ROWS, FEATURES).astype(jnp.bfloat16)
            lhs[...] = jnp.dot(both, order[...], preferred_element_type=jnp.float32).astype(jnp.bfloat16)
            rhs[...] = grads[LAYERS - 1 - layer][...]


def curvature_kernel(micro, final, *refs):
    section, pair, w_out_t, slope, order, opening_n = refs[:6]
    norms, refs = refs[6 : 5 + LAYERS], refs[5 + LAYERS :]
    grads, refs = refs[: LAYERS - 1], refs[LAYERS - 1 :]
    if final:
        away_in, stay_in, refs = refs[0], refs[1], refs[2:]
    away, stay, lhs, rhs = refs
    curvature_operands(micro, section, pair, w_out_t, slope, order, opening_n, norms, grads, lhs, rhs)

    def step(chunk, carry):
        now = columns(chunk)

        def product(half):
            return lax.dot_general(lhs[:, half], rhs[:, now], CONTRACT_FIRST, preferred_element_type=jnp.float32)

        if final:
            away[:, now] = (away_in[:, now] + product(OTHER_HALF)).astype(jnp.bfloat16)
            stay[:, now] = stay_in[:, now] + product(OWN_HALF)
        else:
            away[:, now] = product(OTHER_HALF)
            stay[:, now] = product(OWN_HALF)
        return carry

    lax.fori_loop(0, CHUNKS, step, 0, unroll=UNROLL_LAST)


def curvature_call(micro, section, pair, w_out_t, slope, order, opening_n, norms, grads, sums):
    half = (FEATURES // 2, HIDDEN)
    final = bool(sums)
    operands = [section, pair, w_out_t, slope, order, opening_n, *norms, *grads, *sums]
    return pl.pallas_call(
        functools.partial(curvature_kernel, micro, final),
        out_shape=[
            jax.ShapeDtypeStruct(half, jnp.bfloat16 if final else jnp.float32),
            jax.ShapeDtypeStruct(half, jnp.float32),
        ],
        in_specs=[SMEM] + [WHOLE] * (len(operands) - 1),
        out_specs=[WHOLE] * 2,
        scratch_shapes=[
            pltpu.VMEM((2 * ROWS, FEATURES), jnp.bfloat16),
            pltpu.VMEM((2 * ROWS, HIDDEN), jnp.bfloat16),
        ],
        compiler_params=PARAMS,
        name="curvature_last" if final else "curvature_first",
    )(*operands)


def shards(inputs, targets, w_in, w_out, probes):
    place = [jnp.reshape(lax.axis_index(name), (1,)).astype(jnp.int32) for name in (*DP, SECTION)]
    section = place[-1]
    out_block = settled_call(place, w_out[0])
    probe = probes[0]
    own_in, other_in = gathered(w_in[0], True)
    full_out = placed_call(place, *gathered(out_block, False))
    order, curvature_order, opening_n, opening_t = opening_call(place, inputs, probe)
    goal = routed(targets, goal_route)
    pairs, slopes, kept, grads = [None] * MICRO, [], [], []
    for micro in range(MICRO):
        kept.append([])
        grads.append([])
    for tick in range(LAYERS):
        for micro in range(MICRO):
            if tick == 0:
                pair, slope = first_call(
                    micro, section, inputs, opening_n, opening_t, order, own_in, other_in, full_out
                )
                slopes.append(slope)
            else:
                goal_now = goal[micro * ROWS : (micro + 1) * ROWS]
                pair, *stores = forward_call(
                    tick, section, pairs[micro], own_in, other_in, probe, full_out, order, goal_now
                )
                kept[micro].append(stores)
            if tick < LAYERS - 1:
                pairs[micro] = [routed(pair, up_across if tick + 1 == CROSS_TICK else up_from(tick))]
            else:
                pairs[micro] = [pair]
            if tick + 1 == CROSS_TICK:
                pairs[micro].append(routed(pairs[micro][0], up_relayed))
        if tick == TURN_TICK:
            turned = turned_call(own_in, other_in, probe, full_out, order, kept[-1][-1][0])
    for tick in range(LAYERS - 1):
        for micro in range(MICRO):
            pair, low_grads = backward_call(tick, section, pairs[micro], *turned, kept[micro][LAYERS - 2 - tick])
            grads[micro].append(low_grads)
            pairs[micro] = [routed(pair, down_across if tick + 1 == CROSS_TICK else down_from(LAYERS - 1 - tick))]
            if tick + 1 == CROSS_TICK:
                pairs[micro].append(routed(pairs[micro][0], down_relayed))
    sums = ()
    for micro in range(MICRO):
        norms = [stores[0] for stores in kept[micro]]
        sums = curvature_call(
            micro, section, pairs[micro][0], turned[2], slopes[micro], curvature_order, opening_n, norms, grads[micro], sums
        )
    away, stay = sums
    other = routed(away, swap_core)
    summed = (stay + other.astype(jnp.float32)).astype(jnp.bfloat16)
    summed = lax.all_to_all(summed.reshape(4, 64, HIDDEN), "y", 0, 0, tiled=True)
    summed = jnp.sum(summed.astype(jnp.float32), axis=0).astype(jnp.bfloat16)
    summed = lax.all_to_all(summed.reshape(8, 8, HIDDEN), ("b1", "b2", "b4"), 0, 0, tiled=True)
    summed = jnp.sum(summed.astype(jnp.float32), axis=0)
    probe_own = lax.dynamic_slice_in_dim(probe, lax.axis_index(DP) * 8, 8, 0)
    return (probe_own.astype(jnp.float32) * summed)[None]


def solution(mesh):
    fine = Mesh(mesh.devices.reshape(SIZES), NAMES)
    return jax.shard_map(
        shards,
        mesh=fine,
        in_specs=(
            P(DP, None),
            P(DP, None),
            P(SECTION, DP, None),
            P(SECTION, DP, None),
            P(SECTION, None, None),
        ),
        out_specs=P(SECTION, DP, None),
        check_vma=False,
    )
```

```python
import functools
import itertools

import jax
import jax.numpy as jnp
from jax import lax
from jax.experimental import pallas as pl
from jax.experimental.pallas import tpu as pltpu
from jax.sharding import Mesh, PartitionSpec as P

EPSILON = 1e-05
SQRT_HALF = 0.7071067811865476
INV_ROOT_TWO_PI = 0.3989422804014327
CONTRACT_FIRST = (((0,), (0,)), ((), ()))

NAMES = ("zh", "x", "b4", "b2", "b1", "y", "c")
SIZES = (2, 4, 2, 2, 2, 4, 2)
SECTION = ("zh", "x")
DP = ("b4", "b2", "b1", "y", "c")
PLACES = 6
LAYERS = 8
FEATURES = 512
HIDDEN = 2048
MICRO = 2
ROWS = 128 // MICRO
UNROLL_UP = 1
UNROLL_LAST = 2
TURN_TICK = 3
CROSS_TICK = 4
TOKENS = 8192
CHUNK = 1024
CHUNKS = HIDDEN // CHUNK
VMEM_BYTES = 4 * 1024 * 1024
WHOLE = pl.BlockSpec(memory_space=pltpu.VMEM)
SMEM = pl.BlockSpec(memory_space=pltpu.SMEM)


def flat(place):
    index = 0
    for size, at in zip(SIZES, place):
        index = index * size + at
    return index


def routed(value, route):
    pairs = []
    for place in itertools.product(*(range(size) for size in SIZES)):
        there = route(*place)
        if there is not None:
            pairs.append((flat(place), flat(there)))
    return lax.ppermute(value, NAMES, pairs)


def swap_b4(zh, x, b4, b2, b1, y, c):
    return (zh, x, 1 - b4, b2, b1, y, c)


def goal_route(zh, x, b4, b2, b1, y, c):
    return (zh, x, 1 - b4, 1 - b2, 1 - b1, y, c) if (zh, x) == (1, 3) else None


def swap_b2(zh, x, b4, b2, b1, y, c):
    return (zh, x, b4, 1 - b2, b1, y, c)


def swap_b1(zh, x, b4, b2, b1, y, c):
    return (zh, x, b4, b2, 1 - b1, y, c)


def swap_even(zh, x, b4, b2, b1, y, c):
    return (zh, x, b4, b2, b1, y ^ 1, c)


def swap_odd(zh, x, b4, b2, b1, y, c):
    return (zh, x, b4, b2, b1, y ^ 3, c)


def swap_core(zh, x, b4, b2, b1, y, c):
    return (zh, x, b4, b2, b1, y, 1 - c)


def up_from(section):
    def route(zh, x, b4, b2, b1, y, c):
        return (zh, x + 1, b4, b2, b1, y, c) if x == section % 4 else None

    return route


def down_from(section):
    def route(zh, x, b4, b2, b1, y, c):
        return (zh, x - 1, b4, b2, b1, y, c) if x == section % 4 else None

    return route


def up_across(zh, x, b4, b2, b1, y, c):
    if (zh, x) != (0, 3):
        return None
    return (0, 0, b4, b2, b1, y, 1) if c else (1, 0, 1 - b4, 1 - b2, 1 - b1, y, 0)


def up_relayed(zh, x, b4, b2, b1, y, c):
    return (1, 0, 1 - b4, 1 - b2, 1 - b1, y, 1) if (zh, x, c) == (0, 0, 1) else None


def down_across(zh, x, b4, b2, b1, y, c):
    if (zh, x) != (1, 0):
        return None
    return (1, 3, b4, b2, b1, y, 1) if c else (0, 3, 1 - b4, 1 - b2, 1 - b1, y, 0)


def down_relayed(zh, x, b4, b2, b1, y, c):
    return (0, 3, 1 - b4, 1 - b2, 1 - b1, y, 1) if (zh, x, c) == (1, 3, 1) else None


def doubled(block, route):
    return jnp.concatenate([block, routed(block, route)], axis=0)


def gathered(block, even_first):
    for route in (swap_b4, swap_b2, swap_b1) + ((swap_even, swap_odd) if even_first else (swap_odd, swap_even)):
        block = doubled(block, route)
    return block, routed(block, swap_core)


def natural_block(place, b4, b2, b1, y, c):
    z = (b4 ^ place[0][0]) * 4 + (b2 ^ place[1][0]) * 2 + (b1 ^ place[2][0])
    return z * 8 + (y ^ place[3][0]) * 2 + (c ^ place[4][0])


def settled_kernel(*refs):
    block_in, block = refs[PLACES:]
    block[...] = block_in[...]


def settled_call(place, block):
    return pl.pallas_call(
        settled_kernel,
        out_shape=jax.ShapeDtypeStruct(block.shape, block.dtype),
        in_specs=[SMEM] * PLACES + [WHOLE],
        out_specs=WHOLE,
        compiler_params=PARAMS,
        name="settled",
    )(*place, block)


def placed_kernel(*refs):
    place = refs[:PLACES]
    own_out, other_out, full_out = refs[PLACES:]
    rows = HIDDEN // 64
    for core, half in enumerate((own_out, other_out)):
        for index in range(32):
            odd, even = index // 8 % 2, index // 16
            there = natural_block(place, index % 2, index // 2 % 2, index // 4 % 2, even ^ (odd * 3), core)
            full_out[pl.ds(pl.multiple_of(there * rows, rows), rows), :] = half[index * rows : (index + 1) * rows, :]


def placed_call(place, own_out, other_out):
    return pl.pallas_call(
        placed_kernel,
        out_shape=jax.ShapeDtypeStruct((HIDDEN, FEATURES), jnp.bfloat16),
        in_specs=[SMEM] * PLACES + [WHOLE] * 2,
        out_specs=WHOLE,
        compiler_params=PARAMS,
        name="placed_w_out",
    )(*place, own_out, other_out)


def row_mean(values):
    return jnp.mean(values, axis=-1, keepdims=True)


def columns(chunk):
    return pl.ds(pl.multiple_of(chunk * CHUNK, CHUNK), CHUNK)


def one_hot(natural_row):
    natural = lax.broadcasted_iota(jnp.int32, (FEATURES, FEATURES), 0)
    return jnp.where(natural == natural_row, 1.0, 0.0).astype(jnp.bfloat16)


def opening_kernel(*refs):
    place = refs[:PLACES]
    inputs, probe, order, curvature_order, normed_out, preact_t = refs[PLACES:]
    at = lax.broadcasted_iota(jnp.int32, (FEATURES, FEATURES), 1)
    row, b4, b2, b1 = at % 8, (at // 8) % 2, (at // 16) % 2, (at // 32) % 2
    even, odd, core = (at // 64) % 2, (at // 128) % 2, at // 256
    order[...] = one_hot(natural_block(place, b4, b2, b1, even ^ (odd * 3), core) * 8 + row)
    block = (b4 * 4 + b2 * 2 + b1) * 8 + ((at // 64) % 4) * 2 + (core ^ place[4][0])
    curvature_order[...] = one_hot(block * 8 + row)
    inflow = inputs[...].astype(jnp.float32)
    centred = inflow - row_mean(inflow)
    normed = (centred * lax.rsqrt(row_mean(centred * centred) + EPSILON)).astype(jnp.bfloat16)
    normed_out[...] = normed

    def step(chunk, carry):
        preact_t[:, columns(chunk)] = jnp.dot(normed, probe[:, columns(chunk)], preferred_element_type=jnp.float32)
        return carry

    lax.fori_loop(0, CHUNKS, step, 0)


def opening_call(place, inputs, probe):
    rows = inputs.shape[0]
    order = jax.ShapeDtypeStruct((FEATURES, FEATURES), jnp.bfloat16)
    return pl.pallas_call(
        opening_kernel,
        out_shape=[
            order,
            order,
            jax.ShapeDtypeStruct((rows, FEATURES), jnp.bfloat16),
            jax.ShapeDtypeStruct((rows, HIDDEN), jnp.float32),
        ],
        in_specs=[SMEM] * PLACES + [WHOLE] * 2,
        out_specs=[WHOLE] * 4,
        compiler_params=PARAMS,
        name="opening",
    )(*place, inputs, probe)


def gelu_slopes(preact, preact_t, slope_out, chunk):
    normal_cdf = 0.5 * (1.0 + lax.erf(preact * SQRT_HALF))
    density = INV_ROOT_TWO_PI * jnp.exp(-0.5 * preact * preact)
    slope = normal_cdf + preact * density
    slope_out[0, :, columns(chunk)] = slope
    slope_out[1, :, columns(chunk)] = density * (2.0 - preact * preact) * preact_t
    return jnp.concatenate([preact * normal_cdf, slope * preact_t], axis=0).astype(jnp.bfloat16)


def halves_product(lhs, own_in, other_in, now):
    return jnp.dot(lhs[:, OWN_HALF], own_in[:, now], preferred_element_type=jnp.float32) + jnp.dot(
        lhs[:, OTHER_HALF], other_in[:, now], preferred_element_type=jnp.float32
    )


def first_kernel(micro, section, inputs, opening_n, opening_t, order, own_in, other_in, w_out, pair_out, slope_out, lhs, acc):
    rows = slice(micro * ROWS, (micro + 1) * ROWS)

    @pl.when(section[0] == 0)
    def _():
        lhs[...] = jnp.dot(opening_n[rows], order[...], preferred_element_type=jnp.float32).astype(jnp.bfloat16)
        acc[:ROWS] = inputs[rows].astype(jnp.float32)
        acc[ROWS:] = jnp.zeros((ROWS, FEATURES), jnp.float32)

        def step(chunk, carry):
            preact = halves_product(lhs[...], own_in, other_in, columns(chunk))
            hidden = gelu_slopes(preact, opening_t[rows, columns(chunk)], slope_out, chunk)
            acc[...] += jnp.dot(hidden, w_out[columns(chunk), :], preferred_element_type=jnp.float32)
            return carry

        lax.fori_loop(0, CHUNKS, step, 0, unroll=UNROLL_LAST)
        pair_out[0] = acc[:ROWS].astype(jnp.bfloat16)
        pair_out[1] = acc[ROWS:].astype(jnp.bfloat16)


def forward_kernel(tick, *refs):
    last = tick == LAYERS - 1
    section, own_in, other_in, probe, w_out, order = refs[:6]
    pairs, refs = (refs[6:8], refs[8:]) if tick == CROSS_TICK else (refs[6:7], refs[7:])
    if last:
        goal, refs = refs[0], refs[1:]
    pair_out, norm, stat, slope_out, natural, lhs, acc = refs

    @pl.when(section[0] == tick)
    def _():
        inflow = sum(pair[0].astype(jnp.float32) for pair in pairs)
        inflow_t = sum(pair[1].astype(jnp.float32) for pair in pairs)
        centred = inflow - row_mean(inflow)
        rscale = lax.rsqrt(row_mean(centred * centred) + EPSILON)
        normed = centred * rscale
        tangent_dot = row_mean(normed * inflow_t)
        normed_t = rscale * (inflow_t - row_mean(inflow_t) - normed * tangent_dot)
        norm[0] = normed
        norm[1] = normed_t
        stat[0] = jnp.broadcast_to(rscale, (ROWS, 128))
        stat[1] = jnp.broadcast_to(tangent_dot, (ROWS, 128))
        acc[:ROWS] = inflow
        acc[ROWS:] = inflow_t
        natural[:ROWS] = normed.astype(jnp.bfloat16)
        natural[ROWS:] = normed_t.astype(jnp.bfloat16)
        lhs[...] = jnp.dot(natural[...], order[...], preferred_element_type=jnp.float32).astype(jnp.bfloat16)

        def step(chunk, carry):
            both = halves_product(lhs[...], own_in, other_in, columns(chunk))
            preact_t = both[ROWS:] + jnp.dot(
                natural[:ROWS], probe[:, columns(chunk)], preferred_element_type=jnp.float32
            )
            hidden = gelu_slopes(both[:ROWS], preact_t, slope_out, chunk)
            acc[...] += jnp.dot(hidden, w_out[columns(chunk), :], preferred_element_type=jnp.float32)
            return carry

        lax.fori_loop(0, CHUNKS, step, 0, unroll=UNROLL_UP)
        if last:
            pair_out[0] = ((acc[:ROWS] - goal[...].astype(jnp.float32)) / TOKENS).astype(jnp.bfloat16)
            pair_out[1] = (acc[ROWS:] / TOKENS).astype(jnp.bfloat16)
        else:
            pair_out[0] = acc[:ROWS].astype(jnp.bfloat16)
            pair_out[1] = acc[ROWS:].astype(jnp.bfloat16)


NORM = jax.ShapeDtypeStruct((2, ROWS, FEATURES), jnp.float32)
STAT = jax.ShapeDtypeStruct((2, ROWS, 128), jnp.float32)
SLOPE = jax.ShapeDtypeStruct((2, ROWS, HIDDEN), jnp.float32)
PAIR = jax.ShapeDtypeStruct((2, ROWS, FEATURES), jnp.bfloat16)
GRADS = jax.ShapeDtypeStruct((2 * ROWS, HIDDEN), jnp.bfloat16)
PARAMS = pltpu.CompilerParams(vmem_limit_bytes=VMEM_BYTES)


def first_call(micro, section, inputs, opening_n, opening_t, order, own_in, other_in, w_out):
    return pl.pallas_call(
        functools.partial(first_kernel, micro),
        out_shape=[PAIR, SLOPE],
        in_specs=[SMEM] + [WHOLE] * 7,
        out_specs=[WHOLE] * 2,
        scratch_shapes=[
            pltpu.VMEM((ROWS, FEATURES), jnp.bfloat16),
            pltpu.VMEM((2 * ROWS, FEATURES), jnp.float32),
        ],
        compiler_params=PARAMS,
        name="layer_up_0",
    )(section, inputs, opening_n, opening_t, order, own_in, other_in, w_out)


def forward_call(tick, section, pairs, own_in, other_in, probe, w_out, order, goal):
    operands = [section, own_in, other_in, probe, w_out, order, *pairs] + ([goal] if tick == LAYERS - 1 else [])
    return pl.pallas_call(
        functools.partial(forward_kernel, tick),
        out_shape=[PAIR, NORM, STAT, SLOPE],
        in_specs=[SMEM] + [WHOLE] * (len(operands) - 1),
        out_specs=[WHOLE] * 4,
        scratch_shapes=[
            pltpu.VMEM((2 * ROWS, FEATURES), jnp.bfloat16),
            pltpu.VMEM((2 * ROWS, FEATURES), jnp.bfloat16),
            pltpu.VMEM((2 * ROWS, FEATURES), jnp.float32),
        ],
        compiler_params=PARAMS,
        name=f"layer_up_{tick}",
    )(*operands)


def turned_kernel(own_in, other_in, probe, w_out, order, token, w_in_t, probe_t, w_out_t):
    by_place = (((0,), (1,)), ((), ()))

    def step(index, carry):
        now = pl.ds(pl.multiple_of(index * FEATURES, FEATURES), FEATURES)
        own = lax.dot_general(own_in[:, now], order[:, OWN_HALF], by_place, preferred_element_type=jnp.float32)
        other = lax.dot_general(other_in[:, now], order[:, OTHER_HALF], by_place, preferred_element_type=jnp.float32)
        w_in_t[now, :] = (own + other).astype(jnp.bfloat16)
        probe_t[now, :] = probe[:, now].T
        w_out_t[:, now] = w_out[now, :].T
        return carry

    lax.fori_loop(0, HIDDEN // FEATURES, step, 0)


def turned_call(own_in, other_in, probe, w_out, order, token):
    tall = jax.ShapeDtypeStruct((HIDDEN, FEATURES), jnp.bfloat16)
    wide = jax.ShapeDtypeStruct((FEATURES, HIDDEN), jnp.bfloat16)
    return pl.pallas_call(
        turned_kernel,
        out_shape=[tall, tall, wide],
        in_specs=[WHOLE] * 5 + [pl.BlockSpec(memory_space=pl.ANY)],
        out_specs=[WHOLE] * 3,
        compiler_params=PARAMS,
        name="turned_weights",
    )(own_in, other_in, probe, w_out, order, token)


def hidden_grads(pair, w_out_t, slope, now):
    both = jnp.dot(
        pair[...].reshape(2 * ROWS, FEATURES), w_out_t[:, now], preferred_element_type=jnp.float32
    )
    grad_hidden, grad_hidden_t = both[:ROWS], both[ROWS:]
    slope_chunk = slope[0, :, now]
    grad_pre = grad_hidden * slope_chunk
    grad_pre_t = grad_hidden_t * slope_chunk + grad_hidden * slope[1, :, now]
    return grad_pre.astype(jnp.bfloat16), grad_pre_t.astype(jnp.bfloat16)


def norm_apply(values, normed, rscale):
    return rscale * (values - row_mean(values) - normed * row_mean(normed * values))


def backward_kernel(tick, *refs):
    section, pair, w_in_t, probe_t, w_out_t, norm, stat, slope = refs[:8]
    refs = refs[8:]
    if tick == CROSS_TICK:
        other_pair, pair_out, grads, acc, acc_t, whole = refs
    else:
        pair_out, grads, acc, acc_t = refs

    @pl.when(section[0] == LAYERS - 1 - tick)
    def _():
        adjoint = pair
        if tick == CROSS_TICK:
            adjoint = whole
            whole[...] = (pair[...].astype(jnp.float32) + other_pair[...].astype(jnp.float32)).astype(jnp.bfloat16)
        for chunk in range(CHUNKS):
            now = slice(chunk * CHUNK, (chunk + 1) * CHUNK)
            low_grad, low_grad_t = hidden_grads(adjoint, w_out_t, slope, now)
            both = jnp.concatenate([low_grad_t, low_grad], axis=0)
            grads[:, now] = both
            product = jnp.dot(both, w_in_t[now, :], preferred_element_type=jnp.float32)
            product_t = jnp.dot(low_grad, probe_t[now, :], preferred_element_type=jnp.float32)
            if chunk:
                acc[...] += product
                acc_t[...] += product_t
            else:
                acc[...] = product
                acc_t[...] = product_t

        normed, normed_t = norm[0], norm[1]
        rscale, tangent_dot = stat[0][:, :1], stat[1][:, :1]
        grad_norm = acc[ROWS:]
        grad_norm_t = acc[:ROWS] + acc_t[...]
        through = norm_apply(grad_norm, normed, rscale)
        through_t = (
            norm_apply(grad_norm_t, normed, rscale)
            - rscale * tangent_dot * through
            - rscale * (normed_t * row_mean(normed * grad_norm) + normed * row_mean(normed_t * grad_norm))
        )
        pair_out[0] = (adjoint[0].astype(jnp.float32) + through).astype(jnp.bfloat16)
        pair_out[1] = (adjoint[1].astype(jnp.float32) + through_t).astype(jnp.bfloat16)


def backward_call(tick, section, pairs, w_in_t, probe_t, w_out_t, kept):
    operands = [section, pairs[0], w_in_t, probe_t, w_out_t, *kept, *pairs[1:]]
    whole = [pltpu.VMEM(PAIR.shape, PAIR.dtype)] if tick == CROSS_TICK else []
    return pl.pallas_call(
        functools.partial(backward_kernel, tick),
        out_shape=[PAIR, GRADS],
        in_specs=[SMEM] + [WHOLE] * (len(operands) - 1),
        out_specs=[WHOLE] * 2,
        scratch_shapes=[
            pltpu.VMEM((2 * ROWS, FEATURES), jnp.float32),
            pltpu.VMEM((ROWS, FEATURES), jnp.float32),
            *whole,
        ],
        compiler_params=PARAMS,
        name=f"layer_down_{tick}",
    )(*operands)


OWN_HALF = slice(0, FEATURES // 2)
OTHER_HALF = slice(FEATURES // 2, FEATURES)


def curvature_operands(micro, section, pair, w_out_t, slope, order, opening_n, norms, grads, lhs, rhs):
    @pl.when(section[0] == 0)
    def _():
        rows = slice(micro * ROWS, (micro + 1) * ROWS)
        lhs[:ROWS] = jnp.dot(opening_n[rows], order[...], preferred_element_type=jnp.float32).astype(jnp.bfloat16)
        lhs[ROWS:] = jnp.zeros((ROWS, FEATURES), jnp.bfloat16)

        def bottom(chunk, carry):
            low_grad, low_grad_t = hidden_grads(pair, w_out_t, slope, columns(chunk))
            rhs[:, columns(chunk)] = jnp.concatenate([low_grad_t, low_grad], axis=0)
            return carry

        lax.fori_loop(0, CHUNKS, bottom, 0, unroll=UNROLL_LAST)

    for layer in range(1, LAYERS):

        @pl.when(section[0] == layer)
        def _():
            both = norms[layer - 1][...].reshape(2 * ROWS, FEATURES).astype(jnp.bfloat16)
            lhs[...] = jnp.dot(both, order[...], preferred_element_type=jnp.float32).astype(jnp.bfloat16)
            rhs[...] = grads[LAYERS - 1 - layer][...]


def curvature_kernel(micro, final, *refs):
    section, pair, w_out_t, slope, order, opening_n = refs[:6]
    norms, refs = refs[6 : 5 + LAYERS], refs[5 + LAYERS :]
    grads, refs = refs[: LAYERS - 1], refs[LAYERS - 1 :]
    if final:
        away_in, stay_in, refs = refs[0], refs[1], refs[2:]
    away, stay, lhs, rhs = refs
    curvature_operands(micro, section, pair, w_out_t, slope, order, opening_n, norms, grads, lhs, rhs)

    def step(chunk, carry):
        now = columns(chunk)

        def product(half):
            return lax.dot_general(lhs[:, half], rhs[:, now], CONTRACT_FIRST, preferred_element_type=jnp.float32)

        if final:
            away[:, now] = (away_in[:, now] + product(OTHER_HALF)).astype(jnp.bfloat16)
            stay[:, now] = stay_in[:, now] + product(OWN_HALF)
        else:
            away[:, now] = product(OTHER_HALF)
            stay[:, now] = product(OWN_HALF)
        return carry

    lax.fori_loop(0, CHUNKS, step, 0, unroll=UNROLL_LAST)


def curvature_call(micro, section, pair, w_out_t, slope, order, opening_n, norms, grads, sums):
    half = (FEATURES // 2, HIDDEN)
    final = bool(sums)
    operands = [section, pair, w_out_t, slope, order, opening_n, *norms, *grads, *sums]
    return pl.pallas_call(
        functools.partial(curvature_kernel, micro, final),
        out_shape=[
            jax.ShapeDtypeStruct(half, jnp.bfloat16 if final else jnp.float32),
            jax.ShapeDtypeStruct(half, jnp.float32),
        ],
        in_specs=[SMEM] + [WHOLE] * (len(operands) - 1),
        out_specs=[WHOLE] * 2,
        scratch_shapes=[
            pltpu.VMEM((2 * ROWS, FEATURES), jnp.bfloat16),
            pltpu.VMEM((2 * ROWS, HIDDEN), jnp.bfloat16),
        ],
        compiler_params=PARAMS,
        name="curvature_last" if final else "curvature_first",
    )(*operands)


def block_sum_kernel(blocks, total):
    total[...] = sum(blocks[index].astype(jnp.float32) for index in range(4)).astype(jnp.bfloat16)


def block_sum_call(blocks):
    return pl.pallas_call(
        block_sum_kernel,
        out_shape=jax.ShapeDtypeStruct(blocks.shape[1:], jnp.bfloat16),
        in_specs=[WHOLE],
        out_specs=WHOLE,
        compiler_params=PARAMS,
        name="block_sum",
    )(blocks)


def shards(inputs, targets, w_in, w_out, probes):
    place = [jnp.reshape(lax.axis_index(name), (1,)).astype(jnp.int32) for name in (*DP, SECTION)]
    section = place[-1]
    out_block = settled_call(place, w_out[0])
    probe = probes[0]
    own_in, other_in = gathered(w_in[0], True)
    full_out = placed_call(place, *gathered(out_block, False))
    order, curvature_order, opening_n, opening_t = opening_call(place, inputs, probe)
    goal = routed(targets, goal_route)
    pairs, slopes, kept, grads = [None] * MICRO, [], [], []
    for micro in range(MICRO):
        kept.append([])
        grads.append([])
    for tick in range(LAYERS):
        for micro in range(MICRO):
            if tick == 0:
                pair, slope = first_call(
                    micro, section, inputs, opening_n, opening_t, order, own_in, other_in, full_out
                )
                slopes.append(slope)
            else:
                goal_now = goal[micro * ROWS : (micro + 1) * ROWS]
                pair, *stores = forward_call(
                    tick, section, pairs[micro], own_in, other_in, probe, full_out, order, goal_now
                )
                kept[micro].append(stores)
            if tick < LAYERS - 1:
                pairs[micro] = [routed(pair, up_across if tick + 1 == CROSS_TICK else up_from(tick))]
            else:
                pairs[micro] = [pair]
            if tick + 1 == CROSS_TICK:
                pairs[micro].append(routed(pairs[micro][0], up_relayed))
        if tick == TURN_TICK:
            turned = turned_call(own_in, other_in, probe, full_out, order, kept[-1][-1][0])
    for tick in range(LAYERS - 1):
        for micro in range(MICRO):
            pair, low_grads = backward_call(tick, section, pairs[micro], *turned, kept[micro][LAYERS - 2 - tick])
            grads[micro].append(low_grads)
            pairs[micro] = [routed(pair, down_across if tick + 1 == CROSS_TICK else down_from(LAYERS - 1 - tick))]
            if tick + 1 == CROSS_TICK:
                pairs[micro].append(routed(pairs[micro][0], down_relayed))
    sums = ()
    for micro in range(MICRO):
        norms = [stores[0] for stores in kept[micro]]
        sums = curvature_call(
            micro, section, pairs[micro][0], turned[2], slopes[micro], curvature_order, opening_n, norms, grads[micro], sums
        )
    away, stay = sums
    other = routed(away, swap_core)
    summed = (stay + other.astype(jnp.float32)).astype(jnp.bfloat16)
    summed = lax.all_to_all(summed.reshape(4, 64, HIDDEN), "y", 0, 0, tiled=True)
    summed = block_sum_call(summed)
    summed = lax.all_to_all(summed.reshape(8, 8, HIDDEN), ("b1", "b2", "b4"), 0, 0, tiled=True)
    summed = jnp.sum(summed.astype(jnp.float32), axis=0)
    probe_own = lax.dynamic_slice_in_dim(probe, lax.axis_index(DP) * 8, 8, 0)
    return (probe_own.astype(jnp.float32) * summed)[None]


def solution(mesh):
    fine = Mesh(mesh.devices.reshape(SIZES), NAMES)
    return jax.shard_map(
        shards,
        mesh=fine,
        in_specs=(
            P(DP, None),
            P(DP, None),
            P(SECTION, DP, None),
            P(SECTION, DP, None),
            P(SECTION, None, None),
        ),
        out_specs=P(SECTION, DP, None),
        check_vma=False,
    )
```

```python
import functools
import itertools

import jax
import jax.numpy as jnp
from jax import lax
from jax.experimental import pallas as pl
from jax.experimental.pallas import tpu as pltpu
from jax.sharding import Mesh, PartitionSpec as P

EPSILON = 1e-05
SQRT_HALF = 0.7071067811865476
INV_ROOT_TWO_PI = 0.3989422804014327
CONTRACT_FIRST = (((0,), (0,)), ((), ()))

NAMES = ("zh", "x", "b4", "b2", "b1", "y", "c")
SIZES = (2, 4, 2, 2, 2, 4, 2)
SECTION = ("zh", "x")
DP = ("b4", "b2", "b1", "y", "c")
PLACES = 6
LAYERS = 8
FEATURES = 512
HIDDEN = 2048
MICRO = 2
ROWS = 128 // MICRO
UNROLL_UP = 1
UNROLL_LAST = 2
TURN_TICK = 3
CROSS_TICK = 4
TOKENS = 8192
CHUNK = 1024
CHUNKS = HIDDEN // CHUNK
VMEM_BYTES = 4 * 1024 * 1024
WHOLE = pl.BlockSpec(memory_space=pltpu.VMEM)
SMEM = pl.BlockSpec(memory_space=pltpu.SMEM)


def flat(place):
    index = 0
    for size, at in zip(SIZES, place):
        index = index * size + at
    return index


def routed(value, route):
    pairs = []
    for place in itertools.product(*(range(size) for size in SIZES)):
        there = route(*place)
        if there is not None:
            pairs.append((flat(place), flat(there)))
    return lax.ppermute(value, NAMES, pairs)


def swap_b4(zh, x, b4, b2, b1, y, c):
    return (zh, x, 1 - b4, b2, b1, y, c)


def goal_route(zh, x, b4, b2, b1, y, c):
    return (zh, x, 1 - b4, 1 - b2, 1 - b1, y, c) if (zh, x) == (1, 3) else None


def swap_b2(zh, x, b4, b2, b1, y, c):
    return (zh, x, b4, 1 - b2, b1, y, c)


def swap_b1(zh, x, b4, b2, b1, y, c):
    return (zh, x, b4, b2, 1 - b1, y, c)


def swap_even(zh, x, b4, b2, b1, y, c):
    return (zh, x, b4, b2, b1, y ^ 1, c)


def swap_odd(zh, x, b4, b2, b1, y, c):
    return (zh, x, b4, b2, b1, y ^ 3, c)


def swap_core(zh, x, b4, b2, b1, y, c):
    return (zh, x, b4, b2, b1, y, 1 - c)


def up_from(section):
    def route(zh, x, b4, b2, b1, y, c):
        return (zh, x + 1, b4, b2, b1, y, c) if x == section % 4 else None

    return route


def down_from(section):
    def route(zh, x, b4, b2, b1, y, c):
        return (zh, x - 1, b4, b2, b1, y, c) if x == section % 4 else None

    return route


def up_across(zh, x, b4, b2, b1, y, c):
    if (zh, x) != (0, 3):
        return None
    return (0, 0, b4, b2, b1, y, 1) if c else (1, 0, 1 - b4, 1 - b2, 1 - b1, y, 0)


def up_relayed(zh, x, b4, b2, b1, y, c):
    return (1, 0, 1 - b4, 1 - b2, 1 - b1, y, 1) if (zh, x, c) == (0, 0, 1) else None


def down_across(zh, x, b4, b2, b1, y, c):
    if (zh, x) != (1, 0):
        return None
    return (1, 3, b4, b2, b1, y, 1) if c else (0, 3, 1 - b4, 1 - b2, 1 - b1, y, 0)


def down_relayed(zh, x, b4, b2, b1, y, c):
    return (0, 3, 1 - b4, 1 - b2, 1 - b1, y, 1) if (zh, x, c) == (1, 3, 1) else None


def doubled(block, route):
    return jnp.concatenate([block, routed(block, route)], axis=0)


def gathered(block, even_first):
    for route in (swap_b4, swap_b2, swap_b1) + ((swap_even, swap_odd) if even_first else (swap_odd, swap_even)):
        block = doubled(block, route)
    return block, routed(block, swap_core)


def natural_block(place, b4, b2, b1, y, c):
    z = (b4 ^ place[0][0]) * 4 + (b2 ^ place[1][0]) * 2 + (b1 ^ place[2][0])
    return z * 8 + (y ^ place[3][0]) * 2 + (c ^ place[4][0])


def settled_kernel(*refs):
    block_in, block = refs[PLACES:]
    block[...] = block_in[...]


def settled_call(place, block):
    return pl.pallas_call(
        settled_kernel,
        out_shape=jax.ShapeDtypeStruct(block.shape, block.dtype),
        in_specs=[SMEM] * PLACES + [WHOLE],
        out_specs=WHOLE,
        compiler_params=PARAMS,
        name="settled",
    )(*place, block)


def placed_kernel(*refs):
    place = refs[:PLACES]
    own_out, other_out, full_out = refs[PLACES:]
    rows = HIDDEN // 64
    for core, half in enumerate((own_out, other_out)):
        for index in range(32):
            odd, even = index // 8 % 2, index // 16
            there = natural_block(place, index % 2, index // 2 % 2, index // 4 % 2, even ^ (odd * 3), core)
            full_out[pl.ds(pl.multiple_of(there * rows, rows), rows), :] = half[index * rows : (index + 1) * rows, :]


def placed_call(place, own_out, other_out):
    return pl.pallas_call(
        placed_kernel,
        out_shape=jax.ShapeDtypeStruct((HIDDEN, FEATURES), jnp.bfloat16),
        in_specs=[SMEM] * PLACES + [WHOLE] * 2,
        out_specs=WHOLE,
        compiler_params=PARAMS,
        name="placed_w_out",
    )(*place, own_out, other_out)


def row_mean(values):
    return jnp.mean(values, axis=-1, keepdims=True)


def columns(chunk):
    return pl.ds(pl.multiple_of(chunk * CHUNK, CHUNK), CHUNK)


def one_hot(natural_row):
    natural = lax.broadcasted_iota(jnp.int32, (FEATURES, FEATURES), 0)
    return jnp.where(natural == natural_row, 1.0, 0.0).astype(jnp.bfloat16)


def opening_kernel(*refs):
    place = refs[:PLACES]
    inputs, probe, order, curvature_order, normed_out, preact_t = refs[PLACES:]
    at = lax.broadcasted_iota(jnp.int32, (FEATURES, FEATURES), 1)
    row, b4, b2, b1 = at % 8, (at // 8) % 2, (at // 16) % 2, (at // 32) % 2
    even, odd, core = (at // 64) % 2, (at // 128) % 2, at // 256
    order[...] = one_hot(natural_block(place, b4, b2, b1, even ^ (odd * 3), core) * 8 + row)
    block = (b4 * 4 + b2 * 2 + b1) * 8 + ((at // 64) % 4) * 2 + (core ^ place[4][0])
    curvature_order[...] = one_hot(block * 8 + row)
    inflow = inputs[...].astype(jnp.float32)
    centred = inflow - row_mean(inflow)
    normed = (centred * lax.rsqrt(row_mean(centred * centred) + EPSILON)).astype(jnp.bfloat16)
    normed_out[...] = normed

    def step(chunk, carry):
        preact_t[:, columns(chunk)] = jnp.dot(normed, probe[:, columns(chunk)], preferred_element_type=jnp.float32)
        return carry

    lax.fori_loop(0, CHUNKS, step, 0)


def opening_call(place, inputs, probe):
    rows = inputs.shape[0]
    order = jax.ShapeDtypeStruct((FEATURES, FEATURES), jnp.bfloat16)
    return pl.pallas_call(
        opening_kernel,
        out_shape=[
            order,
            order,
            jax.ShapeDtypeStruct((rows, FEATURES), jnp.bfloat16),
            jax.ShapeDtypeStruct((rows, HIDDEN), jnp.float32),
        ],
        in_specs=[SMEM] * PLACES + [WHOLE] * 2,
        out_specs=[WHOLE] * 4,
        compiler_params=PARAMS,
        name="opening",
    )(*place, inputs, probe)


def gelu_slopes(preact, preact_t, slope_out, chunk):
    normal_cdf = 0.5 * (1.0 + lax.erf(preact * SQRT_HALF))
    density = INV_ROOT_TWO_PI * jnp.exp(-0.5 * preact * preact)
    slope = normal_cdf + preact * density
    slope_out[0, :, columns(chunk)] = slope
    slope_out[1, :, columns(chunk)] = density * (2.0 - preact * preact) * preact_t
    return jnp.concatenate([preact * normal_cdf, slope * preact_t], axis=0).astype(jnp.bfloat16)


def halves_product(lhs, own_in, other_in, now):
    return jnp.dot(lhs[:, OWN_HALF], own_in[:, now], preferred_element_type=jnp.float32) + jnp.dot(
        lhs[:, OTHER_HALF], other_in[:, now], preferred_element_type=jnp.float32
    )


def first_kernel(micro, section, inputs, opening_n, opening_t, order, own_in, other_in, w_out, pair_out, slope_out, lhs, acc):
    rows = slice(micro * ROWS, (micro + 1) * ROWS)

    @pl.when(section[0] == 0)
    def _():
        lhs[...] = jnp.dot(opening_n[rows], order[...], preferred_element_type=jnp.float32).astype(jnp.bfloat16)
        acc[:ROWS] = inputs[rows].astype(jnp.float32)
        acc[ROWS:] = jnp.zeros((ROWS, FEATURES), jnp.float32)

        def step(chunk, carry):
            preact = halves_product(lhs[...], own_in, other_in, columns(chunk))
            hidden = gelu_slopes(preact, opening_t[rows, columns(chunk)], slope_out, chunk)
            acc[...] += jnp.dot(hidden, w_out[columns(chunk), :], preferred_element_type=jnp.float32)
            return carry

        lax.fori_loop(0, CHUNKS, step, 0, unroll=UNROLL_LAST)
        pair_out[0] = acc[:ROWS].astype(jnp.bfloat16)
        pair_out[1] = acc[ROWS:].astype(jnp.bfloat16)


def forward_kernel(tick, *refs):
    last = tick == LAYERS - 1
    section, own_in, other_in, probe, w_out, order = refs[:6]
    pairs, refs = (refs[6:8], refs[8:]) if tick == CROSS_TICK else (refs[6:7], refs[7:])
    if last:
        goal, refs = refs[0], refs[1:]
    pair_out, norm, stat, slope_out, natural, lhs, acc = refs

    @pl.when(section[0] == tick)
    def _():
        inflow = sum(pair[0].astype(jnp.float32) for pair in pairs)
        inflow_t = sum(pair[1].astype(jnp.float32) for pair in pairs)
        centred = inflow - row_mean(inflow)
        rscale = lax.rsqrt(row_mean(centred * centred) + EPSILON)
        normed = centred * rscale
        tangent_dot = row_mean(normed * inflow_t)
        normed_t = rscale * (inflow_t - row_mean(inflow_t) - normed * tangent_dot)
        norm[0] = normed
        norm[1] = normed_t
        stat[0] = jnp.broadcast_to(rscale, (ROWS, 128))
        stat[1] = jnp.broadcast_to(tangent_dot, (ROWS, 128))
        acc[:ROWS] = inflow
        acc[ROWS:] = inflow_t
        natural[:ROWS] = normed.astype(jnp.bfloat16)
        natural[ROWS:] = normed_t.astype(jnp.bfloat16)
        lhs[...] = jnp.dot(natural[...], order[...], preferred_element_type=jnp.float32).astype(jnp.bfloat16)

        def step(chunk, carry):
            both = halves_product(lhs[...], own_in, other_in, columns(chunk))
            preact_t = both[ROWS:] + jnp.dot(
                natural[:ROWS], probe[:, columns(chunk)], preferred_element_type=jnp.float32
            )
            hidden = gelu_slopes(both[:ROWS], preact_t, slope_out, chunk)
            acc[...] += jnp.dot(hidden, w_out[columns(chunk), :], preferred_element_type=jnp.float32)
            return carry

        lax.fori_loop(0, CHUNKS, step, 0, unroll=2 if tick <= 2 else UNROLL_UP)
        if last:
            pair_out[0] = ((acc[:ROWS] - goal[...].astype(jnp.float32)) / TOKENS).astype(jnp.bfloat16)
            pair_out[1] = (acc[ROWS:] / TOKENS).astype(jnp.bfloat16)
        else:
            pair_out[0] = acc[:ROWS].astype(jnp.bfloat16)
            pair_out[1] = acc[ROWS:].astype(jnp.bfloat16)


NORM = jax.ShapeDtypeStruct((2, ROWS, FEATURES), jnp.float32)
STAT = jax.ShapeDtypeStruct((2, ROWS, 128), jnp.float32)
SLOPE = jax.ShapeDtypeStruct((2, ROWS, HIDDEN), jnp.float32)
PAIR = jax.ShapeDtypeStruct((2, ROWS, FEATURES), jnp.bfloat16)
GRADS = jax.ShapeDtypeStruct((2 * ROWS, HIDDEN), jnp.bfloat16)
PARAMS = pltpu.CompilerParams(vmem_limit_bytes=VMEM_BYTES)


def first_call(micro, section, inputs, opening_n, opening_t, order, own_in, other_in, w_out):
    return pl.pallas_call(
        functools.partial(first_kernel, micro),
        out_shape=[PAIR, SLOPE],
        in_specs=[SMEM] + [WHOLE] * 7,
        out_specs=[WHOLE] * 2,
        scratch_shapes=[
            pltpu.VMEM((ROWS, FEATURES), jnp.bfloat16),
            pltpu.VMEM((2 * ROWS, FEATURES), jnp.float32),
        ],
        compiler_params=PARAMS,
        name="layer_up_0",
    )(section, inputs, opening_n, opening_t, order, own_in, other_in, w_out)


def forward_call(tick, section, pairs, own_in, other_in, probe, w_out, order, goal):
    operands = [section, own_in, other_in, probe, w_out, order, *pairs] + ([goal] if tick == LAYERS - 1 else [])
    return pl.pallas_call(
        functools.partial(forward_kernel, tick),
        out_shape=[PAIR, NORM, STAT, SLOPE],
        in_specs=[SMEM] + [WHOLE] * (len(operands) - 1),
        out_specs=[WHOLE] * 4,
        scratch_shapes=[
            pltpu.VMEM((2 * ROWS, FEATURES), jnp.bfloat16),
            pltpu.VMEM((2 * ROWS, FEATURES), jnp.bfloat16),
            pltpu.VMEM((2 * ROWS, FEATURES), jnp.float32),
        ],
        compiler_params=PARAMS,
        name=f"layer_up_{tick}",
    )(*operands)


def turned_kernel(own_in, other_in, probe, w_out, order, token, w_in_t, probe_t, w_out_t):
    by_place = (((0,), (1,)), ((), ()))

    def step(index, carry):
        now = pl.ds(pl.multiple_of(index * FEATURES, FEATURES), FEATURES)
        own = lax.dot_general(own_in[:, now], order[:, OWN_HALF], by_place, preferred_element_type=jnp.float32)
        other = lax.dot_general(other_in[:, now], order[:, OTHER_HALF], by_place, preferred_element_type=jnp.float32)
        w_in_t[now, :] = (own + other).astype(jnp.bfloat16)
        probe_t[now, :] = probe[:, now].T
        w_out_t[:, now] = w_out[now, :].T
        return carry

    lax.fori_loop(0, HIDDEN // FEATURES, step, 0)


def turned_call(own_in, other_in, probe, w_out, order, token):
    tall = jax.ShapeDtypeStruct((HIDDEN, FEATURES), jnp.bfloat16)
    wide = jax.ShapeDtypeStruct((FEATURES, HIDDEN), jnp.bfloat16)
    return pl.pallas_call(
        turned_kernel,
        out_shape=[tall, tall, wide],
        in_specs=[WHOLE] * 5 + [pl.BlockSpec(memory_space=pl.ANY)],
        out_specs=[WHOLE] * 3,
        compiler_params=PARAMS,
        name="turned_weights",
    )(own_in, other_in, probe, w_out, order, token)


def hidden_grads(pair, w_out_t, slope, now):
    both = jnp.dot(
        pair[...].reshape(2 * ROWS, FEATURES), w_out_t[:, now], preferred_element_type=jnp.float32
    )
    grad_hidden, grad_hidden_t = both[:ROWS], both[ROWS:]
    slope_chunk = slope[0, :, now]
    grad_pre = grad_hidden * slope_chunk
    grad_pre_t = grad_hidden_t * slope_chunk + grad_hidden * slope[1, :, now]
    return grad_pre.astype(jnp.bfloat16), grad_pre_t.astype(jnp.bfloat16)


def norm_apply(values, normed, rscale):
    return rscale * (values - row_mean(values) - normed * row_mean(normed * values))


def backward_kernel(tick, *refs):
    section, pair, w_in_t, probe_t, w_out_t, norm, stat, slope = refs[:8]
    refs = refs[8:]
    if tick == CROSS_TICK:
        other_pair, pair_out, grads, acc, acc_t, whole = refs
    else:
        pair_out, grads, acc, acc_t = refs

    @pl.when(section[0] == LAYERS - 1 - tick)
    def _():
        adjoint = pair
        if tick == CROSS_TICK:
            adjoint = whole
            whole[...] = (pair[...].astype(jnp.float32) + other_pair[...].astype(jnp.float32)).astype(jnp.bfloat16)
        for chunk in range(CHUNKS):
            now = slice(chunk * CHUNK, (chunk + 1) * CHUNK)
            low_grad, low_grad_t = hidden_grads(adjoint, w_out_t, slope, now)
            both = jnp.concatenate([low_grad_t, low_grad], axis=0)
            grads[:, now] = both
            product = jnp.dot(both, w_in_t[now, :], preferred_element_type=jnp.float32)
            product_t = jnp.dot(low_grad, probe_t[now, :], preferred_element_type=jnp.float32)
            if chunk:
                acc[...] += product
                acc_t[...] += product_t
            else:
                acc[...] = product
                acc_t[...] = product_t

        normed, normed_t = norm[0], norm[1]
        rscale, tangent_dot = stat[0][:, :1], stat[1][:, :1]
        grad_norm = acc[ROWS:]
        grad_norm_t = acc[:ROWS] + acc_t[...]
        through = norm_apply(grad_norm, normed, rscale)
        through_t = (
            norm_apply(grad_norm_t, normed, rscale)
            - rscale * tangent_dot * through
            - rscale * (normed_t * row_mean(normed * grad_norm) + normed * row_mean(normed_t * grad_norm))
        )
        pair_out[0] = (adjoint[0].astype(jnp.float32) + through).astype(jnp.bfloat16)
        pair_out[1] = (adjoint[1].astype(jnp.float32) + through_t).astype(jnp.bfloat16)


def backward_call(tick, section, pairs, w_in_t, probe_t, w_out_t, kept):
    operands = [section, pairs[0], w_in_t, probe_t, w_out_t, *kept, *pairs[1:]]
    whole = [pltpu.VMEM(PAIR.shape, PAIR.dtype)] if tick == CROSS_TICK else []
    return pl.pallas_call(
        functools.partial(backward_kernel, tick),
        out_shape=[PAIR, GRADS],
        in_specs=[SMEM] + [WHOLE] * (len(operands) - 1),
        out_specs=[WHOLE] * 2,
        scratch_shapes=[
            pltpu.VMEM((2 * ROWS, FEATURES), jnp.float32),
            pltpu.VMEM((ROWS, FEATURES), jnp.float32),
            *whole,
        ],
        compiler_params=PARAMS,
        name=f"layer_down_{tick}",
    )(*operands)


OWN_HALF = slice(0, FEATURES // 2)
OTHER_HALF = slice(FEATURES // 2, FEATURES)


def curvature_operands(micro, section, pair, w_out_t, slope, order, opening_n, norms, grads, lhs, rhs):
    @pl.when(section[0] == 0)
    def _():
        rows = slice(micro * ROWS, (micro + 1) * ROWS)
        lhs[:ROWS] = jnp.dot(opening_n[rows], order[...], preferred_element_type=jnp.float32).astype(jnp.bfloat16)
        lhs[ROWS:] = jnp.zeros((ROWS, FEATURES), jnp.bfloat16)

        def bottom(chunk, carry):
            low_grad, low_grad_t = hidden_grads(pair, w_out_t, slope, columns(chunk))
            rhs[:, columns(chunk)] = jnp.concatenate([low_grad_t, low_grad], axis=0)
            return carry

        lax.fori_loop(0, CHUNKS, bottom, 0, unroll=UNROLL_LAST)

    for layer in range(1, LAYERS):

        @pl.when(section[0] == layer)
        def _():
            both = norms[layer - 1][...].reshape(2 * ROWS, FEATURES).astype(jnp.bfloat16)
            lhs[...] = jnp.dot(both, order[...], preferred_element_type=jnp.float32).astype(jnp.bfloat16)
            rhs[...] = grads[LAYERS - 1 - layer][...]


def curvature_kernel(micro, final, *refs):
    section, pair, w_out_t, slope, order, opening_n = refs[:6]
    norms, refs = refs[6 : 5 + LAYERS], refs[5 + LAYERS :]
    grads, refs = refs[: LAYERS - 1], refs[LAYERS - 1 :]
    if final:
        away_in, stay_in, refs = refs[0], refs[1], refs[2:]
    away, stay, lhs, rhs = refs
    curvature_operands(micro, section, pair, w_out_t, slope, order, opening_n, norms, grads, lhs, rhs)

    def step(chunk, carry):
        now = columns(chunk)

        def product(half):
            return lax.dot_general(lhs[:, half], rhs[:, now], CONTRACT_FIRST, preferred_element_type=jnp.float32)

        if final:
            away[:, now] = (away_in[:, now] + product(OTHER_HALF)).astype(jnp.bfloat16)
            stay[:, now] = stay_in[:, now] + product(OWN_HALF)
        else:
            away[:, now] = product(OTHER_HALF)
            stay[:, now] = product(OWN_HALF)
        return carry

    lax.fori_loop(0, CHUNKS, step, 0, unroll=UNROLL_LAST)


def curvature_call(micro, section, pair, w_out_t, slope, order, opening_n, norms, grads, sums):
    half = (FEATURES // 2, HIDDEN)
    final = bool(sums)
    operands = [section, pair, w_out_t, slope, order, opening_n, *norms, *grads, *sums]
    return pl.pallas_call(
        functools.partial(curvature_kernel, micro, final),
        out_shape=[
            jax.ShapeDtypeStruct(half, jnp.bfloat16 if final else jnp.float32),
            jax.ShapeDtypeStruct(half, jnp.float32),
        ],
        in_specs=[SMEM] + [WHOLE] * (len(operands) - 1),
        out_specs=[WHOLE] * 2,
        scratch_shapes=[
            pltpu.VMEM((2 * ROWS, FEATURES), jnp.bfloat16),
            pltpu.VMEM((2 * ROWS, HIDDEN), jnp.bfloat16),
        ],
        compiler_params=PARAMS,
        name="curvature_last" if final else "curvature_first",
    )(*operands)


def block_sum_kernel(blocks, total):
    total[...] = sum(blocks[index].astype(jnp.float32) for index in range(4)).astype(jnp.bfloat16)


def block_sum_call(blocks):
    return pl.pallas_call(
        block_sum_kernel,
        out_shape=jax.ShapeDtypeStruct(blocks.shape[1:], jnp.bfloat16),
        in_specs=[WHOLE],
        out_specs=WHOLE,
        compiler_params=PARAMS,
        name="block_sum",
    )(blocks)


def shards(inputs, targets, w_in, w_out, probes):
    place = [jnp.reshape(lax.axis_index(name), (1,)).astype(jnp.int32) for name in (*DP, SECTION)]
    section = place[-1]
    out_block = settled_call(place, w_out[0])
    probe = probes[0]
    own_in, other_in = gathered(w_in[0], True)
    full_out = placed_call(place, *gathered(out_block, False))
    order, curvature_order, opening_n, opening_t = opening_call(place, inputs, probe)
    goal = routed(targets, goal_route)
    pairs, slopes, kept, grads = [None] * MICRO, [], [], []
    for micro in range(MICRO):
        kept.append([])
        grads.append([])
    for tick in range(LAYERS):
        for micro in range(MICRO):
            if tick == 0:
                pair, slope = first_call(
                    micro, section, inputs, opening_n, opening_t, order, own_in, other_in, full_out
                )
                slopes.append(slope)
            else:
                goal_now = goal[micro * ROWS : (micro + 1) * ROWS]
                pair, *stores = forward_call(
                    tick, section, pairs[micro], own_in, other_in, probe, full_out, order, goal_now
                )
                kept[micro].append(stores)
            if tick < LAYERS - 1:
                pairs[micro] = [routed(pair, up_across if tick + 1 == CROSS_TICK else up_from(tick))]
            else:
                pairs[micro] = [pair]
            if tick + 1 == CROSS_TICK:
                pairs[micro].append(routed(pairs[micro][0], up_relayed))
        if tick == TURN_TICK:
            turned = turned_call(own_in, other_in, probe, full_out, order, kept[-1][-1][0])
    for tick in range(LAYERS - 1):
        for micro in range(MICRO):
            pair, low_grads = backward_call(tick, section, pairs[micro], *turned, kept[micro][LAYERS - 2 - tick])
            grads[micro].append(low_grads)
            pairs[micro] = [routed(pair, down_across if tick + 1 == CROSS_TICK else down_from(LAYERS - 1 - tick))]
            if tick + 1 == CROSS_TICK:
                pairs[micro].append(routed(pairs[micro][0], down_relayed))
    sums = ()
    for micro in range(MICRO):
        norms = [stores[0] for stores in kept[micro]]
        sums = curvature_call(
            micro, section, pairs[micro][0], turned[2], slopes[micro], curvature_order, opening_n, norms, grads[micro], sums
        )
    away, stay = sums
    other = routed(away, swap_core)
    summed = (stay + other.astype(jnp.float32)).astype(jnp.bfloat16)
    summed = lax.all_to_all(summed.reshape(4, 64, HIDDEN), "y", 0, 0, tiled=True)
    summed = block_sum_call(summed)
    summed = lax.all_to_all(summed.reshape(8, 8, HIDDEN), ("b1", "b2", "b4"), 0, 0, tiled=True)
    summed = jnp.sum(summed.astype(jnp.float32), axis=0)
    probe_own = lax.dynamic_slice_in_dim(probe, lax.axis_index(DP) * 8, 8, 0)
    return (probe_own.astype(jnp.float32) * summed)[None]


def solution(mesh):
    fine = Mesh(mesh.devices.reshape(SIZES), NAMES)
    return jax.shard_map(
        shards,
        mesh=fine,
        in_specs=(
            P(DP, None),
            P(DP, None),
            P(SECTION, DP, None),
            P(SECTION, DP, None),
            P(SECTION, None, None),
        ),
        out_specs=P(SECTION, DP, None),
        check_vma=False,
    )
```
